32 devices in a mesh: dp: 4 (over z), seq: 8 (over y, x, core).
Axes of the slice: x: 2, y: 2, z: 4, core: 2. Of those that a mesh axis runs over, the one named last changes fastest.
Arguments:
- query: bfloat16 [4, 2048, 1024], P('dp', 'seq'), may hold values from -150 to 150
- key: bfloat16 [4, 2048, 128], P('dp', 'seq'), may hold values from -5 to 5
- value: bfloat16 [4, 2048, 128], P('dp', 'seq'), may hold values from -6 to 6
- ssm_input: bfloat16 [4, 2048, 1024], P('dp', 'seq'), may hold values from -9 to 9
- in_b: bfloat16 [4, 2048, 128], P('dp', 'seq'), may hold values from -0.625 to 0.625
- in_c: bfloat16 [4, 2048, 128], P('dp', 'seq'), may hold values from -0.625 to 0.625
- step: float32 [4, 2048, 8], P('dp', 'seq'), may hold values from 0.3 to 6144
- rate_log: float32 [8], replicated, may hold values from -20 to 0
- skip: float32 [8], replicated, may hold values from 0.5 to 1.5
- block_mask: int32 [4, 16, 16], P('dp'), may hold values from 0 to 1, as said below
- grad_out: bfloat16 [4, 2048, 1024], P('dp', 'seq'), may hold values from -10 to 10
Outputs:
- layer_out: bfloat16 [4, 2048, 1024], P('dp', 'seq')
- query_gradient: bfloat16 [4, 2048, 1024], P('dp', 'seq')
- key_gradient: bfloat16 [4, 2048, 128], P('dp', 'seq')
- value_gradient: bfloat16 [4, 2048, 128], P('dp', 'seq')
- grad_input: bfloat16 [4, 2048, 1024], P('dp', 'seq')
- grad_in_b: bfloat16 [4, 2048, 128], P('dp', 'seq')
- grad_in_c: bfloat16 [4, 2048, 128], P('dp', 'seq')
- grad_rate_log: float32 [8], replicated
- grad_skip: float32 [8], replicated
The draws below stay inside these ranges and needn't reach their ends.
Inputs may be any that keep to these rules, and one draw needn't show every extreme that they name: block_mask[b, i, i] = 1; every row holds at most 6 ones, and the last row of every sequence's mask holds exactly 6.
All inputs are finite; a program needn't handle non-finite values.
Results may differ from the reference program's by a relative error of at most 0.02.
Values may be sent and summed in bfloat16 or wider, within the bound.
No kernel may reach another device: no remote copies, remote signals or barrier semaphores. Data moves between devices by JAX's collectives and lax.ppermute only.
A program may use at most 192 MiB of HBM per device.

```python
import math
import jax
import jax.numpy as jnp
from jax import lax

HEAD_WIDTH = 128
QUERY_HEADS = 8
KEY_VALUE_HEADS = 1
HS = 8
P_SIZE = 128
NS = 128
BLOCK_TOKENS = 128
TOK_DEV = 256
STREAM_TOTAL_NUM = 4
STREAM_SPAN = 2048
NB = 16
MOST_KEY_BLOCKS = 6


def query_key_pair(key):
    baseline_level = jax.random.fold_in(key, 11)
    key_q, random_key_keys = jax.random.split(baseline_level, 2)
    key_rows = jnp.clip(jax.random.normal(random_key_keys, (STREAM_TOTAL_NUM, STREAM_SPAN, KEY_VALUE_HEADS * HEAD_WIDTH), jnp.float32), -5.0, 5.0)
    query_rows = jnp.clip(jax.random.normal(key_q, (STREAM_TOTAL_NUM, STREAM_SPAN, QUERY_HEADS * HEAD_WIDTH), jnp.float32), -5.0, 5.0)
    return (query_rows, key_rows)


def draw_query(key, part):
    return query_key_pair(key)[0].astype(jnp.bfloat16)


def draw_key(key, part):
    return query_key_pair(key)[1].astype(jnp.bfloat16)


def input_pair(key):
    key_x, key_g = jax.random.split(jax.random.fold_in(key, 23))
    shape = (STREAM_TOTAL_NUM, STREAM_SPAN, HS * P_SIZE)
    place = (jnp.arange(STREAM_SPAN, dtype=jnp.float32) / STREAM_SPAN)[None, :, None]
    inputs = jax.random.normal(key_x, shape, jnp.float32) * (0.7 + 0.6 * place)
    gradient_list = jax.random.normal(key_g, shape, jnp.float32) * (0.6 + 0.8 * place) + 0.25 * inputs
    return (jnp.clip(inputs, -9.0, 9.0), jnp.clip(gradient_list, -10.0, 10.0))


def draw_ssm_input(key, part):
    return input_pair(key)[0].astype(jnp.bfloat16)


def draw_grad_out(key, part):
    return input_pair(key)[1].astype(jnp.bfloat16)


def decay_pair(key):
    key_p, key_s, key_f, entropy_seed_later, key_u, key_a, key_r = jax.random.split(jax.random.fold_in(key, 37), 7)
    ranking = jax.random.permutation(key_p, HS)
    slow_count = HS // 2
    slow = ranking < slow_count
    slow_rate = jnp.exp(jax.random.uniform(key_s, (HS,), jnp.float32, math.log(0.16), math.log(0.5))) / STREAM_SPAN
    fast_rate = jax.random.uniform(key_f, (HS,), jnp.float32, 2.5, 4.0) / BLOCK_TOKENS
    speed_factor = jnp.where(slow, slow_rate, fast_rate)
    regions = STREAM_SPAN // TOK_DEV
    district_multiplier = jnp.exp(jax.random.uniform(key_r, (STREAM_TOTAL_NUM, regions, HS), jnp.float32, math.log(0.7), math.log(1.4)))
    district_multiplier = jnp.repeat(district_multiplier, TOK_DEV, axis=1)
    baseline_level = jnp.exp(jax.random.uniform(key_a, (STREAM_TOTAL_NUM, STREAM_SPAN, HS), jnp.float32, math.log(0.5), math.log(2.0)))
    surge_location = jax.random.randint(entropy_seed_later, (STREAM_TOTAL_NUM, 3), 0, STREAM_SPAN)
    surge_switched_on = jnp.any(jnp.arange(STREAM_SPAN)[None, :, None] == surge_location[:, None, :], axis=-1)
    objective_trace = jax.random.uniform(key_u, (STREAM_TOTAL_NUM, STREAM_SPAN, HS), jnp.float32, 0.2, 0.45)
    iteration_number = jnp.where(surge_switched_on[:, :, None], objective_trace / speed_factor[None, None, :], baseline_level * district_multiplier)
    return (jnp.log(speed_factor), iteration_number)


def draw_rate_log(key, part):
    return decay_pair(key)[0]


def draw_step(key, part):
    return decay_pair(key)[1]


def draw_block_mask(key, part):
    key_c, key_s = jax.random.split(jax.random.fold_in(key, 51))
    block_rows = jnp.arange(NB, dtype=jnp.int32)
    ramp_count = 1 + (MOST_KEY_BLOCKS - 1) * block_rows * block_rows // ((NB - 1) * (NB - 1))
    lowest = jnp.maximum(ramp_count // 2, 1)
    counts = jax.random.randint(key_c, (STREAM_TOTAL_NUM, NB), 0, 1 << 20) % (ramp_count - lowest + 1)[None, :] + lowest[None, :]
    counts = counts.at[:, NB - 1].set(MOST_KEY_BLOCKS)
    ranking_scores = jax.random.randint(key_s, (STREAM_TOTAL_NUM, NB, NB), 0, 1 << 16) * NB + block_rows[None, None, :]
    ranking_scores = jnp.where((block_rows[:, None] == block_rows[None, :])[None, :, :], -1, ranking_scores)
    ordering = jnp.argsort(ranking_scores, axis=-1)
    ranks = jnp.argsort(ordering, axis=-1)
    return (ranks < counts[:, :, None]).astype(jnp.int32)


def steps_of(own_key, dims, cuts, smallest, largest):
    def one(dim, parts):
        steps = jax.random.uniform(jax.random.fold_in(jax.random.fold_in(own_key, 6), dim), (parts,), jnp.float32, smallest / len(cuts), largest / len(cuts))
        return jnp.repeat(jnp.exp(steps), dims[dim] // parts).reshape((-1,) + (1,) * (len(dims) - dim - 1))

    level = one(*cuts[0])
    for cut in cuts[1:]:
        level = level * one(*cut)
    return level


def bell_draw(rng, dims, deviation, reach, shards=(), kind=jnp.bfloat16):
    array = jax.random.normal(rng, dims, jnp.float32) * deviation
    if len(shards) > 0:
        array = steps_of(rng, dims, shards, -0.22, 0.18) * array
    return jnp.clip(array, min=-reach, max=reach).astype(kind)


def setup_inputs(seed: int = 0) -> dict:
    seeds = jax.random.split(jax.random.key(seed), 12)
    return {
        "query": draw_query(jax.random.fold_in(seeds[11], 71), 0),
        "key": draw_key(jax.random.fold_in(seeds[11], 71), 0),
        "value": bell_draw(seeds[2], (STREAM_TOTAL_NUM, STREAM_SPAN, KEY_VALUE_HEADS * HEAD_WIDTH), 1.0, 6.0, ((0, 4), (1, 8))),
        "ssm_input": draw_ssm_input(jax.random.fold_in(seeds[11], 71), 0),
        "in_b": bell_draw(seeds[4], (STREAM_TOTAL_NUM, STREAM_SPAN, NS), ((NS * STREAM_SPAN) ** -0.25), 0.625, ((0, 4), (1, 8))),
        "in_c": bell_draw(seeds[5], (STREAM_TOTAL_NUM, STREAM_SPAN, NS), ((NS * STREAM_SPAN) ** -0.25), 0.625, ((0, 4), (1, 8))),
        "step": draw_step(jax.random.fold_in(seeds[11], 71), 0),
        "rate_log": draw_rate_log(jax.random.fold_in(seeds[11], 71), 0),
        "skip": jnp.clip(1.0 + 0.1 * jax.random.normal(seeds[8], (HS,), jnp.float32), 0.5, 1.5),
        "block_mask": draw_block_mask(jax.random.fold_in(seeds[11], 71), 0),
        "grad_out": draw_grad_out(jax.random.fold_in(seeds[11], 71), 0),
    }


HIGH = lax.Precision.HIGHEST

def ssm_blocks(h_start, x_seq, b_seq, c_seq, rate_log, skip, step_sizes):
    heads = rate_log.shape[0]
    length = x_seq.shape[0]
    width = x_seq.shape[1] // heads
    count_of_blocks = length // BLOCK_TOKENS
    decay_log = -step_sizes * jnp.exp(rate_log)[None, :]
    lower = jnp.arange(BLOCK_TOKENS)[:, None] >= jnp.arange(BLOCK_TOKENS)[None, :]

    def one_block(state, pieces):
        x_block, b_block, c_block, log_block = pieces
        running = jnp.cumsum(log_block, axis=0)
        spread = running.T[:, :, None] - running.T[:, None, :]
        decay = jnp.exp(jnp.where(lower[None, :, :], spread, -jnp.inf))
        inner = jnp.dot(c_block, b_block.T, precision=HIGH)
        y_inner = jnp.einsum('hij,jhp->ihp', decay * inner[None, :, :], x_block, precision=HIGH)
        carried = jnp.einsum('in,hpn->ihp', c_block, state, precision=HIGH)
        y_block = y_inner + jnp.exp(running)[:, :, None] * carried + skip[None, :, None] * x_block
        tail = jnp.exp(running[-1][None, :] - running)
        fresh = jnp.einsum('jh,jhp,jn->hpn', tail, x_block, b_block, precision=HIGH)
        new_state = jnp.exp(running[-1])[:, None, None] * state + fresh
        return (new_state, y_block)
    pieces = (x_seq.reshape(count_of_blocks, BLOCK_TOKENS, heads, width), b_seq.reshape(count_of_blocks, BLOCK_TOKENS, -1), c_seq.reshape(count_of_blocks, BLOCK_TOKENS, -1), decay_log.reshape(count_of_blocks, BLOCK_TOKENS, heads))
    h_end, y_all = lax.scan(one_block, h_start, pieces)
    return (y_all.reshape(length, heads * width), h_end)

def attend_block(query_block, block_gradient, mask_row, key_rows, value_rows):
    count_of_blocks = mask_row.shape[0]
    head_groups = QUERY_HEADS // KEY_VALUE_HEADS
    factor = HEAD_WIDTH ** (-0.5)
    ranking = jnp.argsort((1 - mask_row) * count_of_blocks + jnp.arange(count_of_blocks, dtype=jnp.int32))
    picked_blocks = ranking[:MOST_KEY_BLOCKS].astype(jnp.int32)
    live = jnp.arange(MOST_KEY_BLOCKS, dtype=jnp.int32) < jnp.sum(mask_row)
    selected_keys = key_rows.reshape(count_of_blocks, BLOCK_TOKENS, KEY_VALUE_HEADS, HEAD_WIDTH)[picked_blocks].reshape(MOST_KEY_BLOCKS * BLOCK_TOKENS, KEY_VALUE_HEADS, HEAD_WIDTH).astype(jnp.float32)
    selected_values = value_rows.reshape(count_of_blocks, BLOCK_TOKENS, KEY_VALUE_HEADS, HEAD_WIDTH)[picked_blocks].reshape(MOST_KEY_BLOCKS * BLOCK_TOKENS, KEY_VALUE_HEADS, HEAD_WIDTH).astype(jnp.float32)
    query_rows = query_block.reshape(BLOCK_TOKENS, KEY_VALUE_HEADS, head_groups, HEAD_WIDTH).astype(jnp.float32)
    gradient_list = block_gradient.reshape(BLOCK_TOKENS, KEY_VALUE_HEADS, head_groups, HEAD_WIDTH).astype(jnp.float32)
    scores = jnp.einsum('qhgd,khd->hgqk', query_rows, selected_keys) * factor
    scores = jnp.where(jnp.repeat(live, BLOCK_TOKENS)[None, None, None, :], scores, -jnp.inf)
    best = lax.optimization_barrier(jnp.max(scores, axis=-1, keepdims=True))
    weights = jnp.exp(scores - best)
    total = lax.optimization_barrier(jnp.sum(weights, axis=-1, keepdims=True))
    rounded = lax.optimization_barrier(weights.astype(jnp.bfloat16)).astype(jnp.float32)
    output = jnp.einsum('hgqk,khd->hgqd', rounded, selected_values) / total
    delta = lax.optimization_barrier(jnp.sum(jnp.transpose(gradient_list, (1, 2, 0, 3)) * output, axis=-1, keepdims=True))
    probs = weights / total
    probs_low = lax.optimization_barrier(probs.astype(jnp.bfloat16)).astype(jnp.float32)
    dprobs = jnp.einsum('qhgd,khd->hgqk', gradient_list, selected_values)
    dscores = lax.optimization_barrier((probs * (dprobs - delta)).astype(jnp.bfloat16)).astype(jnp.float32)
    query_gradient_part = jnp.einsum('hgqk,khd->qhgd', dscores, selected_keys) * factor
    key_gradient_part = jnp.einsum('hgqk,qhgd->khd', dscores, query_rows) * factor
    value_gradient_part = jnp.einsum('hgqk,qhgd->khd', probs_low, gradient_list)
    output_row_block = jnp.transpose(output, (2, 0, 1, 3)).reshape(BLOCK_TOKENS, QUERY_HEADS * HEAD_WIDTH)
    return (output_row_block, query_gradient_part.reshape(BLOCK_TOKENS, QUERY_HEADS * HEAD_WIDTH), picked_blocks, key_gradient_part.reshape(MOST_KEY_BLOCKS, BLOCK_TOKENS, KEY_VALUE_HEADS * HEAD_WIDTH), value_gradient_part.reshape(MOST_KEY_BLOCKS, BLOCK_TOKENS, KEY_VALUE_HEADS * HEAD_WIDTH))

def one_sequence(items, rate_log, skip):
    query, key, value, ssm_input, in_b, in_c, step, block_mask, grad_out = items
    count_of_blocks = STREAM_SPAN // BLOCK_TOKENS

    def per_block(holding_array, pieces):
        query_block, block_gradient, mask_row = pieces
        output_row_block, grad_rows, picked_blocks, key_gradient_part, value_gradient_part = attend_block(query_block, block_gradient, mask_row, key, value)
        holding_array = holding_array.at[picked_blocks].add(jnp.concatenate([key_gradient_part, value_gradient_part], axis=-1))
        return (holding_array, (output_row_block, grad_rows))
    blank_rows = jnp.zeros((count_of_blocks, BLOCK_TOKENS, 2 * KEY_VALUE_HEADS * HEAD_WIDTH), jnp.float32)
    holding_array, (attention, query_gradient) = lax.scan(per_block, blank_rows, (query.reshape(count_of_blocks, BLOCK_TOKENS, QUERY_HEADS * HEAD_WIDTH), grad_out.reshape(count_of_blocks, BLOCK_TOKENS, QUERY_HEADS * HEAD_WIDTH), block_mask))
    attention = attention.reshape(STREAM_SPAN, QUERY_HEADS * HEAD_WIDTH)
    holding_array = holding_array.reshape(STREAM_SPAN, 2 * KEY_VALUE_HEADS * HEAD_WIDTH)

    def branch(x_float, b_float, c_float, rate_value, gain):
        outcome, final_state = ssm_blocks(jnp.zeros((HS, P_SIZE, NS), jnp.float32), x_float, b_float, c_float, rate_value, gain, step)
        return outcome
    ssm_out, pullback = jax.vjp(branch, ssm_input.astype(jnp.float32), in_b.astype(jnp.float32), in_c.astype(jnp.float32), rate_log, skip)
    input_gradient, gradient_input_weights, gradient_output_weights, rate_gradient, gain_gradient = pullback(grad_out.astype(jnp.float32))
    layer_function = (attention + ssm_out).astype(jnp.bfloat16)
    return (layer_function, query_gradient.reshape(STREAM_SPAN, QUERY_HEADS * HEAD_WIDTH).astype(jnp.bfloat16), holding_array[:, :KEY_VALUE_HEADS * HEAD_WIDTH].astype(jnp.bfloat16), holding_array[:, KEY_VALUE_HEADS * HEAD_WIDTH:].astype(jnp.bfloat16), input_gradient.astype(jnp.bfloat16), gradient_input_weights.astype(jnp.bfloat16), gradient_output_weights.astype(jnp.bfloat16), rate_gradient, gain_gradient)

def reference(query, key, value, ssm_input, in_b, in_c, step, rate_log, skip, block_mask, grad_out):
    results = lax.map(lambda items: one_sequence(items, rate_log, skip), (query, key, value, ssm_input, in_b, in_c, step, block_mask, grad_out))
    tokens_all = STREAM_TOTAL_NUM * STREAM_SPAN
    grad_rate_log = lax.optimization_barrier(jnp.sum(results[7], axis=0)) / tokens_all
    grad_skip = lax.optimization_barrier(jnp.sum(results[8], axis=0)) / (tokens_all * P_SIZE)
    return (results[0], results[1], results[2], results[3], results[4], results[5], results[6], grad_rate_log, grad_skip)
```

```python
import jax
import jax.numpy as jnp
from jax import lax
from jax.experimental import pallas as pl
from jax.experimental.pallas import tpu as pltpu
from jax.sharding import PartitionSpec as P

HEAD_WIDTH = 128
QUERY_HEADS = 8
HS = 8
P_SIZE = 128
NS = 128
BLOCK = 128
WIDE = HS * P_SIZE
LANES = 128
FACTOR = HEAD_WIDTH ** (-0.5)
LOG2E = 1.4426950408889634
NEG = -1e30
HIGH = lax.Precision.HIGHEST
F32 = jnp.float32
BF16 = jnp.bfloat16

VMEM = pl.BlockSpec(memory_space=pltpu.VMEM)
SMEM = pl.BlockSpec(memory_space=pltpu.SMEM)


def params(limit=56 << 20):
    return pltpu.CompilerParams(vmem_limit_bytes=limit)


def dot(a, b, ca, cb, precision=None):
    return lax.dot_general(
        a, b, (((ca,), (cb,)), ((), ())), preferred_element_type=F32, precision=precision
    )


def head(h):
    return slice(h * LANES, (h + 1) * LANES)


def running_logs(step_ref, rate_ref, pad_ref):
    pad_ref[...] = jnp.zeros_like(pad_ref)
    pad_ref[:, :HS] = -step_ref[...] * jnp.exp(rate_ref[...])
    row = lax.broadcasted_iota(jnp.int32, (BLOCK, BLOCK), 0)
    col = lax.broadcasted_iota(jnp.int32, (BLOCK, BLOCK), 1)
    lower = jnp.where(row >= col, 1.0, 0.0).astype(F32)
    run0 = dot(lower, pad_ref[:BLOCK], 1, 0, HIGH)
    run1 = dot(lower, pad_ref[BLOCK:], 1, 0, HIGH)
    return run0, run1


def scaled(x_ref, column, out_ref):
    for h in range(HS):
        out_ref[:, head(h)] = (x_ref[:, head(h)].astype(F32) * column[:, h : h + 1]).astype(BF16)


def local_states_kernel(
    x_ref, g_ref, b_ref, c_ref, step_ref, rate_ref, out_ref, pad_ref, xt_ref, gt_ref
):
    run0, run1 = running_logs(step_ref, rate_ref, pad_ref)
    t0, t1 = run0[BLOCK - 1 :, :], run1[BLOCK - 1 :, :]
    enter = jnp.exp(jnp.concatenate([run0, run1 + t0], axis=0))
    tail = jnp.exp(jnp.concatenate([(t0 - run0) + t1, t1 - run1], axis=0))
    scaled(x_ref, tail, xt_ref)
    scaled(g_ref, enter, gt_ref)
    out_ref[0, :, :WIDE] = dot(b_ref[...], xt_ref[...], 0, 0).astype(BF16)
    out_ref[1, :, :WIDE] = dot(c_ref[...], gt_ref[...], 0, 0).astype(BF16)
    total = t0 + t1
    high = total.astype(BF16).astype(F32)
    middle = (total - high).astype(BF16).astype(F32)
    low = total - high - middle
    place = lax.broadcasted_iota(jnp.int32, (NS, LANES), 0) % 4
    logs = jnp.where(place == 0, high, jnp.where(place == 1, middle, low)).astype(BF16)
    out_ref[0, :, WIDE:] = logs
    out_ref[1, :, WIDE:] = logs


def chain_kernel(n, rows, in_ref, out_ref):
    decays = []
    for e in range(n):
        logs = in_ref[0, e * rows : (e + 1) * rows, WIDE:].astype(F32)
        total = logs[0:1, :] + logs[1:2, :] + logs[2:3, :]
        factor = jnp.exp(total)
        decays.append([factor[:, h : h + 1] for h in range(HS)])
    for direction in range(2):
        for h in range(HS):
            state = jnp.zeros((rows, LANES), F32)
            for e in range(n) if direction == 0 else range(n - 1, -1, -1):
                at = slice(e * rows, (e + 1) * rows)
                out_ref[direction, at, head(h)] = state.astype(BF16)
                state = state * decays[e][h] + in_ref[direction, at, head(h)].astype(F32)


def attention_kernel(
    mask_ref, first_ref, q_ref, g_ref, kv_ref, out_ref, dq_ref, dkv_ref,
    index_ref, s_ref, acc_ref, qs_ref, gs_ref, ds_ref, pr_ref, o_ref, dqt_ref, rows_ref,
):
    count = mask_ref.shape[0]
    columns = QUERY_HEADS * BLOCK
    acc_ref[...] = jnp.zeros_like(acc_ref)
    scale = FACTOR * LOG2E
    for block in range(q_ref.shape[0] // BLOCK):
        at = slice(block * BLOCK, (block + 1) * BLOCK)
        row = first_ref[0] + block

        def note(j, n):
            @pl.when(mask_ref[row, j] == 1)
            def _():
                index_ref[n] = j

            return n + mask_ref[row, j]

        allowed = lax.fori_loop(0, count, note, 0)
        index_ref[allowed] = row
        pairs = (allowed + 1) // 2
        for h in range(QUERY_HEADS):
            qs_ref[head(h), :] = q_ref[at, head(h)]
            gs_ref[head(h), :] = g_ref[at, head(h)]

        def spans(t):
            first = pl.multiple_of(index_ref[2 * t] * BLOCK, BLOCK)
            second = pl.multiple_of(index_ref[2 * t + 1] * BLOCK, BLOCK)
            return pl.ds(first, BLOCK), pl.ds(second, BLOCK)

        def tile(t, lanes):
            one, two = spans(t)
            return jnp.concatenate([kv_ref[one, lanes], kv_ref[two, lanes]], axis=0)

        def scores_step(t, best):
            k_tile = tile(t, slice(0, LANES))
            live = 2 * t + 1 < allowed
            outs = []
            for part in range(columns // 256):
                lanes = slice(part * 256, (part + 1) * 256)
                s = dot(k_tile, qs_ref[lanes, :], 1, 1)
                low = s[:BLOCK]
                high = jnp.where(live, s[BLOCK:], NEG)
                s_ref[t, :BLOCK, lanes] = low
                s_ref[t, BLOCK:, lanes] = high
                both = jnp.maximum(low, high).reshape(BLOCK // 8, 8, 256)
                outs.append(jnp.maximum(best[part], jnp.max(both, axis=0)))
            return tuple(outs)

        best = lax.fori_loop(
            0, pairs, scores_step, tuple(jnp.full((8, 256), NEG, F32) for _ in range(columns // 256))
        )
        for part in range(columns // 256):
            lanes = slice(part * 256, (part + 1) * 256)
            rows_ref[0:1, lanes] = jnp.max(best[part], axis=0, keepdims=True) * scale
        o_ref[...] = jnp.zeros_like(o_ref)

        def weights_step(t, total):
            v_tile = tile(t, slice(LANES, 2 * LANES))
            outs = []
            for part in range(columns // 256):
                lanes = slice(part * 256, (part + 1) * 256)
                w = jnp.exp2(s_ref[t, :, lanes] * scale - rows_ref[0:1, lanes])
                s_ref[t, :, lanes] = w
                outs.append(total[part] + jnp.sum(w.reshape(32, 8, 256), axis=0))
                o_ref[:, lanes] += dot(v_tile, w.astype(BF16), 0, 0)
            return tuple(outs)

        total = lax.fori_loop(
            0, pairs, weights_step, tuple(jnp.zeros((8, 256), F32) for _ in range(columns // 256))
        )
        for part in range(columns // 256):
            lanes = slice(part * 256, (part + 1) * 256)
            inverse = 1.0 / jnp.sum(total[part], axis=0, keepdims=True)
            rows_ref[1:2, lanes] = inverse
            o = o_ref[:, lanes] * inverse
            o_ref[:, lanes] = o
            g_t = gs_ref[lanes, :].astype(F32).T
            rows_ref[2:3, lanes] = jnp.sum(o * g_t, axis=0, keepdims=True)
        for h in range(QUERY_HEADS):
            out_ref[at, head(h)] = o_ref[:, head(h)].T
        dqt_ref[...] = jnp.zeros_like(dqt_ref)

        def grads_step(t, carry):
            k_tile = tile(t, slice(0, LANES))
            v_tile = tile(t, slice(LANES, 2 * LANES))
            for part in range(columns // 256):
                lanes = slice(part * 256, (part + 1) * 256)
                dp = dot(v_tile, gs_ref[lanes, :], 1, 1)
                probs = s_ref[t, :, lanes] * rows_ref[1:2, lanes]
                ds = (probs * (dp - rows_ref[2:3, lanes])).astype(BF16)
                ds_ref[:, lanes] = ds
                pr_ref[:, lanes] = probs.astype(BF16)
                dqt_ref[:, lanes] += dot(k_tile, ds, 0, 0)
            dk = dot(ds_ref[...], qs_ref[...], 1, 0) * FACTOR
            dv = dot(pr_ref[...], gs_ref[...], 1, 0)
            one, two = spans(t)
            acc_ref[one, :LANES] += dk[:BLOCK]
            acc_ref[one, LANES:] += dv[:BLOCK]
            acc_ref[two, :LANES] += dk[BLOCK:]
            acc_ref[two, LANES:] += dv[BLOCK:]
            return carry

        lax.fori_loop(0, pairs, grads_step, 0)
        for h in range(QUERY_HEADS):
            dq_ref[at, head(h)] = (dqt_ref[:, head(h)].T * FACTOR).astype(BF16)
    dkv_ref[...] = acc_ref[...].astype(BF16)


def ssm_kernel(
    x_ref, g_ref, b_ref, c_ref, step_ref, rate_ref, skip_ref, ent_ref, att_ref,
    y_ref, dx_ref, db_ref, dc_ref, sums_ref,
    pad_ref, xt_ref, gt_ref, inner_ref, dinner_ref, m_ref, runt_ref,
):
    tokens = 2 * BLOCK
    run0, run1 = running_logs(step_ref, rate_ref, pad_ref)
    t0, t1 = run0[BLOCK - 1 :, :], run1[BLOCK - 1 :, :]
    enter_log = jnp.concatenate([run0, run1 + t0], axis=0)
    tail_log = jnp.concatenate([(t0 - run0) + t1, t1 - run1], axis=0)
    enter, tail = jnp.exp(enter_log), jnp.exp(tail_log)
    scaled(x_ref, tail, xt_ref)
    scaled(g_ref, enter, gt_ref)
    own = jnp.concatenate([run0, run1], axis=0)
    runt_ref[:, :tokens] = own.T
    runt_ref[:, tokens:] = jnp.concatenate([run0 - t0, run1], axis=0).T
    b = b_ref[...]
    c = c_ref[...]
    inner_ref[...] = dot(c, b, 1, 1)
    dinner_ref[...] = jnp.zeros_like(dinner_ref)
    row0 = lax.broadcasted_iota(jnp.int32, (BLOCK, BLOCK), 0)
    col0 = lax.broadcasted_iota(jnp.int32, (BLOCK, BLOCK), 1)
    row1 = lax.broadcasted_iota(jnp.int32, (BLOCK, tokens), 0)
    col1 = lax.broadcasted_iota(jnp.int32, (BLOCK, tokens), 1)
    seen0 = row0 >= col0
    seen1 = row1 + BLOCK >= col1
    m_ref[:BLOCK, BLOCK:] = jnp.zeros((BLOCK, BLOCK), BF16)
    both = t0 + t1
    for h in range(HS):
        lanes = head(h)
        x = x_ref[:, lanes]
        g = g_ref[:, lanes]
        xf, gf = x.astype(F32), g.astype(F32)
        gain = skip_ref[0, h]
        spread0 = jnp.where(seen0, own[:BLOCK, h : h + 1] - runt_ref[h : h + 1, :BLOCK], NEG)
        spread1 = jnp.where(seen1, own[BLOCK:, h : h + 1] - runt_ref[h : h + 1, tokens:], NEG)
        decay0, decay1 = jnp.exp(spread0), jnp.exp(spread1)
        dm = dot(g, x, 1, 1)
        e0, e1 = decay0 * dm[:BLOCK, :BLOCK], decay1 * dm[BLOCK:, :]
        m_ref[:BLOCK, :BLOCK] = (decay0 * inner_ref[:BLOCK, :BLOCK]).astype(BF16)
        m_ref[BLOCK:, :] = (decay1 * inner_ref[BLOCK:, :]).astype(BF16)
        dinner_ref[:BLOCK, :BLOCK] += e0
        dinner_ref[BLOCK:, :] += e1
        w0 = jnp.sum(spread0 * (e0 * inner_ref[:BLOCK, :BLOCK]), axis=0, keepdims=True)
        w1 = jnp.sum(spread1 * (e1 * inner_ref[BLOCK:, :]), axis=0, keepdims=True)
        rate = w0 + w1[:, :BLOCK] + w1[:, BLOCK:]
        h0 = ent_ref[0, :, lanes]
        later = ent_ref[1, :, lanes]
        carried = dot(c, h0, 1, 0) * enter[:, h : h + 1]
        back = dot(b, later, 1, 0) * tail[:, h : h + 1]
        m = m_ref[...]
        y = dot(m, x, 1, 0) + carried + gain * xf
        y_ref[:, lanes] = (y + att_ref[:, lanes]).astype(BF16)
        dx_ref[:, lanes] = (dot(m, g, 0, 0) + back + gain * gf).astype(BF16)
        rate += jnp.sum(
            gf * carried * enter_log[:, h : h + 1] + xf * back * tail_log[:, h : h + 1],
            axis=0,
            keepdims=True,
        )
        cross = jnp.sum(h0.astype(F32) * later.astype(F32), axis=0, keepdims=True)
        whole = both[:, h : h + 1]
        rate += cross * (whole * jnp.exp(whole))
        sums_ref[h : h + 1, :] = rate
        sums_ref[HS + h : HS + h + 1, :] = jnp.sum(gf * xf, axis=0, keepdims=True)
    dinner = dinner_ref[...].astype(BF16)
    dc = dot(dinner, b, 1, 0) + dot(gt_ref[...], ent_ref[0], 1, 1)
    db = dot(dinner, c, 0, 0) + dot(xt_ref[...], ent_ref[1], 1, 1)
    dc_ref[...] = dc.astype(BF16)
    db_ref[...] = db.astype(BF16)


def body(query, key, value, ssm_input, in_b, in_c, step, rate_log, skip, block_mask, grad_out):
    n = lax.axis_size("seq")
    tokens = query.shape[1]
    per_device = tokens // BLOCK
    blocks = block_mask.shape[1]
    most = 3 * blocks // 8
    every = blocks * BLOCK
    q, g, x = query[0], grad_out[0], ssm_input[0]
    b, c = in_b[0], in_c[0]
    rate_row, skip_row = rate_log.reshape(1, HS), skip.reshape(1, HS)
    shape = jax.ShapeDtypeStruct

    kv = jnp.concatenate([key[0], value[0]], axis=1)
    kv_all = lax.all_gather(kv, "seq", axis=0, tiled=True)

    states = pl.pallas_call(
        local_states_kernel,
        out_shape=shape((2, NS, WIDE + LANES), BF16),
        in_specs=[VMEM] * 6,
        out_specs=VMEM,
        scratch_shapes=[
            pltpu.VMEM((tokens, LANES), F32),
            pltpu.VMEM((tokens, WIDE), BF16),
            pltpu.VMEM((tokens, WIDE), BF16),
        ],
        compiler_params=params(),
        name="local_states",
    )(x, g, b, c, step[0], rate_row)
    rows = NS // n
    swapped = lax.all_to_all(states, "seq", split_axis=1, concat_axis=1, tiled=True)
    chained = pl.pallas_call(
        lambda *refs: chain_kernel(n, rows, *refs),
        out_shape=shape((2, NS, WIDE), BF16),
        in_specs=[VMEM],
        out_specs=VMEM,
        compiler_params=params(),
        name="chain_states",
    )(swapped)
    entering = lax.all_to_all(chained, "seq", split_axis=1, concat_axis=1, tiled=True)

    first = (lax.axis_index("seq") * per_device).astype(jnp.int32).reshape(1)
    columns = QUERY_HEADS * BLOCK
    attention, dq, dkv = pl.pallas_call(
        attention_kernel,
        out_shape=(
            shape((tokens, columns), F32),
            shape((tokens, columns), BF16),
            shape((every, 2 * LANES), BF16),
        ),
        in_specs=[SMEM, SMEM, VMEM, VMEM, VMEM],
        out_specs=(VMEM, VMEM, VMEM),
        scratch_shapes=[
            pltpu.SMEM((blocks + 1,), jnp.int32),
            pltpu.VMEM(((most + 1) // 2, 2 * BLOCK, columns), F32),
            pltpu.VMEM((every, 2 * LANES), F32),
            pltpu.VMEM((columns, LANES), BF16),
            pltpu.VMEM((columns, LANES), BF16),
            pltpu.VMEM((2 * BLOCK, columns), BF16),
            pltpu.VMEM((2 * BLOCK, columns), BF16),
            pltpu.VMEM((LANES, columns), F32),
            pltpu.VMEM((LANES, columns), F32),
            pltpu.VMEM((8, columns), F32),
        ],
        compiler_params=params(),
        name="attention",
    )(block_mask[0], first, q, g, kv_all)
    parts = lax.all_to_all(
        dkv.reshape(n, tokens, 2 * LANES), "seq", split_axis=0, concat_axis=0, tiled=True
    )

    y, dx, db, dc, sums = pl.pallas_call(
        ssm_kernel,
        out_shape=(
            shape((tokens, WIDE), BF16),
            shape((tokens, WIDE), BF16),
            shape((tokens, NS), BF16),
            shape((tokens, NS), BF16),
            shape((2 * HS, LANES), F32),
        ),
        in_specs=[VMEM] * 6 + [SMEM] + [VMEM] * 2,
        out_specs=(VMEM,) * 5,
        scratch_shapes=[
            pltpu.VMEM((tokens, LANES), F32),
            pltpu.VMEM((tokens, WIDE), BF16),
            pltpu.VMEM((tokens, WIDE), BF16),
            pltpu.VMEM((tokens, tokens), F32),
            pltpu.VMEM((tokens, tokens), F32),
            pltpu.VMEM((tokens, tokens), BF16),
            pltpu.VMEM((LANES, 2 * tokens), F32),
        ],
        compiler_params=params(),
        name="ssm",
    )(x, g, b, c, step[0], rate_row, skip_row, entering, attention)

    summed = lax.all_gather(jnp.sum(sums, axis=1), ("dp", "seq"), axis=0)
    totals = jnp.sum(summed, axis=0)
    tokens_all = lax.axis_size("dp") * n * tokens
    grad_rate_log = totals[:HS] / tokens_all
    grad_skip = totals[HS:] / (tokens_all * P_SIZE)
    owned = jnp.sum(parts.astype(F32), axis=0).astype(BF16)
    return (
        y[None],
        dq[None],
        owned[:, :LANES][None],
        owned[:, LANES:][None],
        dx[None],
        db[None],
        dc[None],
        grad_rate_log,
        grad_skip,
    )


def solution(mesh):
    split = P("dp", "seq", None)
    in_specs = (split,) * 7 + (P(), P(), P("dp", None, None), split)
    out_specs = (split,) * 7 + (P(), P())
    return jax.shard_map(body, mesh=mesh, in_specs=in_specs, out_specs=out_specs, check_vma=False)
```

```python
import jax
import jax.numpy as jnp
from jax import lax
from jax.experimental import pallas as pl
from jax.experimental.pallas import tpu as pltpu
from jax.sharding import PartitionSpec as P

HEAD_WIDTH = 128
QUERY_HEADS = 8
HS = 8
P_SIZE = 128
NS = 128
BLOCK = 128
WIDE = HS * P_SIZE
LANES = 128
FACTOR = HEAD_WIDTH ** (-0.5)
LOG2E = 1.4426950408889634
NEG = -1e30
HIGH = lax.Precision.HIGHEST
F32 = jnp.float32
BF16 = jnp.bfloat16

VMEM = pl.BlockSpec(memory_space=pltpu.VMEM)
SMEM = pl.BlockSpec(memory_space=pltpu.SMEM)


def params(limit=56 << 20):
    return pltpu.CompilerParams(vmem_limit_bytes=limit)


def cost(microseconds):
    return pl.CostEstimate(
        flops=int(microseconds * 1.1e9), bytes_accessed=1 << 20, transcendentals=0
    )


def dot(a, b, ca, cb, precision=None):
    return lax.dot_general(
        a, b, (((ca,), (cb,)), ((), ())), preferred_element_type=F32, precision=precision
    )


def head(h):
    return slice(h * LANES, (h + 1) * LANES)


def running_logs(step_ref, rate_ref, pad_ref):
    pad_ref[...] = jnp.zeros_like(pad_ref)
    for h in range(HS):
        rate = jnp.exp(jnp.full((1, 2 * BLOCK), rate_ref[h], F32))
        pad_ref[h : h + 1, :] = -step_ref[h : h + 1, :] * rate
    row = lax.broadcasted_iota(jnp.int32, (BLOCK, BLOCK), 0)
    col = lax.broadcasted_iota(jnp.int32, (BLOCK, BLOCK), 1)
    upper = jnp.where(row <= col, 1.0, 0.0).astype(F32)
    flat0 = dot(pad_ref[:, :BLOCK], upper, 1, 0, HIGH)
    flat1 = dot(pad_ref[:, BLOCK:], upper, 1, 0, HIGH)
    return flat0, flat1, flat0.T, flat1.T


def scaled(x_ref, column, out_ref):
    for h in range(HS):
        out_ref[:, head(h)] = (x_ref[:, head(h)].astype(F32) * column[:, h : h + 1]).astype(BF16)


def pieces(n):
    groups = max(1, (n * 16) // NS)
    return NS * groups // n, groups


def local_states_kernel(
    n, x_ref, g_ref, b_ref, c_ref, step_ref, rate_ref, out_ref, pad_ref, high_ref, rest_ref
):
    rows, groups = pieces(n)
    heads = HS // groups
    width = heads * LANES
    _, _, run0, run1 = running_logs(step_ref, rate_ref, pad_ref)
    t0, t1 = run0[BLOCK - 1 :, :], run1[BLOCK - 1 :, :]
    enter = jnp.exp(jnp.concatenate([run0, run1 + t0], axis=0))
    tail = jnp.exp(jnp.concatenate([(t0 - run0) + t1, t1 - run1], axis=0))
    total = t0 + t1
    high = total.astype(BF16).astype(F32)
    middle = (total - high).astype(BF16).astype(F32)
    low = total - high - middle
    place = lax.broadcasted_iota(jnp.int32, (rows, LANES), 0) % 4
    logs = jnp.where(place == 0, high, jnp.where(place == 1, middle, low))
    for direction, (left, right, column) in enumerate(((b_ref, x_ref, tail), (c_ref, g_ref, enter))):
        for h in range(HS):
            product = right[:, head(h)].astype(F32) * column[:, h : h + 1]
            rounded = product.astype(BF16)
            high_ref[:, head(h)] = rounded
            rest_ref[:, head(h)] = (product - rounded.astype(F32)).astype(BF16)
        state = (
            dot(left[...], high_ref[...], 0, 0) + dot(left[...], rest_ref[...], 0, 0)
        ).astype(BF16)
        for d in range(n):
            at = (d // groups) * rows
            shift = (d % groups) * heads
            out_ref[d, direction, :, :width] = state[
                at : at + rows, shift * LANES : shift * LANES + width
            ]
            own = logs if shift == 0 else pltpu.roll(logs, LANES - shift, 1)
            out_ref[d, direction, :, width:] = own.astype(BF16)


def chain_kernel(n, in_ref, out_ref, cross_ref, held_ref):
    rows, groups = pieces(n)
    heads = HS // groups
    width = heads * LANES
    logs = []
    for e in range(n):
        parts = in_ref[e, 0, :, width:].astype(F32)
        logs.append(parts[0:1, :] + parts[1:2, :] + parts[2:3, :])
    decays = [jnp.exp(log) for log in logs]
    cross_ref[...] = jnp.zeros_like(cross_ref)
    for h in range(heads):
        state = jnp.zeros((rows, LANES), F32)
        for e in range(n):
            held_ref[e] = state
            out_ref[e, 0, :, head(h)] = state.astype(BF16)
            state = state * decays[e][:, h : h + 1] + in_ref[e, 0, :, head(h)].astype(F32)
        state = jnp.zeros((rows, LANES), F32)
        cross = jnp.zeros((1, LANES), F32)
        for e in range(n - 1, -1, -1):
            out_ref[e, 1, :, head(h)] = state.astype(BF16)
            weight = (logs[e] * decays[e])[:, h : h + 1]
            cross += jnp.sum(state * held_ref[e], axis=0, keepdims=True) * weight
            state = state * decays[e][:, h : h + 1] + in_ref[e, 1, :, head(h)].astype(F32)
        cross_ref[h : h + 1, :] = cross


def attention_kernel(
    n, mask_ref, place_ref, q_ref, g_ref, *refs
):
    key_parts, value_parts = refs[:n], refs[n : 2 * n]
    out_ref, dq_ref = refs[2 * n : 2 * n + 2]
    dkv_parts = refs[2 * n + 2 : 3 * n + 2]
    (
        index_ref, kv_ref, s_ref, acc_ref, qs_ref, gs_ref, ds_ref, pr_ref, o_ref, dqt_ref, rows_ref,
    ) = refs[3 * n + 2 :]
    count = mask_ref.shape[0]
    columns = QUERY_HEADS * BLOCK
    tokens = q_ref.shape[0]
    me = place_ref[0]
    acc_ref[...] = jnp.zeros_like(acc_ref)
    for k in range(n):
        source = pl.ds(pl.multiple_of(lax.rem(me + n - k, n) * tokens, tokens), tokens)
        kv_ref[source, :LANES] = key_parts[k][...]
        kv_ref[source, LANES:] = value_parts[k][...]
    scale = FACTOR * LOG2E
    for block in range(tokens // BLOCK):
        at = slice(block * BLOCK, (block + 1) * BLOCK)
        row = me * (tokens // BLOCK) + block

        def note(j, n):
            @pl.when(mask_ref[row, j] == 1)
            def _():
                index_ref[n] = j

            return n + mask_ref[row, j]

        allowed = lax.fori_loop(0, count, note, 0)
        index_ref[allowed] = row
        pairs = (allowed + 1) // 2
        for h in range(QUERY_HEADS):
            qs_ref[head(h), :] = q_ref[at, head(h)]
            gs_ref[head(h), :] = g_ref[at, head(h)]

        def spans(t):
            first = pl.multiple_of(index_ref[2 * t] * BLOCK, BLOCK)
            second = pl.multiple_of(index_ref[2 * t + 1] * BLOCK, BLOCK)
            return pl.ds(first, BLOCK), pl.ds(second, BLOCK)

        def tile(t, lanes):
            one, two = spans(t)
            return jnp.concatenate([kv_ref[one, lanes], kv_ref[two, lanes]], axis=0)

        def scores_step(t, best):
            k_tile = tile(t, slice(0, LANES))
            live = 2 * t + 1 < allowed
            outs = []
            for part in range(columns // 256):
                lanes = slice(part * 256, (part + 1) * 256)
                s = dot(k_tile, qs_ref[lanes, :], 1, 1)
                low = s[:BLOCK]
                high = jnp.where(live, s[BLOCK:], NEG)
                s_ref[t, :BLOCK, lanes] = low
                s_ref[t, BLOCK:, lanes] = high
                both = jnp.maximum(low, high).reshape(BLOCK // 8, 8, 256)
                outs.append(jnp.maximum(best[part], jnp.max(both, axis=0)))
            return tuple(outs)

        best = lax.fori_loop(
            0, pairs, scores_step, tuple(jnp.full((8, 256), NEG, F32) for _ in range(columns // 256))
        )
        for part in range(columns // 256):
            lanes = slice(part * 256, (part + 1) * 256)
            rows_ref[0:1, lanes] = jnp.max(best[part], axis=0, keepdims=True) * scale
        o_ref[...] = jnp.zeros_like(o_ref)

        def weights_step(t, total):
            v_tile = tile(t, slice(LANES, 2 * LANES))
            outs = []
            for part in range(columns // 256):
                lanes = slice(part * 256, (part + 1) * 256)
                w = jnp.exp2(s_ref[t, :, lanes] * scale - rows_ref[0:1, lanes])
                s_ref[t, :, lanes] = w
                outs.append(total[part] + jnp.sum(w.reshape(32, 8, 256), axis=0))
                o_ref[:, lanes] += dot(v_tile, w.astype(BF16), 0, 0)
            return tuple(outs)

        total = lax.fori_loop(
            0, pairs, weights_step, tuple(jnp.zeros((8, 256), F32) for _ in range(columns // 256))
        )
        for part in range(columns // 256):
            lanes = slice(part * 256, (part + 1) * 256)
            inverse = 1.0 / jnp.sum(total[part], axis=0, keepdims=True)
            rows_ref[1:2, lanes] = inverse
            o = o_ref[:, lanes] * inverse
            o_ref[:, lanes] = o
            g_t = gs_ref[lanes, :].astype(F32).T
            rows_ref[2:3, lanes] = jnp.sum(o * g_t, axis=0, keepdims=True)
        for h in range(QUERY_HEADS):
            out_ref[at, head(h)] = o_ref[:, head(h)].T
        dqt_ref[...] = jnp.zeros_like(dqt_ref)

        def grads_step(t, carry):
            k_tile = tile(t, slice(0, LANES))
            v_tile = tile(t, slice(LANES, 2 * LANES))
            for part in range(columns // 256):
                lanes = slice(part * 256, (part + 1) * 256)
                dp = dot(v_tile, gs_ref[lanes, :], 1, 1)
                probs = s_ref[t, :, lanes] * rows_ref[1:2, lanes]
                ds = (probs * (dp - rows_ref[2:3, lanes])).astype(BF16)
                ds_ref[:, lanes] = ds
                pr_ref[:, lanes] = probs.astype(BF16)
                dqt_ref[:, lanes] += dot(k_tile, ds, 0, 0)
            dk = dot(ds_ref[...], qs_ref[...], 1, 0) * FACTOR
            dv = dot(pr_ref[...], gs_ref[...], 1, 0)
            one, two = spans(t)
            acc_ref[one, :LANES] += dk[:BLOCK]
            acc_ref[one, LANES:] += dv[:BLOCK]
            acc_ref[two, :LANES] += dk[BLOCK:]
            acc_ref[two, LANES:] += dv[BLOCK:]
            return carry

        lax.fori_loop(0, pairs, grads_step, 0)
        for h in range(QUERY_HEADS):
            dq_ref[at, head(h)] = (dqt_ref[:, head(h)].T * FACTOR).astype(BF16)
    for k in range(n):
        target = pl.ds(pl.multiple_of(lax.rem(me + k, n) * tokens, tokens), tokens)
        dkv_parts[k][...] = acc_ref[target, :].astype(BF16)


def owner_sum_kernel(*refs):
    parts, (dk_ref, dv_ref) = refs[:-2], refs[-2:]
    for out_ref, lanes in ((dk_ref, slice(0, LANES)), (dv_ref, slice(LANES, 2 * LANES))):
        total = parts[0][:, lanes].astype(F32)
        for part in parts[1:]:
            total += part[:, lanes].astype(F32)
        out_ref[...] = total.astype(BF16)


def ssm_kernel(
    n, x_ref, g_ref, b_ref, c_ref, step_ref, rate_ref, skip_ref, pieces_ref, cross_ref, att_ref,
    y_ref, dx_ref, db_ref, dc_ref, sums_ref,
    pad_ref, xt_ref, gt_ref, inner_ref, dinner_ref, m_ref, runt_ref, ent_ref,
):
    tokens = 2 * BLOCK
    rows, groups = pieces(n)
    width = HS // groups * LANES
    for d in range(n):
        at, lanes = (d // groups) * rows, (d % groups) * width
        ent_ref[:, at : at + rows, lanes : lanes + width] = pieces_ref[d]
    flat0, flat1, run0, run1 = running_logs(step_ref, rate_ref, pad_ref)
    t0, t1 = run0[BLOCK - 1 :, :], run1[BLOCK - 1 :, :]
    enter_log = jnp.concatenate([run0, run1 + t0], axis=0)
    tail_log = jnp.concatenate([(t0 - run0) + t1, t1 - run1], axis=0)
    enter, tail = jnp.exp(enter_log), jnp.exp(tail_log)
    scaled(x_ref, tail, xt_ref)
    scaled(g_ref, enter, gt_ref)
    own = jnp.concatenate([run0, run1], axis=0)
    runt_ref[:, :BLOCK] = flat0
    runt_ref[:, tokens : tokens + BLOCK] = flat0 - flat0[:, BLOCK - 1 :]
    runt_ref[:, tokens + BLOCK :] = flat1
    b = b_ref[...]
    c = c_ref[...]
    inner_ref[...] = dot(c, b, 1, 1)
    dinner_ref[...] = jnp.zeros_like(dinner_ref)
    row0 = lax.broadcasted_iota(jnp.int32, (BLOCK, BLOCK), 0)
    col0 = lax.broadcasted_iota(jnp.int32, (BLOCK, BLOCK), 1)
    row1 = lax.broadcasted_iota(jnp.int32, (BLOCK, tokens), 0)
    col1 = lax.broadcasted_iota(jnp.int32, (BLOCK, tokens), 1)
    seen0 = row0 >= col0
    seen1 = row1 + BLOCK >= col1
    m_ref[:BLOCK, BLOCK:] = jnp.zeros((BLOCK, BLOCK), BF16)
    for h in range(HS):
        lanes = head(h)
        x = x_ref[:, lanes]
        g = g_ref[:, lanes]
        xf, gf = x.astype(F32), g.astype(F32)
        gain = skip_ref[h]
        spread0 = jnp.where(seen0, own[:BLOCK, h : h + 1] - runt_ref[h : h + 1, :BLOCK], NEG)
        spread1 = jnp.where(seen1, own[BLOCK:, h : h + 1] - runt_ref[h : h + 1, tokens:], NEG)
        decay0, decay1 = jnp.exp(spread0), jnp.exp(spread1)
        dm = dot(g, x, 1, 1)
        e0, e1 = decay0 * dm[:BLOCK, :BLOCK], decay1 * dm[BLOCK:, :]
        m_ref[:BLOCK, :BLOCK] = (decay0 * inner_ref[:BLOCK, :BLOCK]).astype(BF16)
        m_ref[BLOCK:, :] = (decay1 * inner_ref[BLOCK:, :]).astype(BF16)
        dinner_ref[:BLOCK, :BLOCK] += e0
        dinner_ref[BLOCK:, :] += e1
        w0 = jnp.sum(spread0 * (e0 * inner_ref[:BLOCK, :BLOCK]), axis=0, keepdims=True)
        w1 = jnp.sum(spread1 * (e1 * inner_ref[BLOCK:, :]), axis=0, keepdims=True)
        rate = w0 + w1[:, :BLOCK] + w1[:, BLOCK:]
        h0 = ent_ref[0, :, lanes]
        later = ent_ref[1, :, lanes]
        carried = dot(c, h0, 1, 0) * enter[:, h : h + 1]
        back = dot(b, later, 1, 0) * tail[:, h : h + 1]
        m = m_ref[...]
        y = dot(m, x, 1, 0) + carried + gain * xf
        y_ref[:, lanes] = (y + att_ref[:, lanes]).astype(BF16)
        dx_ref[:, lanes] = (dot(m, g, 0, 0) + back + gain * gf).astype(BF16)
        rate += jnp.sum(
            gf * carried * enter_log[:, h : h + 1] + xf * back * tail_log[:, h : h + 1],
            axis=0,
            keepdims=True,
        )
        sums_ref[h : h + 1, :] = rate + cross_ref[h : h + 1, :]
        sums_ref[HS + h : HS + h + 1, :] = jnp.sum(gf * xf, axis=0, keepdims=True)
    dinner = dinner_ref[...].astype(BF16)
    dc = dot(dinner, b, 1, 0) + dot(gt_ref[...], ent_ref[0], 1, 1)
    db = dot(dinner, c, 0, 0) + dot(xt_ref[...], ent_ref[1], 1, 1)
    dc_ref[...] = dc.astype(BF16)
    db_ref[...] = db.astype(BF16)


def turned(array, axis, k):
    n = lax.axis_size(axis)
    return lax.ppermute(array, axis, [(i, (i + k) % n) for i in range(n)])


def everywhere(array, axis):
    return [array] + [turned(array, axis, k) for k in range(1, lax.axis_size(axis))]


def total_over(array, axis):
    return sum(everywhere(array, axis))


def body(query, key, value, ssm_input, in_b, in_c, step, rate_log, skip, block_mask, grad_out):
    n = lax.axis_size("seq")
    tokens = query.shape[1]
    blocks = block_mask.shape[1]
    most = 3 * blocks // 8
    every = blocks * BLOCK
    rows, groups = pieces(n)
    heads = HS // groups
    q, g, x = query[0], grad_out[0], ssm_input[0]
    b, c, steps = in_b[0], in_c[0], step[0].T
    shape = jax.ShapeDtypeStruct

    key_parts = everywhere(key[0], "seq")
    value_parts = everywhere(value[0], "seq")

    states = pl.pallas_call(
        lambda *refs: local_states_kernel(n, *refs),
        out_shape=shape((n, 2, rows, (heads + 1) * LANES), BF16),
        in_specs=[VMEM] * 5 + [SMEM],
        out_specs=VMEM,
        scratch_shapes=[
            pltpu.VMEM((LANES, tokens), F32),
            pltpu.VMEM((tokens, WIDE), BF16),
            pltpu.VMEM((tokens, WIDE), BF16),
        ],
        compiler_params=params(),
        cost_estimate=cost(3),
        name="local_states",
    )(x, g, b, c, steps, rate_log)
    swapped = lax.all_to_all(states, "seq", split_axis=0, concat_axis=0, tiled=True)
    chained, cross = pl.pallas_call(
        lambda *refs: chain_kernel(n, *refs),
        out_shape=(shape((n, 2, rows, heads * LANES), BF16), shape((HS, LANES), F32)),
        in_specs=[VMEM],
        out_specs=(VMEM, VMEM),
        scratch_shapes=[pltpu.VMEM((n, rows, LANES), F32)],
        compiler_params=params(),
        cost_estimate=cost(2),
        name="chain_states",
    )(swapped)
    if groups > 1:
        at = (lax.axis_index("seq") % groups) * heads
        cross = lax.dynamic_update_slice_in_dim(jnp.zeros_like(cross), cross[:heads], at, 0)
    entering = lax.all_to_all(chained, "seq", split_axis=0, concat_axis=0, tiled=True)

    place = lax.axis_index("seq").astype(jnp.int32).reshape(1)
    columns = QUERY_HEADS * BLOCK
    attention, dq, *dkv_parts = pl.pallas_call(
        lambda *refs: attention_kernel(n, *refs),
        out_shape=(shape((tokens, columns), F32), shape((tokens, columns), BF16))
        + (shape((tokens, 2 * LANES), BF16),) * n,
        in_specs=[SMEM, SMEM] + [VMEM] * (2 + 2 * n),
        out_specs=(VMEM,) * (2 + n),
        scratch_shapes=[
            pltpu.SMEM((blocks + 1,), jnp.int32),
            pltpu.VMEM((every, 2 * LANES), BF16),
            pltpu.VMEM(((most + 1) // 2, 2 * BLOCK, columns), F32),
            pltpu.VMEM((every, 2 * LANES), F32),
            pltpu.VMEM((columns, LANES), BF16),
            pltpu.VMEM((columns, LANES), BF16),
            pltpu.VMEM((2 * BLOCK, columns), BF16),
            pltpu.VMEM((2 * BLOCK, columns), BF16),
            pltpu.VMEM((LANES, columns), F32),
            pltpu.VMEM((LANES, columns), F32),
            pltpu.VMEM((8, columns), F32),
        ],
        compiler_params=params(),
        cost_estimate=cost(10),
        name="attention",
    )(block_mask[0], place, q, g, *key_parts, *value_parts)
    owned = [dkv_parts[0]] + [turned(dkv_parts[k], "seq", k) for k in range(1, n)]

    y, dx, db, dc, sums = pl.pallas_call(
        lambda *refs: ssm_kernel(n, *refs),
        out_shape=(
            shape((tokens, WIDE), BF16),
            shape((tokens, WIDE), BF16),
            shape((tokens, NS), BF16),
            shape((tokens, NS), BF16),
            shape((2 * HS, LANES), F32),
        ),
        in_specs=[VMEM] * 5 + [SMEM] * 2 + [VMEM] * 3,
        out_specs=(VMEM,) * 5,
        scratch_shapes=[
            pltpu.VMEM((LANES, tokens), F32),
            pltpu.VMEM((tokens, WIDE), BF16),
            pltpu.VMEM((tokens, WIDE), BF16),
            pltpu.VMEM((tokens, tokens), F32),
            pltpu.VMEM((tokens, tokens), F32),
            pltpu.VMEM((tokens, tokens), BF16),
            pltpu.VMEM((LANES, 2 * tokens), F32),
            pltpu.VMEM((2, NS, WIDE), BF16),
        ],
        compiler_params=params(),
        cost_estimate=cost(6),
        name="ssm",
    )(x, g, b, c, steps, rate_log, skip, entering, cross, attention)

    totals = jnp.sum(total_over(total_over(sums, "seq"), "dp"), axis=1)
    tokens_all = lax.axis_size("dp") * n * tokens
    grad_rate_log = totals[:HS] / tokens_all
    grad_skip = totals[HS:] / (tokens_all * P_SIZE)
    dk, dv = pl.pallas_call(
        owner_sum_kernel,
        out_shape=(shape((tokens, LANES), BF16),) * 2,
        in_specs=[VMEM] * n,
        out_specs=(VMEM, VMEM),
        compiler_params=params(),
        cost_estimate=cost(1),
        name="owner_sum",
    )(*owned)
    return (
        y[None],
        dq[None],
        dk[None],
        dv[None],
        dx[None],
        db[None],
        dc[None],
        grad_rate_log,
        grad_skip,
    )


def solution(mesh):
    split = P("dp", "seq", None)
    in_specs = (split,) * 7 + (P(), P(), P("dp", None, None), split)
    out_specs = (split,) * 7 + (P(), P())
    return jax.shard_map(body, mesh=mesh, in_specs=in_specs, out_specs=out_specs, check_vma=False)
```

```python
import jax
import jax.numpy as jnp
from jax import lax
from jax.experimental import pallas as pl
from jax.experimental.pallas import tpu as pltpu
from jax.sharding import PartitionSpec as P

HEAD_WIDTH = 128
QUERY_HEADS = 8
HS = 8
P_SIZE = 128
NS = 128
BLOCK = 128
WIDE = HS * P_SIZE
LANES = 128
FACTOR = HEAD_WIDTH ** (-0.5)
LOG2E = 1.4426950408889634
NEG = -1e30
HALF = NS // 2
HIGH = lax.Precision.HIGHEST
F32 = jnp.float32
BF16 = jnp.bfloat16

VMEM = pl.BlockSpec(memory_space=pltpu.VMEM)
SMEM = pl.BlockSpec(memory_space=pltpu.SMEM)


def params(limit=56 << 20):
    return pltpu.CompilerParams(vmem_limit_bytes=limit)


def cost(microseconds):
    return pl.CostEstimate(
        flops=int(microseconds * 1.1e9), bytes_accessed=1 << 20, transcendentals=0
    )


def dot(a, b, ca, cb, precision=None):
    return lax.dot_general(
        a, b, (((ca,), (cb,)), ((), ())), preferred_element_type=F32, precision=precision
    )


def head(h):
    return slice(h * LANES, (h + 1) * LANES)


def running_logs(step_ref, rate_ref, pad_ref):
    pad_ref[...] = jnp.zeros_like(pad_ref)
    for h in range(HS):
        rate = jnp.exp(jnp.full((1, 2 * BLOCK), rate_ref[h], F32))
        pad_ref[h : h + 1, :] = -step_ref[h : h + 1, :] * rate
    row = lax.broadcasted_iota(jnp.int32, (BLOCK, BLOCK), 0)
    col = lax.broadcasted_iota(jnp.int32, (BLOCK, BLOCK), 1)
    upper = jnp.where(row <= col, 1.0, 0.0).astype(F32)
    flat0 = dot(pad_ref[:, :BLOCK], upper, 1, 0, HIGH)
    flat1 = dot(pad_ref[:, BLOCK:], upper, 1, 0, HIGH)
    return flat0, flat1, flat0.T, flat1.T


def scaled(x_ref, column, out_ref):
    for h in range(HS):
        out_ref[:, head(h)] = (x_ref[:, head(h)].astype(F32) * column[:, h : h + 1]).astype(BF16)


def pack_kernel(key_ref, value_ref, out_ref):
    out_ref[:, :LANES] = key_ref[...]
    out_ref[:, LANES:] = value_ref[...]


def enter_and_tail(run0, run1):
    t0, t1 = run0[BLOCK - 1 :, :], run1[BLOCK - 1 :, :]
    enter = jnp.concatenate([run0, run1 + t0], axis=0)
    tail = jnp.concatenate([(t0 - run0) + t1, t1 - run1], axis=0)
    return enter, tail, t0 + t1


def local_states_kernel(
    place_ref, x_ref, g_ref, b_ref, c_ref, step_ref, rate_ref, keep_ref, give_ref,
    pad_ref, high_ref, rest_ref, log_ref, state_ref,
):
    core = place_ref[1]
    _, _, run0, run1 = running_logs(step_ref, rate_ref, pad_ref)
    enter_log, tail_log, total = enter_and_tail(run0, run1)
    enter, tail = jnp.exp(enter_log), jnp.exp(tail_log)
    high = total.astype(BF16).astype(F32)
    middle = (total - high).astype(BF16).astype(F32)
    low = total - high - middle
    index = lax.broadcasted_iota(jnp.int32, (HALF, LANES), 0)
    logs = jnp.where(index == 0, high, jnp.where(index == 1, middle, low)).astype(BF16)
    mine = pl.ds(pl.multiple_of(core * HALF, HALF), HALF)
    other = pl.ds(pl.multiple_of((1 - core) * HALF, HALF), HALF)
    cases = ((b_ref, x_ref, tail, tail_log), (c_ref, g_ref, enter, enter_log))
    for direction, (left, right, factor, weight) in enumerate(cases):
        for h in range(HS):
            product = right[:, head(h)].astype(F32) * factor[:, h : h + 1]
            rounded = product.astype(BF16)
            high_ref[:, head(h)] = rounded
            rest_ref[:, head(h)] = (product - rounded.astype(F32)).astype(BF16)
            log_ref[:, head(h)] = (product * weight[:, h : h + 1]).astype(BF16)
        turned_left = left[...].astype(F32).T.astype(BF16)
        state_ref[direction, :, :WIDE] = (
            dot(turned_left, high_ref[...], 1, 0) + dot(turned_left, rest_ref[...], 1, 0)
        ).astype(BF16)
        state_ref[3 - direction, :, :WIDE] = dot(turned_left, log_ref[...], 1, 0).astype(BF16)
    for kind in range(4):
        keep_ref[kind, :, :WIDE] = state_ref[kind, mine, :]
        keep_ref[kind, :, WIDE:] = logs
        give_ref[kind, :, :WIDE] = state_ref[kind, other, :]
        give_ref[kind, :, WIDE:] = logs


def log_row(ref, at):
    parts = ref[at + (slice(0, 16), slice(WIDE, WIDE + LANES))].astype(F32)
    return parts[0:1, :] + parts[1:2, :] + parts[2:3, :]


def combine_kernel(chips, place_ref, keep_ref, recv_ref, *message_refs):
    chip, core = place_ref[0], place_ref[1]
    is0 = core == 0
    log_mine, log_other = log_row(keep_ref, (0,)), log_row(recv_ref, (0,))
    log0, log1 = jnp.where(is0, log_mine, log_other), jnp.where(is0, log_other, log_mine)
    total = log0 + log1
    high = total.astype(BF16).astype(F32)
    middle = (total - high).astype(BF16).astype(F32)
    low = total - high - middle
    index = lax.broadcasted_iota(jnp.int32, (HALF, LANES), 0)
    logs = jnp.where(index == 0, high, jnp.where(index == 1, middle, low)).astype(BF16)
    decay0, decay1 = jnp.exp(log0), jnp.exp(log1)
    for h in range(HS):
        mine, other = keep_ref[0, :, head(h)].astype(F32), recv_ref[0, :, head(h)].astype(F32)
        first, second = jnp.where(is0, mine, other), jnp.where(is0, other, mine)
        state = (first * decay1[:, h : h + 1] + second).astype(BF16)
        mine, other = keep_ref[1, :, head(h)].astype(F32), recv_ref[1, :, head(h)].astype(F32)
        first, second = jnp.where(is0, mine, other), jnp.where(is0, other, mine)
        grad = (second * decay0[:, h : h + 1] + first).astype(BF16)
        for k in range(1, chips):
            later = chip + k < chips
            message_refs[k - 1][:, head(h)] = jnp.where(later, state, grad)
    for k in range(1, chips):
        message_refs[k - 1][:, WIDE:] = logs


def chain_kernel(chips, place_ref, keep_ref, recv_ref, sums_ref, *refs):
    message_refs = refs[: chips - 1]
    own_ref, give_ref, total_ref = refs[chips - 1 :]
    chip, core = place_ref[0], place_ref[1]
    is0 = core == 0
    log_mine, log_other = log_row(keep_ref, (0,)), log_row(recv_ref, (0,))
    log0, log1 = jnp.where(is0, log_mine, log_other), jnp.where(is0, log_other, log_mine)
    decay0, decay1 = jnp.exp(log0), jnp.exp(log1)
    weight0, weight1 = log0 * decay0, log1 * decay1
    factors = [None] + [jnp.exp(log_row(ref, ())) for ref in message_refs]
    total_ref[...] = sums_ref[...]
    for h in range(HS):
        column = slice(h, h + 1)
        states = [
            (keep_ref[kind, :, head(h)].astype(F32), recv_ref[kind, :, head(h)].astype(F32))
            for kind in range(4)
        ]
        (s0, s1), (g0, g1), (qs0, qs1), (qg0, qg1) = [
            (jnp.where(is0, mine, other), jnp.where(is0, other, mine)) for mine, other in states
        ]
        state = jnp.zeros((HALF, LANES), F32)
        for k in range(chips - 1, 0, -1):
            new = state * factors[k][:, column] + message_refs[k - 1][:, head(h)].astype(F32)
            state = jnp.where(k <= chip, new, state)
        grad = jnp.zeros((HALF, LANES), F32)
        for k in range(1, chips):
            new = grad * factors[k][:, column] + message_refs[k - 1][:, head(h)].astype(F32)
            grad = jnp.where(k > chip, new, grad)
        h0, l1 = state, grad
        h1 = h0 * decay0[:, column] + s0
        l0 = l1 * decay1[:, column] + g1
        cross = h0 * (l0 * weight0[:, column] + qs0) + h1 * (l1 * weight1[:, column] + qs1)
        cross += l0 * qg0 + l1 * qg1
        total_ref[h : h + 1, :] += jnp.sum(cross, axis=0, keepdims=True)
        h0, h1, l0, l1 = (value.astype(BF16) for value in (h0, h1, l0, l1))
        own_ref[0, :, head(h)] = jnp.where(is0, h0, h1)
        own_ref[1, :, head(h)] = jnp.where(is0, l0, l1)
        give_ref[0, :, head(h)] = jnp.where(is0, h1, h0)
        give_ref[1, :, head(h)] = jnp.where(is0, l1, l0)


def attention_kernel(
    chips, mask_ref, place_ref, after_ref, q_ref, g_ref, *refs
):
    kv_parts = refs[: 2 * chips]
    (
        out_ref, dq_ref, keep_ref, give_ref,
        index_ref, kv_ref, s_ref, acc_ref, qs_ref, gs_ref, ds_ref, pr_ref, o_ref, dqt_ref, rows_ref,
    ) = refs[2 * chips :]
    count = mask_ref.shape[0]
    columns = QUERY_HEADS * BLOCK
    tokens = q_ref.shape[0]
    chip, core = place_ref[0], place_ref[1]
    me = 2 * chip + core
    acc_ref[...] = jnp.zeros_like(acc_ref)
    for k in range(chips):
        for other in range(2):
            source = 2 * lax.rem(chip + chips - k, chips) + lax.rem(core + other, 2)
            at = pl.ds(pl.multiple_of(source * tokens, tokens), tokens)
            kv_ref[at, :] = kv_parts[2 * k + other][...]
    scale = FACTOR * LOG2E
    for block in range(tokens // BLOCK):
        at = slice(block * BLOCK, (block + 1) * BLOCK)
        row = me * (tokens // BLOCK) + block

        def note(j, n):
            @pl.when(mask_ref[row, j] == 1)
            def _():
                index_ref[n] = j

            return n + mask_ref[row, j]

        allowed = lax.fori_loop(0, count, note, 0)
        index_ref[allowed] = row
        pairs = (allowed + 1) // 2
        for h in range(QUERY_HEADS):
            qs_ref[head(h), :] = q_ref[at, head(h)]
            gs_ref[head(h), :] = g_ref[at, head(h)]

        def spans(t):
            first = pl.multiple_of(index_ref[2 * t] * BLOCK, BLOCK)
            second = pl.multiple_of(index_ref[2 * t + 1] * BLOCK, BLOCK)
            return pl.ds(first, BLOCK), pl.ds(second, BLOCK)

        def tile(t, lanes):
            one, two = spans(t)
            return jnp.concatenate([kv_ref[one, lanes], kv_ref[two, lanes]], axis=0)

        def scores_step(t, best):
            k_tile = tile(t, slice(0, LANES))
            live = 2 * t + 1 < allowed
            outs = []
            for part in range(columns // 256):
                lanes = slice(part * 256, (part + 1) * 256)
                s = dot(k_tile, qs_ref[lanes, :], 1, 1)
                low = s[:BLOCK]
                high = jnp.where(live, s[BLOCK:], NEG)
                s_ref[t, :BLOCK, lanes] = low
                s_ref[t, BLOCK:, lanes] = high
                both = jnp.maximum(low, high).reshape(BLOCK // 8, 8, 256)
                outs.append(jnp.maximum(best[part], jnp.max(both, axis=0)))
            return tuple(outs)

        best = lax.fori_loop(
            0, pairs, scores_step, tuple(jnp.full((8, 256), NEG, F32) for _ in range(columns // 256))
        )
        for part in range(columns // 256):
            lanes = slice(part * 256, (part + 1) * 256)
            rows_ref[0:1, lanes] = jnp.max(best[part], axis=0, keepdims=True) * scale
        o_ref[...] = jnp.zeros_like(o_ref)

        def weights_step(t, total):
            v_tile = tile(t, slice(LANES, 2 * LANES))
            outs = []
            for part in range(columns // 256):
                lanes = slice(part * 256, (part + 1) * 256)
                w = jnp.exp2(s_ref[t, :, lanes] * scale - rows_ref[0:1, lanes])
                s_ref[t, :, lanes] = w
                outs.append(total[part] + jnp.sum(w.reshape(32, 8, 256), axis=0))
                o_ref[:, lanes] += dot(v_tile, w.astype(BF16), 0, 0)
            return tuple(outs)

        total = lax.fori_loop(
            0, pairs, weights_step, tuple(jnp.zeros((8, 256), F32) for _ in range(columns // 256))
        )
        for part in range(columns // 256):
            lanes = slice(part * 256, (part + 1) * 256)
            inverse = 1.0 / jnp.sum(total[part], axis=0, keepdims=True)
            rows_ref[1:2, lanes] = inverse
            o = o_ref[:, lanes] * inverse
            o_ref[:, lanes] = o
            g_t = gs_ref[lanes, :].astype(F32).T
            rows_ref[2:3, lanes] = jnp.sum(o * g_t, axis=0, keepdims=True)
        for h in range(QUERY_HEADS):
            out_ref[at, head(h)] = o_ref[:, head(h)].T
        dqt_ref[...] = jnp.zeros_like(dqt_ref)

        def grads_step(t, carry):
            k_tile = tile(t, slice(0, LANES))
            v_tile = tile(t, slice(LANES, 2 * LANES))
            for part in range(columns // 256):
                lanes = slice(part * 256, (part + 1) * 256)
                dp = dot(v_tile, gs_ref[lanes, :], 1, 1)
                probs = s_ref[t, :, lanes] * rows_ref[1:2, lanes]
                ds = (probs * (dp - rows_ref[2:3, lanes])).astype(BF16)
                ds_ref[:, lanes] = ds
                pr_ref[:, lanes] = probs.astype(BF16)
                dqt_ref[:, lanes] += dot(k_tile, ds, 0, 0)
            dk = dot(ds_ref[...], qs_ref[...], 1, 0) * FACTOR
            dv = dot(pr_ref[...], gs_ref[...], 1, 0)
            one, two = spans(t)
            acc_ref[one, :LANES] += dk[:BLOCK]
            acc_ref[one, LANES:] += dv[:BLOCK]
            acc_ref[two, :LANES] += dk[BLOCK:]
            acc_ref[two, LANES:] += dv[BLOCK:]
            return carry

        lax.fori_loop(0, pairs, grads_step, 0)
        for h in range(QUERY_HEADS):
            dq_ref[at, head(h)] = (dqt_ref[:, head(h)].T * FACTOR).astype(BF16)
    for k in range(chips):
        mine = pl.multiple_of((2 * k + core) * tokens, tokens)
        other = pl.multiple_of((2 * k + 1 - core) * tokens, tokens)
        keep_ref[k] = acc_ref[pl.ds(mine, tokens), :].astype(BF16)
        give_ref[k] = acc_ref[pl.ds(other, tokens), :].astype(BF16)


def pair_sum_kernel(chips, place_ref, keep_ref, recv_ref, own_ref, *message_refs):
    chip = place_ref[0]
    own_ref[...] = keep_ref[chip].astype(F32) + recv_ref[chip].astype(F32)
    for k in range(1, chips):
        target = lax.rem(chip + k, chips)
        both = keep_ref[target].astype(F32) + recv_ref[target].astype(F32)
        message_refs[k - 1][...] = both.astype(BF16)


def owner_sum_kernel(*refs):
    parts, (dk_ref, dv_ref) = refs[:-2], refs[-2:]
    for out_ref, lanes in ((dk_ref, slice(0, LANES)), (dv_ref, slice(LANES, 2 * LANES))):
        total = parts[0][:, lanes].astype(F32)
        for part in parts[1:]:
            total += part[:, lanes].astype(F32)
        out_ref[...] = total.astype(BF16)


def inner_kernel(
    x_ref, g_ref, b_ref, c_ref, step_ref, rate_ref, skip_ref,
    y_ref, dx_ref, db_ref, dc_ref, sums_ref,
    pad_ref, inner_ref, dinner_ref, m_ref, runt_ref,
):
    tokens = 2 * BLOCK
    flat0, flat1, run0, run1 = running_logs(step_ref, rate_ref, pad_ref)
    own = jnp.concatenate([run0, run1], axis=0)
    runt_ref[:, :BLOCK] = flat0
    runt_ref[:, tokens : tokens + BLOCK] = flat0 - flat0[:, BLOCK - 1 :]
    runt_ref[:, tokens + BLOCK :] = flat1
    b = b_ref[...]
    c = c_ref[...]
    inner_ref[...] = dot(c, b, 1, 1)
    dinner_ref[...] = jnp.zeros_like(dinner_ref)
    row0 = lax.broadcasted_iota(jnp.int32, (BLOCK, BLOCK), 0)
    col0 = lax.broadcasted_iota(jnp.int32, (BLOCK, BLOCK), 1)
    row1 = lax.broadcasted_iota(jnp.int32, (BLOCK, tokens), 0)
    col1 = lax.broadcasted_iota(jnp.int32, (BLOCK, tokens), 1)
    seen0 = row0 >= col0
    seen1 = row1 + BLOCK >= col1
    m_ref[:BLOCK, BLOCK:] = jnp.zeros((BLOCK, BLOCK), BF16)
    for h in range(HS):
        lanes = head(h)
        x = x_ref[:, lanes]
        g = g_ref[:, lanes]
        xf, gf = x.astype(F32), g.astype(F32)
        gain = skip_ref[h]
        spread0 = jnp.where(seen0, own[:BLOCK, h : h + 1] - runt_ref[h : h + 1, :BLOCK], NEG)
        spread1 = jnp.where(seen1, own[BLOCK:, h : h + 1] - runt_ref[h : h + 1, tokens:], NEG)
        decay0, decay1 = jnp.exp(spread0), jnp.exp(spread1)
        dm = dot(g, x, 1, 1)
        e0, e1 = decay0 * dm[:BLOCK, :BLOCK], decay1 * dm[BLOCK:, :]
        m_ref[:BLOCK, :BLOCK] = (decay0 * inner_ref[:BLOCK, :BLOCK]).astype(BF16)
        m_ref[BLOCK:, :] = (decay1 * inner_ref[BLOCK:, :]).astype(BF16)
        dinner_ref[:BLOCK, :BLOCK] += e0
        dinner_ref[BLOCK:, :] += e1
        w0 = jnp.sum(spread0 * (e0 * inner_ref[:BLOCK, :BLOCK]), axis=0, keepdims=True)
        w1 = jnp.sum(spread1 * (e1 * inner_ref[BLOCK:, :]), axis=0, keepdims=True)
        m = m_ref[...]
        y_ref[:, lanes] = dot(m, x, 1, 0) + gain * xf
        dx_ref[:, lanes] = dot(m, g, 0, 0) + gain * gf
        sums_ref[h : h + 1, :] = w0 + w1[:, :BLOCK] + w1[:, BLOCK:]
        sums_ref[HS + h : HS + h + 1, :] = jnp.sum(gf * xf, axis=0, keepdims=True)
    dinner = dinner_ref[...].astype(BF16)
    dc_ref[...] = dot(dinner, b, 1, 0)
    db_ref[...] = dot(dinner, c, 0, 0)


def outer_kernel(
    place_ref, x_ref, g_ref, b_ref, c_ref, step_ref, rate_ref, own_ref, other_ref, att_ref,
    inner_y_ref, inner_dx_ref, inner_db_ref, inner_dc_ref,
    y_ref, dx_ref, db_ref, dc_ref,
    pad_ref, xt_ref, gt_ref, ent_ref,
):
    core = place_ref[1]
    ent_ref[:, pl.ds(pl.multiple_of(core * HALF, HALF), HALF), :] = own_ref[...]
    ent_ref[:, pl.ds(pl.multiple_of((1 - core) * HALF, HALF), HALF), :] = other_ref[...]
    _, _, run0, run1 = running_logs(step_ref, rate_ref, pad_ref)
    enter_log, tail_log, _ = enter_and_tail(run0, run1)
    enter, tail = jnp.exp(enter_log), jnp.exp(tail_log)
    scaled(x_ref, tail, xt_ref)
    scaled(g_ref, enter, gt_ref)
    b = b_ref[...]
    c = c_ref[...]
    for h in range(HS):
        lanes = head(h)
        carried = dot(c, ent_ref[0, :, lanes], 1, 0) * enter[:, h : h + 1]
        back = dot(b, ent_ref[1, :, lanes], 1, 0) * tail[:, h : h + 1]
        y_ref[:, lanes] = (inner_y_ref[:, lanes] + carried + att_ref[:, lanes]).astype(BF16)
        dx_ref[:, lanes] = (inner_dx_ref[:, lanes] + back).astype(BF16)
    dc_ref[...] = (inner_dc_ref[...] + dot(gt_ref[...], ent_ref[0], 1, 1)).astype(BF16)
    db_ref[...] = (inner_db_ref[...] + dot(xt_ref[...], ent_ref[1], 1, 1)).astype(BF16)


def swapped(array):
    return lax.ppermute(array, "seq", [(i, i ^ 1) for i in range(lax.axis_size("seq"))])


def from_chip(array, k):
    n = lax.axis_size("seq")
    return lax.ppermute(array, "seq", [(i, (i + 2 * k) % n) for i in range(n)])


def turned(array, k):
    n = lax.axis_size("dp")
    return lax.ppermute(array, "dp", [(i, (i + k) % n) for i in range(n)])


def call(kernel, outs, ins, scratch, microseconds, name):
    return pl.pallas_call(
        kernel,
        out_shape=tuple(jax.ShapeDtypeStruct(*out) for out in outs),
        in_specs=[SMEM if small else VMEM for small in ins],
        out_specs=(VMEM,) * len(outs),
        scratch_shapes=scratch,
        compiler_params=params(),
        cost_estimate=cost(microseconds),
        name=name,
    )


def body(query, key, value, ssm_input, in_b, in_c, step, rate_log, skip, block_mask, grad_out):
    n = lax.axis_size("seq")
    chips = n // 2
    tokens = query.shape[1]
    blocks = block_mask.shape[1]
    most = 3 * blocks // 8
    every = blocks * BLOCK
    q, g, x = query[0], grad_out[0], ssm_input[0]
    b, c, steps = in_b[0], in_c[0], step[0].T
    me = lax.axis_index("seq").astype(jnp.int32)
    place = jnp.stack([me // 2, me % 2])

    (kv,) = call(pack_kernel, [((tokens, 2 * LANES), BF16)], [0] * 2, [], 1, "pack_kv")(key[0], value[0])
    kv_parts = [kv, swapped(kv)]
    for k in range(1, chips):
        part = from_chip(kv, k)
        kv_parts += [part, swapped(part)]

    half = (4, HALF, WIDE + LANES)
    keep, give = call(
        local_states_kernel,
        [(half, BF16), (half, BF16)],
        [1] + [0] * 5 + [1],
        [
            pltpu.VMEM((LANES, tokens), F32),
            pltpu.VMEM((tokens, WIDE), BF16),
            pltpu.VMEM((tokens, WIDE), BF16),
            pltpu.VMEM((tokens, WIDE), BF16),
            pltpu.VMEM((4, NS, WIDE), BF16),
        ],
        4,
        "local_states",
    )(place, x, g, b, c, steps, rate_log)
    received = swapped(give)

    inner_y, inner_dx, inner_db, inner_dc, sums = call(
        inner_kernel,
        [((tokens, WIDE), F32)] * 2 + [((tokens, NS), F32)] * 2 + [((2 * HS, LANES), F32)],
        [0] * 5 + [1] * 2,
        [
            pltpu.VMEM((LANES, tokens), F32),
            pltpu.VMEM((tokens, tokens), F32),
            pltpu.VMEM((tokens, tokens), F32),
            pltpu.VMEM((tokens, tokens), BF16),
            pltpu.VMEM((LANES, 2 * tokens), F32),
        ],
        5,
        "chunk_inner",
    )(x, g, b, c, steps, rate_log, skip)

    messages = call(
        lambda *refs: combine_kernel(chips, *refs),
        [((HALF, WIDE + LANES), BF16)] * (chips - 1),
        [1, 0, 0],
        [],
        1,
        "combine_states",
    )(place, keep, received)
    arrived = [from_chip(messages[k - 1], k) for k in range(1, chips)]
    entering = ((2, HALF, WIDE), BF16)
    own, give, totals = call(
        lambda *refs: chain_kernel(chips, *refs),
        [entering, entering, ((2 * HS, LANES), F32)],
        [1] + [0] * (2 + chips),
        [],
        2,
        "chain_states",
    )(place, keep, received, sums, *arrived)
    other = swapped(give)

    totals = totals + swapped(totals)
    totals = totals + sum(from_chip(totals, k) for k in range(1, chips))
    totals = totals + sum(turned(totals, k) for k in range(1, lax.axis_size("dp")))
    totals = jnp.sum(totals, axis=1)
    tokens_all = lax.axis_size("dp") * n * tokens
    grad_rate_log = totals[:HS] / tokens_all
    grad_skip = totals[HS:] / (tokens_all * P_SIZE)

    columns = QUERY_HEADS * BLOCK
    split = ((chips, tokens, 2 * LANES), BF16)
    attention, dq, keep, give = call(
        lambda *refs: attention_kernel(chips, *refs),
        [((tokens, columns), F32), ((tokens, columns), BF16), split, split],
        [1, 1] + [0] * (3 + n),
        [
            pltpu.SMEM((blocks + 1,), jnp.int32),
            pltpu.VMEM((every, 2 * LANES), BF16),
            pltpu.VMEM(((most + 1) // 2, 2 * BLOCK, columns), F32),
            pltpu.VMEM((every, 2 * LANES), F32),
            pltpu.VMEM((columns, LANES), BF16),
            pltpu.VMEM((columns, LANES), BF16),
            pltpu.VMEM((2 * BLOCK, columns), BF16),
            pltpu.VMEM((2 * BLOCK, columns), BF16),
            pltpu.VMEM((LANES, columns), F32),
            pltpu.VMEM((LANES, columns), F32),
            pltpu.VMEM((8, columns), F32),
        ],
        10,
        "attention",
    )(block_mask[0], place, sums, q, g, *kv_parts)
    partial, *messages = call(
        lambda *refs: pair_sum_kernel(chips, *refs),
        [((tokens, 2 * LANES), F32)] + [((tokens, 2 * LANES), BF16)] * (chips - 1),
        [1, 0, 0],
        [],
        1,
        "pair_sum",
    )(place, keep, swapped(give))
    owned = [partial] + [from_chip(messages[k - 1], k) for k in range(1, chips)]

    y, dx, db, dc = call(
        outer_kernel,
        [((tokens, WIDE), BF16)] * 2 + [((tokens, NS), BF16)] * 2,
        [1] + [0] * 5 + [1] + [0] * 7,
        [
            pltpu.VMEM((LANES, tokens), F32),
            pltpu.VMEM((tokens, WIDE), BF16),
            pltpu.VMEM((tokens, WIDE), BF16),
            pltpu.VMEM((2, NS, WIDE), BF16),
        ],
        3,
        "chunk_outer",
    )(place, x, g, b, c, steps, rate_log, own, other, attention, inner_y, inner_dx, inner_db, inner_dc)

    dk, dv = call(
        owner_sum_kernel, [((tokens, LANES), BF16)] * 2, [0] * chips, [], 1, "owner_sum"
    )(*owned)
    return (
        y[None],
        dq[None],
        dk[None],
        dv[None],
        dx[None],
        db[None],
        dc[None],
        grad_rate_log,
        grad_skip,
    )


def solution(mesh):
    split = P("dp", "seq", None)
    in_specs = (split,) * 7 + (P(), P(), P("dp", None, None), split)
    out_specs = (split,) * 7 + (P(), P())
    return jax.shard_map(body, mesh=mesh, in_specs=in_specs, out_specs=out_specs, check_vma=False)
```

```python
import jax
import jax.numpy as jnp
from jax import lax
from jax.experimental import pallas as pl
from jax.experimental.pallas import tpu as pltpu
from jax.sharding import PartitionSpec as P

HEAD_WIDTH = 128
QUERY_HEADS = 8
HS = 8
P_SIZE = 128
NS = 128
BLOCK = 128
WIDE = HS * P_SIZE
LANES = 128
FACTOR = HEAD_WIDTH ** (-0.5)
LOG2E = 1.4426950408889634
NEG = -1e30
HALF = NS // 2
HIGH = lax.Precision.HIGHEST
F32 = jnp.float32
BF16 = jnp.bfloat16

VMEM = pl.BlockSpec(memory_space=pltpu.VMEM)
SMEM = pl.BlockSpec(memory_space=pltpu.SMEM)
AFTER = pl.BlockSpec(memory_space=pl.ANY)


def params(limit=56 << 20):
    return pltpu.CompilerParams(vmem_limit_bytes=limit)


def cost(microseconds):
    return pl.CostEstimate(
        flops=int(microseconds * 1.1e9), bytes_accessed=1 << 20, transcendentals=0
    )


def dot(a, b, ca, cb, precision=None):
    return lax.dot_general(
        a, b, (((ca,), (cb,)), ((), ())), preferred_element_type=F32, precision=precision
    )


def head(h):
    return slice(h * LANES, (h + 1) * LANES)


def running_logs(step_ref, rate_ref, pad_ref):
    pad_ref[...] = jnp.zeros_like(pad_ref)
    for h in range(HS):
        rate = jnp.exp(jnp.full((1, 2 * BLOCK), rate_ref[h], F32))
        pad_ref[h : h + 1, :] = -step_ref[h : h + 1, :] * rate
    row = lax.broadcasted_iota(jnp.int32, (BLOCK, BLOCK), 0)
    col = lax.broadcasted_iota(jnp.int32, (BLOCK, BLOCK), 1)
    upper = jnp.where(row <= col, 1.0, 0.0).astype(F32)
    flat0 = dot(pad_ref[:, :BLOCK], upper, 1, 0, HIGH)
    flat1 = dot(pad_ref[:, BLOCK:], upper, 1, 0, HIGH)
    return flat0, flat1, flat0.T, flat1.T


def scaled(x_ref, column, out_ref):
    for h in range(HS):
        out_ref[:, head(h)] = (x_ref[:, head(h)].astype(F32) * column[:, h : h + 1]).astype(BF16)


def chip_and_core():
    me = lax.axis_index("seq")
    return me // 2, me % 2


def pack_kernel(key_ref, value_ref, out_ref):
    out_ref[:, :LANES] = key_ref[...]
    out_ref[:, LANES:] = value_ref[...]


def enter_and_tail(run0, run1):
    t0, t1 = run0[BLOCK - 1 :, :], run1[BLOCK - 1 :, :]
    enter = jnp.concatenate([run0, run1 + t0], axis=0)
    tail = jnp.concatenate([(t0 - run0) + t1, t1 - run1], axis=0)
    return enter, tail, t0 + t1


def local_states_kernel(
    x_ref, g_ref, b_ref, c_ref, step_ref, rate_ref, keep_ref, give_ref,
    pad_ref, high_ref, rest_ref, log_ref, state_ref,
):
    _, core = chip_and_core()
    _, _, run0, run1 = running_logs(step_ref, rate_ref, pad_ref)
    enter_log, tail_log, total = enter_and_tail(run0, run1)
    enter, tail = jnp.exp(enter_log), jnp.exp(tail_log)
    logs = jnp.broadcast_to(total, (HALF, LANES))
    mine = pl.ds(pl.multiple_of(core * HALF, HALF), HALF)
    other = pl.ds(pl.multiple_of((1 - core) * HALF, HALF), HALF)
    cases = ((b_ref, x_ref, tail, tail_log), (c_ref, g_ref, enter, enter_log))
    for direction, (left, right, factor, weight) in enumerate(cases):
        for h in range(HS):
            product = right[:, head(h)].astype(F32) * factor[:, h : h + 1]
            rounded = product.astype(BF16)
            high_ref[:, head(h)] = rounded
            rest_ref[:, head(h)] = (product - rounded.astype(F32)).astype(BF16)
            log_ref[:, head(h)] = (product * weight[:, h : h + 1]).astype(BF16)
        turned_left = left[...].astype(F32).T.astype(BF16)
        state_ref[direction] = dot(turned_left, high_ref[...], 1, 0) + dot(
            turned_left, rest_ref[...], 1, 0
        )
        state_ref[3 - direction] = dot(turned_left, log_ref[...], 1, 0)
    for kind in range(4):
        keep_ref[kind, :, :WIDE] = state_ref[kind, mine, :]
        keep_ref[kind, :, WIDE:] = logs
        give_ref[kind, :, :WIDE] = state_ref[kind, other, :]
        give_ref[kind, :, WIDE:] = logs


def three_parts(value, rows):
    high = value.astype(BF16).astype(F32)
    middle = (value - high).astype(BF16).astype(F32)
    low = value - high - middle
    index = lax.broadcasted_iota(jnp.int32, (rows, LANES), 0)
    return jnp.where(index == 0, high, jnp.where(index == 1, middle, low)).astype(BF16)


def pair_logs(keep_ref, recv_ref, is0):
    mine, other = keep_ref[0, 0:1, WIDE:], recv_ref[0, 0:1, WIDE:]
    return jnp.where(is0, mine, other), jnp.where(is0, other, mine)


def combine_kernel(chips, keep_ref, recv_ref, *message_refs):
    chip, core = chip_and_core()
    is0 = core == 0
    log0, log1 = pair_logs(keep_ref, recv_ref, is0)
    logs = three_parts(log0 + log1, HALF)
    decay0, decay1 = jnp.exp(log0), jnp.exp(log1)
    for h in range(HS):
        mine, other = keep_ref[0, :, head(h)], recv_ref[0, :, head(h)]
        first, second = jnp.where(is0, mine, other), jnp.where(is0, other, mine)
        state = (first * decay1[:, h : h + 1] + second).astype(BF16)
        mine, other = keep_ref[1, :, head(h)], recv_ref[1, :, head(h)]
        first, second = jnp.where(is0, mine, other), jnp.where(is0, other, mine)
        grad = (second * decay0[:, h : h + 1] + first).astype(BF16)
        for k in range(1, chips):
            later = chip + k < chips
            message_refs[k - 1][:, head(h)] = jnp.where(later, state, grad)
    for k in range(1, chips):
        message_refs[k - 1][:, WIDE:] = logs


def chain_kernel(chips, keep_ref, recv_ref, sums_ref, *refs):
    message_refs = refs[: chips - 1]
    own_ref, give_ref, total_ref = refs[chips - 1 :]
    chip, core = chip_and_core()
    is0 = core == 0
    log0, log1 = pair_logs(keep_ref, recv_ref, is0)
    decay0, decay1 = jnp.exp(log0), jnp.exp(log1)
    weight0, weight1 = log0 * decay0, log1 * decay1
    factors = [None]
    for ref in message_refs:
        parts = ref[:16, WIDE:].astype(F32)
        factors.append(jnp.exp(parts[0:1, :] + parts[1:2, :] + parts[2:3, :]))
    total_ref[...] = sums_ref[...]
    for h in range(HS):
        column = slice(h, h + 1)
        states = [(keep_ref[kind, :, head(h)], recv_ref[kind, :, head(h)]) for kind in range(4)]
        (s0, s1), (g0, g1), (qs0, qs1), (qg0, qg1) = [
            (jnp.where(is0, mine, other), jnp.where(is0, other, mine)) for mine, other in states
        ]
        state = jnp.zeros((HALF, LANES), F32)
        for k in range(chips - 1, 0, -1):
            new = state * factors[k][:, column] + message_refs[k - 1][:, head(h)].astype(F32)
            state = jnp.where(k <= chip, new, state)
        grad = jnp.zeros((HALF, LANES), F32)
        for k in range(1, chips):
            new = grad * factors[k][:, column] + message_refs[k - 1][:, head(h)].astype(F32)
            grad = jnp.where(k > chip, new, grad)
        h0, l1 = state, grad
        h1 = h0 * decay0[:, column] + s0
        l0 = l1 * decay1[:, column] + g1
        cross = h0 * (l0 * weight0[:, column] + qs0) + h1 * (l1 * weight1[:, column] + qs1)
        cross += l0 * qg0 + l1 * qg1
        total_ref[h : h + 1, :] += jnp.sum(cross, axis=0, keepdims=True)
        h0, h1, l0, l1 = (value.astype(BF16) for value in (h0, h1, l0, l1))
        own_ref[0, :, head(h)] = jnp.where(is0, h0, h1)
        own_ref[1, :, head(h)] = jnp.where(is0, l0, l1)
        give_ref[0, :, head(h)] = jnp.where(is0, h1, h0)
        give_ref[1, :, head(h)] = jnp.where(is0, l1, l0)


def attention_kernel(chips, most, mask_ref, q_ref, g_ref, *refs):
    kv_parts = refs[: 2 * chips]
    (
        _, out_ref, dq_ref, keep_ref, give_ref,
        kv_ref, acc_ref, k_ref, k_live_ref, v_ref, q_turned_ref, g_turned_ref, ds_ref, pr_ref,
    ) = refs[2 * chips :]
    count = mask_ref.shape[0]
    columns = QUERY_HEADS * BLOCK
    tokens = q_ref.shape[0]
    chip, core = chip_and_core()
    me = 2 * chip + core
    scale = FACTOR * LOG2E
    acc_ref[...] = jnp.zeros_like(acc_ref)
    for k in range(chips):
        for other in range(2):
            source = 2 * lax.rem(chip + chips - k, chips) + lax.rem(core + other, 2)
            at = pl.ds(pl.multiple_of(source * tokens, tokens), tokens)
            kv_ref[at, :] = kv_parts[2 * k + other][...]

    def nth(row, slot):
        def look(j, carry):
            found, seen = carry
            hit = (mask_ref[row, j] == 1) & (seen == slot)
            return jnp.where(hit, j, found), seen + mask_ref[row, j]

        return lax.fori_loop(0, count, look, (row, 0))

    lower, upper = slice(0, LANES), slice(LANES, 2 * LANES)
    for block in range(tokens // BLOCK):
        at = slice(block * BLOCK, (block + 1) * BLOCK)
        row = me * (tokens // BLOCK) + block
        slots = []
        for slot in range(most):
            index, allowed = nth(row, slot)
            live = slot < allowed
            slots.append((index, live))
            source = pl.ds(pl.multiple_of(index * BLOCK, BLOCK), BLOCK)
            target = slice(slot * BLOCK, (slot + 1) * BLOCK)
            k_tile, v_tile = kv_ref[source, lower], kv_ref[source, upper]
            k_ref[target, :] = k_tile
            k_live_ref[target, :] = jnp.where(live, k_tile, jnp.zeros_like(k_tile))
            v_ref[target, lower] = jnp.where(live, v_tile, jnp.zeros_like(v_tile))
            v_ref[target, upper] = jnp.full((BLOCK, LANES), jnp.where(live, 1.0, 0.0), F32).astype(BF16)
        for h in range(QUERY_HEADS):
            rows = slice(h * BLOCK, (h + 1) * BLOCK)
            q_turned_ref[:, rows] = q_ref[at, head(h)].T
            g_turned_ref[:, rows] = g_ref[at, head(h)].T
        group = 2
        for first in range(0, QUERY_HEADS, group):
            heads = range(first, first + group)
            rows = slice(first * BLOCK, (first + group) * BLOCK)
            q = jnp.concatenate([q_ref[at, head(h)] for h in heads], axis=0)
            g = jnp.concatenate([g_ref[at, head(h)] for h in heads], axis=0)
            scores = dot(q, k_ref[...], 1, 1)
            best = jnp.max(scores, axis=1, keepdims=True)
            weights = jnp.exp2((scores - best) * scale)
            both = dot(weights.astype(BF16), v_ref[...], 1, 0)
            inverse = 1.0 / both[:, upper]
            out = both[:, lower] * inverse
            delta = jnp.sum(out * g.astype(F32), axis=1, keepdims=True)
            probs = weights * jnp.concatenate([inverse] * most, axis=1)
            dprobs = dot(g, v_ref[:, lower], 1, 1)
            ds = (probs * (dprobs - delta)).astype(BF16)
            pr_ref[rows, :] = probs.astype(BF16)
            ds_ref[rows, :] = ds
            dq = (dot(ds, k_live_ref[...], 1, 0) * FACTOR).astype(BF16)
            for place, h in enumerate(heads):
                part = slice(place * BLOCK, (place + 1) * BLOCK)
                out_ref[at, head(h)] = out[part]
                dq_ref[at, head(h)] = dq[part]
        dk = dot(q_turned_ref[...], ds_ref[...], 1, 0)
        dv = dot(g_turned_ref[...], pr_ref[...], 1, 0)
        for slot, (index, live) in enumerate(slots):
            source = slice(slot * BLOCK, (slot + 1) * BLOCK)

            @pl.when(live)
            def _():
                target = pl.ds(pl.multiple_of(index * BLOCK, BLOCK), BLOCK)
                acc_ref[lower, target] += dk[:, source]
                acc_ref[upper, target] += dv[:, source]

    for k in range(chips):
        mine = pl.multiple_of((2 * k + core) * tokens, tokens)
        other = pl.multiple_of((2 * k + 1 - core) * tokens, tokens)
        keep_ref[k] = acc_ref[:, pl.ds(mine, tokens)].astype(BF16)
        give_ref[k] = acc_ref[:, pl.ds(other, tokens)].astype(BF16)


def pair_sum_kernel(chips, keep_ref, recv_ref, sums_ref, other_ref, own_ref, total_ref, *message_refs):
    chip, _ = chip_and_core()
    rows = own_ref.shape[0]
    own_ref[...] = keep_ref[chip].astype(F32) + recv_ref[chip].astype(F32)
    total = sums_ref[...] + other_ref[...]
    total_ref[...] = total
    high = total.astype(BF16)
    middle = (total - high.astype(F32)).astype(BF16)
    low = (total - high.astype(F32) - middle.astype(F32)).astype(BF16)
    tail = jnp.concatenate(
        [
            jnp.concatenate([high, middle], axis=1),
            jnp.concatenate([low, jnp.zeros_like(low)], axis=1),
        ],
        axis=0,
    )
    for k in range(1, chips):
        target = lax.rem(chip + k, chips)
        both = keep_ref[target].astype(F32) + recv_ref[target].astype(F32)
        message_refs[k - 1][:rows, :] = both.astype(BF16)
        message_refs[k - 1][rows:, :] = tail


def owner_sum_kernel(chips, tokens_all, own_ref, sums_ref, *refs):
    parts, (dk_ref, dv_ref, rate_ref, skip_ref) = refs[: chips - 1], refs[chips - 1 :]
    rows = own_ref.shape[0]
    total = own_ref[...]
    sums = sums_ref[...]
    for part in parts:
        total += part[:rows, :].astype(F32)
        tail = part[rows:, :].astype(F32)
        sums += tail[:16, :LANES] + tail[:16, LANES:] + tail[16:, :LANES]
    dk_ref[...] = (total[:LANES].T * FACTOR).astype(BF16)
    dv_ref[...] = total[LANES:].T.astype(BF16)
    ones = jnp.ones((8, LANES), F32)
    rate = dot(ones, sums[:HS], 1, 1, HIGH) * (1.0 / tokens_all)
    skip = dot(ones, sums[HS:], 1, 1, HIGH) * (1.0 / (tokens_all * P_SIZE))
    rate_ref[...] = rate[0:1, :]
    skip_ref[...] = skip[0:1, :]


def inner_kernel(
    x_ref, g_ref, b_ref, c_ref, step_ref, rate_ref, skip_ref, _,
    y_ref, dx_ref, db_ref, dc_ref, sums_ref,
    pad_ref, inner_ref, dinner_ref, m_ref, runt_ref,
):
    tokens = 2 * BLOCK
    flat0, flat1, run0, run1 = running_logs(step_ref, rate_ref, pad_ref)
    own = jnp.concatenate([run0, run1], axis=0)
    runt_ref[:, :BLOCK] = flat0
    runt_ref[:, tokens : tokens + BLOCK] = flat0 - flat0[:, BLOCK - 1 :]
    runt_ref[:, tokens + BLOCK :] = flat1
    b = b_ref[...]
    c = c_ref[...]
    inner_ref[...] = dot(c, b, 1, 1)
    dinner_ref[...] = jnp.zeros_like(dinner_ref)
    row0 = lax.broadcasted_iota(jnp.int32, (BLOCK, BLOCK), 0)
    col0 = lax.broadcasted_iota(jnp.int32, (BLOCK, BLOCK), 1)
    row1 = lax.broadcasted_iota(jnp.int32, (BLOCK, tokens), 0)
    col1 = lax.broadcasted_iota(jnp.int32, (BLOCK, tokens), 1)
    seen0 = row0 >= col0
    seen1 = row1 + BLOCK >= col1
    m_ref[:BLOCK, BLOCK:] = jnp.zeros((BLOCK, BLOCK), BF16)
    for h in range(HS):
        lanes = head(h)
        x = x_ref[:, lanes]
        g = g_ref[:, lanes]
        xf, gf = x.astype(F32), g.astype(F32)
        gain = skip_ref[h]
        spread0 = jnp.where(seen0, own[:BLOCK, h : h + 1] - runt_ref[h : h + 1, :BLOCK], NEG)
        spread1 = jnp.where(seen1, own[BLOCK:, h : h + 1] - runt_ref[h : h + 1, tokens:], NEG)
        decay0, decay1 = jnp.exp(spread0), jnp.exp(spread1)
        dm = dot(g, x, 1, 1)
        e0, e1 = decay0 * dm[:BLOCK, :BLOCK], decay1 * dm[BLOCK:, :]
        m_ref[:BLOCK, :BLOCK] = (decay0 * inner_ref[:BLOCK, :BLOCK]).astype(BF16)
        m_ref[BLOCK:, :] = (decay1 * inner_ref[BLOCK:, :]).astype(BF16)
        dinner_ref[:BLOCK, :BLOCK] += e0
        dinner_ref[BLOCK:, :] += e1
        w0 = jnp.sum(spread0 * (e0 * inner_ref[:BLOCK, :BLOCK]), axis=0, keepdims=True)
        w1 = jnp.sum(spread1 * (e1 * inner_ref[BLOCK:, :]), axis=0, keepdims=True)
        m = m_ref[...]
        y_ref[:, lanes] = dot(m, x, 1, 0) + gain * xf
        dx_ref[:, lanes] = dot(m, g, 0, 0) + gain * gf
        sums_ref[h : h + 1, :] = w0 + w1[:, :BLOCK] + w1[:, BLOCK:]
        sums_ref[HS + h : HS + h + 1, :] = jnp.sum(gf * xf, axis=0, keepdims=True)
    dinner = dinner_ref[...].astype(BF16)
    dc_ref[...] = dot(dinner, b, 1, 0)
    db_ref[...] = dot(dinner, c, 0, 0)


def outer_kernel(
    x_ref, g_ref, b_ref, c_ref, step_ref, rate_ref, own_ref, other_ref, att_ref,
    inner_y_ref, inner_dx_ref, inner_db_ref, inner_dc_ref, _,
    y_ref, dx_ref, db_ref, dc_ref,
    pad_ref, xt_ref, gt_ref, ent_ref,
):
    _, core = chip_and_core()
    ent_ref[:, pl.ds(pl.multiple_of(core * HALF, HALF), HALF), :] = own_ref[...]
    ent_ref[:, pl.ds(pl.multiple_of((1 - core) * HALF, HALF), HALF), :] = other_ref[...]
    _, _, run0, run1 = running_logs(step_ref, rate_ref, pad_ref)
    enter_log, tail_log, _ = enter_and_tail(run0, run1)
    enter, tail = jnp.exp(enter_log), jnp.exp(tail_log)
    scaled(x_ref, tail, xt_ref)
    scaled(g_ref, enter, gt_ref)
    b = b_ref[...]
    c = c_ref[...]
    for h in range(HS):
        lanes = head(h)
        carried = dot(c, ent_ref[0, :, lanes], 1, 0) * enter[:, h : h + 1]
        back = dot(b, ent_ref[1, :, lanes], 1, 0) * tail[:, h : h + 1]
        y_ref[:, lanes] = (inner_y_ref[:, lanes] + carried + att_ref[:, lanes]).astype(BF16)
        dx_ref[:, lanes] = (inner_dx_ref[:, lanes] + back).astype(BF16)
    dc_ref[...] = (inner_dc_ref[...] + dot(gt_ref[...], ent_ref[0], 1, 1)).astype(BF16)
    db_ref[...] = (inner_db_ref[...] + dot(xt_ref[...], ent_ref[1], 1, 1)).astype(BF16)


def swapped(array):
    return lax.ppermute(array, "seq", [(i, i ^ 1) for i in range(lax.axis_size("seq"))])


def from_chip(array, k):
    n = lax.axis_size("seq")
    return lax.ppermute(array, "seq", [(i, (i + 2 * k) % n) for i in range(n)])


def turned(array, k):
    n = lax.axis_size("dp")
    return lax.ppermute(array, "dp", [(i, (i + k) % n) for i in range(n)])


def call(kernel, outs, ins, scratch, microseconds, name):
    return pl.pallas_call(
        kernel,
        out_shape=tuple(jax.ShapeDtypeStruct(*out) for out in outs),
        in_specs=ins,
        out_specs=(VMEM,) * len(outs),
        scratch_shapes=scratch,
        compiler_params=params(),
        cost_estimate=cost(microseconds),
        name=name,
    )


def body(query, key, value, ssm_input, in_b, in_c, step, rate_log, skip, block_mask, grad_out):
    n = lax.axis_size("seq")
    chips = n // 2
    tokens = query.shape[1]
    blocks = block_mask.shape[1]
    most = 3 * blocks // 8
    every = blocks * BLOCK
    q, g, x = query[0], grad_out[0], ssm_input[0]
    b, c, steps = in_b[0], in_c[0], step[0].T

    (kv,) = call(pack_kernel, [((tokens, 2 * LANES), BF16)], [VMEM] * 2, [], 1, "pack_kv")(
        key[0], value[0]
    )
    kv_parts = [kv, swapped(kv)]
    for k in range(1, chips):
        part = from_chip(kv, k)
        kv_parts += [part, swapped(part)]

    half = ((4, HALF, WIDE + LANES), F32)
    keep, give = call(
        local_states_kernel,
        [half, half],
        [VMEM] * 5 + [SMEM],
        [
            pltpu.VMEM((LANES, tokens), F32),
            pltpu.VMEM((tokens, WIDE), BF16),
            pltpu.VMEM((tokens, WIDE), BF16),
            pltpu.VMEM((tokens, WIDE), BF16),
            pltpu.VMEM((4, NS, WIDE), F32),
        ],
        4,
        "local_states",
    )(x, g, b, c, steps, rate_log)
    received = swapped(give)
    messages = call(
        lambda *refs: combine_kernel(chips, *refs),
        [((HALF, WIDE + LANES), BF16)] * (chips - 1),
        [VMEM] * 2,
        [],
        1,
        "combine_states",
    )(keep, received)
    arrived = [from_chip(messages[k - 1], k) for k in range(1, chips)]

    inner_y, inner_dx, inner_db, inner_dc, sums = call(
        inner_kernel,
        [((tokens, WIDE), F32)] * 2 + [((tokens, NS), F32)] * 2 + [((2 * HS, LANES), F32)],
        [VMEM] * 5 + [SMEM] * 2 + [AFTER],
        [
            pltpu.VMEM((LANES, tokens), F32),
            pltpu.VMEM((tokens, tokens), F32),
            pltpu.VMEM((tokens, tokens), F32),
            pltpu.VMEM((tokens, tokens), BF16),
            pltpu.VMEM((LANES, 2 * tokens), F32),
        ],
        5,
        "chunk_inner",
    )(x, g, b, c, steps, rate_log, skip, messages[0])

    entering = ((2, HALF, WIDE), BF16)
    own, give, totals = call(
        lambda *refs: chain_kernel(chips, *refs),
        [entering, entering, ((2 * HS, LANES), F32)],
        [VMEM] * (2 + chips),
        [],
        2,
        "chain_states",
    )(keep, received, sums, *arrived)
    other = swapped(give)
    replicas = lax.axis_size("dp")
    summed = totals + sum(turned(totals, k) for k in range(1, replicas))

    columns = QUERY_HEADS * BLOCK
    split = ((chips, 2 * LANES, tokens), BF16)
    attention, dq, keep, give = call(
        lambda *refs: attention_kernel(chips, most, *refs),
        [((tokens, columns), F32), ((tokens, columns), BF16), split, split],
        [SMEM] + [VMEM] * (2 + n) + [AFTER],
        [
            pltpu.VMEM((every, 2 * LANES), BF16),
            pltpu.VMEM((2 * LANES, every), F32),
            pltpu.VMEM((most * BLOCK, LANES), BF16),
            pltpu.VMEM((most * BLOCK, LANES), BF16),
            pltpu.VMEM((most * BLOCK, 2 * LANES), BF16),
            pltpu.VMEM((LANES, columns), BF16),
            pltpu.VMEM((LANES, columns), BF16),
            pltpu.VMEM((columns, most * BLOCK), BF16),
            pltpu.VMEM((columns, most * BLOCK), BF16),
        ],
        10,
        "attention",
    )(block_mask[0], q, g, *kv_parts, totals)
    partial, summed, *messages = call(
        lambda *refs: pair_sum_kernel(chips, *refs),
        [((2 * LANES, tokens), F32), ((2 * HS, LANES), F32)]
        + [((2 * LANES + 32, tokens), BF16)] * (chips - 1),
        [VMEM] * 4,
        [],
        1,
        "pair_sum",
    )(keep, swapped(give), summed, swapped(summed))
    arrived = [from_chip(messages[k - 1], k) for k in range(1, chips)]

    y, dx, db, dc = call(
        outer_kernel,
        [((tokens, WIDE), BF16)] * 2 + [((tokens, NS), BF16)] * 2,
        [VMEM] * 5 + [SMEM] + [VMEM] * 7 + [AFTER],
        [
            pltpu.VMEM((LANES, tokens), F32),
            pltpu.VMEM((tokens, WIDE), BF16),
            pltpu.VMEM((tokens, WIDE), BF16),
            pltpu.VMEM((2, NS, WIDE), BF16),
        ],
        3,
        "chunk_outer",
    )(
        x, g, b, c, steps, rate_log, own, other, attention,
        inner_y, inner_dx, inner_db, inner_dc, messages[0],
    )

    tokens_all = replicas * n * tokens
    dk, dv, grad_rate_log, grad_skip = call(
        lambda *refs: owner_sum_kernel(chips, tokens_all, *refs),
        [((tokens, LANES), BF16)] * 2 + [((1, HS), F32)] * 2,
        [VMEM] * (chips + 1),
        [],
        1,
        "owner_sum",
    )(partial, summed, *arrived)
    return (
        y[None],
        dq[None],
        dk[None],
        dv[None],
        dx[None],
        db[None],
        dc[None],
        grad_rate_log.reshape(HS),
        grad_skip.reshape(HS),
    )


def solution(mesh):
    split = P("dp", "seq", None)
    in_specs = (split,) * 7 + (P(), P(), P("dp", None, None), split)
    out_specs = (split,) * 7 + (P(), P())
    return jax.shard_map(body, mesh=mesh, in_specs=in_specs, out_specs=out_specs, check_vma=False)
```

```python
import jax
import jax.numpy as jnp
from jax import lax
from jax.experimental import pallas as pl
from jax.experimental.pallas import tpu as pltpu
from jax.sharding import PartitionSpec as P

HEAD_WIDTH = 128
QUERY_HEADS = 8
HS = 8
P_SIZE = 128
NS = 128
BLOCK = 128
WIDE = HS * P_SIZE
LANES = 128
FACTOR = HEAD_WIDTH ** (-0.5)
LOG2E = 1.4426950408889634
NEG = -1e30
HALF = NS // 2
HIGH = lax.Precision.HIGHEST
F32 = jnp.float32
BF16 = jnp.bfloat16

VMEM = pl.BlockSpec(memory_space=pltpu.VMEM)
SMEM = pl.BlockSpec(memory_space=pltpu.SMEM)
AFTER = pl.BlockSpec(memory_space=pl.ANY)


def cost(microseconds):
    return pl.CostEstimate(
        flops=int(microseconds * 1.1e9), bytes_accessed=1 << 20, transcendentals=0
    )


def dot(a, b, ca, cb, precision=None):
    return lax.dot_general(
        a, b, (((ca,), (cb,)), ((), ())), preferred_element_type=F32, precision=precision
    )


def head(h):
    return slice(h * LANES, (h + 1) * LANES)


def running_logs(step_ref, rate_ref, pad_ref):
    pad_ref[...] = jnp.zeros_like(pad_ref)
    for h in range(HS):
        rate = jnp.exp(jnp.full((1, 2 * BLOCK), rate_ref[h], F32))
        pad_ref[h : h + 1, :] = -step_ref[h : h + 1, :] * rate
    row = lax.broadcasted_iota(jnp.int32, (BLOCK, BLOCK), 0)
    col = lax.broadcasted_iota(jnp.int32, (BLOCK, BLOCK), 1)
    upper = jnp.where(row <= col, 1.0, 0.0).astype(F32)
    flat0 = dot(pad_ref[:, :BLOCK], upper, 1, 0, HIGH)
    flat1 = dot(pad_ref[:, BLOCK:], upper, 1, 0, HIGH)
    return flat0, flat1, flat0.T, flat1.T


def scaled(x_ref, column, out_ref):
    for h in range(HS):
        out_ref[:, head(h)] = (x_ref[:, head(h)].astype(F32) * column[:, h : h + 1]).astype(BF16)


def chip_and_core():
    me = lax.axis_index("seq")
    return me // 2, me % 2


def enter_and_tail(run0, run1):
    t0, t1 = run0[BLOCK - 1 :, :], run1[BLOCK - 1 :, :]
    enter = jnp.concatenate([run0, run1 + t0], axis=0)
    tail = jnp.concatenate([(t0 - run0) + t1, t1 - run1], axis=0)
    return enter, tail, t0 + t1


def local_states_kernel(
    x_ref, g_ref, b_ref, c_ref, step_ref, rate_ref, key_ref, value_ref, keep_ref, give_ref, kv_ref,
    pad_ref, high_ref, rest_ref, log_ref, state_ref,
):
    _, core = chip_and_core()
    kv_ref[:, :LANES] = key_ref[...]
    kv_ref[:, LANES:] = value_ref[...]
    _, _, run0, run1 = running_logs(step_ref, rate_ref, pad_ref)
    enter_log, tail_log, total = enter_and_tail(run0, run1)
    enter, tail = jnp.exp(enter_log), jnp.exp(tail_log)
    logs = jnp.broadcast_to(total, (HALF, LANES))
    mine = pl.ds(pl.multiple_of(core * HALF, HALF), HALF)
    other = pl.ds(pl.multiple_of((1 - core) * HALF, HALF), HALF)
    cases = ((b_ref, x_ref, tail, tail_log), (c_ref, g_ref, enter, enter_log))
    for direction, (left, right, factor, weight) in enumerate(cases):
        for h in range(HS):
            product = right[:, head(h)].astype(F32) * factor[:, h : h + 1]
            rounded = product.astype(BF16)
            high_ref[:, head(h)] = rounded
            rest_ref[:, head(h)] = (product - rounded.astype(F32)).astype(BF16)
            log_ref[:, head(h)] = (product * weight[:, h : h + 1]).astype(BF16)
        turned_left = left[...].astype(F32).T.astype(BF16)
        state_ref[direction] = dot(turned_left, high_ref[...], 1, 0) + dot(
            turned_left, rest_ref[...], 1, 0
        )
        state_ref[3 - direction] = dot(turned_left, log_ref[...], 1, 0)
    for kind in range(4):
        keep_ref[kind, :, :WIDE] = state_ref[kind, mine, :]
        keep_ref[kind, :, WIDE:] = logs
        give_ref[kind, :, :WIDE] = state_ref[kind, other, :]
        give_ref[kind, :, WIDE:] = logs


def three_parts(value, rows):
    high = value.astype(BF16).astype(F32)
    middle = (value - high).astype(BF16).astype(F32)
    low = value - high - middle
    index = lax.broadcasted_iota(jnp.int32, (rows, LANES), 0)
    return jnp.where(index == 0, high, jnp.where(index == 1, middle, low)).astype(BF16)


def pair_logs(keep_ref, recv_ref, is0):
    mine, other = keep_ref[0, 0:1, WIDE:], recv_ref[0, 0:1, WIDE:]
    return jnp.where(is0, mine, other), jnp.where(is0, other, mine)


def combine_kernel(chips, keep_ref, recv_ref, *message_refs):
    chip, core = chip_and_core()
    is0 = core == 0
    log0, log1 = pair_logs(keep_ref, recv_ref, is0)
    logs = three_parts(log0 + log1, HALF)
    decay0, decay1 = jnp.exp(log0), jnp.exp(log1)
    for h in range(HS):
        mine, other = keep_ref[0, :, head(h)], recv_ref[0, :, head(h)]
        first, second = jnp.where(is0, mine, other), jnp.where(is0, other, mine)
        state = (first * decay1[:, h : h + 1] + second).astype(BF16)
        mine, other = keep_ref[1, :, head(h)], recv_ref[1, :, head(h)]
        first, second = jnp.where(is0, mine, other), jnp.where(is0, other, mine)
        grad = (second * decay0[:, h : h + 1] + first).astype(BF16)
        for k in range(1, chips):
            later = chip + k < chips
            message_refs[k - 1][:, head(h)] = jnp.where(later, state, grad)
    for k in range(1, chips):
        message_refs[k - 1][:, WIDE:] = logs


def chain_kernel(chips, keep_ref, recv_ref, sums_ref, *refs):
    message_refs = refs[: chips - 1]
    own_ref, give_ref, total_ref = refs[chips - 1 :]
    chip, core = chip_and_core()
    is0 = core == 0
    log0, log1 = pair_logs(keep_ref, recv_ref, is0)
    decay0, decay1 = jnp.exp(log0), jnp.exp(log1)
    weight0, weight1 = log0 * decay0, log1 * decay1
    factors = [None]
    for ref in message_refs:
        parts = ref[:16, WIDE:].astype(F32)
        factors.append(jnp.exp(parts[0:1, :] + parts[1:2, :] + parts[2:3, :]))
    total_ref[...] = sums_ref[...]
    for h in range(HS):
        column = slice(h, h + 1)
        states = [(keep_ref[kind, :, head(h)], recv_ref[kind, :, head(h)]) for kind in range(4)]
        (s0, s1), (g0, g1), (qs0, qs1), (qg0, qg1) = [
            (jnp.where(is0, mine, other), jnp.where(is0, other, mine)) for mine, other in states
        ]
        state = jnp.zeros((HALF, LANES), F32)
        for k in range(chips - 1, 0, -1):
            new = state * factors[k][:, column] + message_refs[k - 1][:, head(h)].astype(F32)
            state = jnp.where(k <= chip, new, state)
        grad = jnp.zeros((HALF, LANES), F32)
        for k in range(1, chips):
            new = grad * factors[k][:, column] + message_refs[k - 1][:, head(h)].astype(F32)
            grad = jnp.where(k > chip, new, grad)
        h0, l1 = state, grad
        h1 = h0 * decay0[:, column] + s0
        l0 = l1 * decay1[:, column] + g1
        cross = h0 * (l0 * weight0[:, column] + qs0) + h1 * (l1 * weight1[:, column] + qs1)
        cross += l0 * qg0 + l1 * qg1
        total_ref[h : h + 1, :] += jnp.sum(cross, axis=0, keepdims=True)
        h0, h1, l0, l1 = (value.astype(BF16) for value in (h0, h1, l0, l1))
        own_ref[0, :, head(h)] = jnp.where(is0, h0, h1)
        own_ref[1, :, head(h)] = jnp.where(is0, l0, l1)
        give_ref[0, :, head(h)] = jnp.where(is0, h1, h0)
        give_ref[1, :, head(h)] = jnp.where(is0, l1, l0)


def attention_kernel(
    chips, most, mask_ref, q_ref, g_ref, stack_ref, other_stack_ref, _, totals_ref, *refs
):
    extra = len(refs) - 15
    (
        out_ref, dq_ref, keep_ref, give_ref, sums_ref,
        slot_ref, kv_ref, acc_ref, k_ref, k_live_ref, v_ref, q_turned_ref, g_turned_ref, ds_ref, wb_ref,
    ) = refs[extra:]
    count = mask_ref.shape[0]
    columns = QUERY_HEADS * BLOCK
    tokens = q_ref.shape[0]
    chip, core = chip_and_core()
    me = 2 * chip + core
    scale = FACTOR * LOG2E
    sums = totals_ref[...]
    for ref in refs[:extra]:
        sums += ref[...]
    sums_ref[...] = sums
    high = sums.astype(BF16)
    middle = (sums - high.astype(F32)).astype(BF16)
    low = (sums - high.astype(F32) - middle.astype(F32)).astype(BF16)
    give_ref[chips * tokens : chips * tokens + 16, :] = jnp.concatenate([high, middle], axis=1)
    give_ref[chips * tokens + 16 :, :] = jnp.concatenate([low, jnp.zeros_like(low)], axis=1)
    acc_ref[...] = jnp.zeros_like(acc_ref)
    for k in range(chips):
        for other, ref in enumerate((stack_ref, other_stack_ref)):
            source = 2 * lax.rem(chip + chips - k, chips) + lax.rem(core + other, 2)
            at = pl.ds(pl.multiple_of(source * tokens, tokens), tokens)
            kv_ref[at, :] = ref[k]

    lower, upper = slice(0, LANES), slice(LANES, 2 * LANES)
    for block in range(tokens // BLOCK):
        at = slice(block * BLOCK, (block + 1) * BLOCK)
        row = me * (tokens // BLOCK) + block
        slots = []
        for slot in range(most):
            slot_ref[block, slot] = row

        def note(j, seen):
            hit = mask_ref[row, j]

            @pl.when(hit == 1)
            def _():
                slot_ref[block, seen] = j

            return seen + hit

        allowed = lax.fori_loop(0, count, note, 0)
        for slot in range(most):
            index, live = slot_ref[block, slot], slot < allowed
            slots.append((index, live))
            source = pl.ds(pl.multiple_of(index * BLOCK, BLOCK), BLOCK)
            target = slice(slot * BLOCK, (slot + 1) * BLOCK)
            k_tile, v_tile = kv_ref[source, lower], kv_ref[source, upper]
            k_ref[target, :] = k_tile
            k_live_ref[target, :] = jnp.where(live, k_tile, jnp.zeros_like(k_tile))
            v_ref[target, lower] = jnp.where(live, v_tile, jnp.zeros_like(v_tile))
            v_ref[target, upper] = jnp.full((BLOCK, LANES), jnp.where(live, 1.0, 0.0), F32).astype(BF16)
        group = 2
        for first in range(0, QUERY_HEADS, group):
            heads = range(first, first + group)
            rows = slice(first * BLOCK, (first + group) * BLOCK)
            q = jnp.concatenate([q_ref[at, head(h)] for h in heads], axis=0)
            g = jnp.concatenate([g_ref[at, head(h)] for h in heads], axis=0)
            scores = dot(q, k_ref[...], 1, 1)
            best = jnp.max(scores, axis=1, keepdims=True)
            weights = jnp.exp2((scores - best) * scale)
            wb_ref[rows, :] = weights.astype(BF16)
            both = dot(wb_ref[rows, :], v_ref[...], 1, 0)
            inverse = 1.0 / both[:, upper]
            out = both[:, lower] * inverse
            delta = jnp.sum(out * g.astype(F32), axis=1, keepdims=True)
            dprobs = dot(g, v_ref[:, lower], 1, 1)
            ds_ref[rows, :] = (weights * (dprobs - delta)).astype(BF16)
            dq = (dot(ds_ref[rows, :], k_live_ref[...], 1, 0) * (inverse * FACTOR)).astype(BF16)
            q_turned_ref[:, rows] = (q.astype(F32) * inverse).astype(BF16).T
            g_turned_ref[:, rows] = (g.astype(F32) * inverse).astype(BF16).T
            for place, h in enumerate(heads):
                part = slice(place * BLOCK, (place + 1) * BLOCK)
                out_ref[at, head(h)] = out[part]
                dq_ref[at, head(h)] = dq[part]
        dk = dot(q_turned_ref[...], ds_ref[...], 1, 0)
        dv = dot(g_turned_ref[...], wb_ref[...], 1, 0)
        for slot, (index, live) in enumerate(slots):
            source = slice(slot * BLOCK, (slot + 1) * BLOCK)

            @pl.when(live)
            def _():
                target = pl.ds(pl.multiple_of(index * BLOCK, BLOCK), BLOCK)
                acc_ref[lower, target] += dk[:, source]
                acc_ref[upper, target] += dv[:, source]

    for k in range(chips):
        mine = pl.multiple_of((2 * k + core) * tokens, tokens)
        other = pl.multiple_of((2 * k + 1 - core) * tokens, tokens)
        rows = slice(k * tokens, (k + 1) * tokens)
        keep_ref[rows, :] = acc_ref[:, pl.ds(mine, tokens)].astype(BF16)
        give_ref[rows, :] = acc_ref[:, pl.ds(other, tokens)].astype(BF16)


def pair_sum_kernel(chips, keep_ref, recv_ref, sums_ref, own_ref, total_ref, *message_refs):
    chip, _ = chip_and_core()
    rows = own_ref.shape[0]
    at = pl.ds(pl.multiple_of(chip * rows, rows), rows)
    own_ref[...] = keep_ref[at, :].astype(F32) + recv_ref[at, :].astype(F32)
    total = sums_ref[...] + whole_sums(recv_ref[chips * rows :, :])
    total_ref[...] = total
    high = total.astype(BF16)
    middle = (total - high.astype(F32)).astype(BF16)
    low = (total - high.astype(F32) - middle.astype(F32)).astype(BF16)
    for k in range(1, chips):
        target = pl.ds(pl.multiple_of(lax.rem(chip + k, chips) * rows, rows), rows)
        both = keep_ref[target, :].astype(F32) + recv_ref[target, :].astype(F32)
        message_refs[k - 1][:rows, :] = both.astype(BF16)
        message_refs[k - 1][rows : rows + 16, :] = jnp.concatenate([high, middle], axis=1)
        message_refs[k - 1][rows + 16 :, :] = jnp.concatenate([low, jnp.zeros_like(low)], axis=1)


def whole_sums(tail):
    tail = tail.astype(F32)
    return tail[:16, :LANES] + tail[:16, LANES:] + tail[16:, :LANES]


def owner_sum_kernel(chips, tokens_all, own_ref, sums_ref, *refs):
    parts, (dk_ref, dv_ref, rate_ref, skip_ref) = refs[: chips - 1], refs[chips - 1 :]
    rows = own_ref.shape[0]
    total = own_ref[...]
    sums = sums_ref[...]
    for part in parts:
        total += part[:rows, :].astype(F32)
        sums += whole_sums(part[rows:, :])
    dk_ref[...] = (total[:LANES].T * FACTOR).astype(BF16)
    dv_ref[...] = total[LANES:].T.astype(BF16)
    ones = jnp.ones((8, LANES), F32)
    rate = dot(ones, sums[:HS], 1, 1, HIGH) * (1.0 / tokens_all)
    skip = dot(ones, sums[HS:], 1, 1, HIGH) * (1.0 / (tokens_all * P_SIZE))
    rate_ref[...] = rate[0:1, :]
    skip_ref[...] = skip[0:1, :]


def inner_kernel(chips, x_ref, g_ref, b_ref, c_ref, step_ref, rate_ref, skip_ref, _, *refs):
    (
        stack_ref, y_ref, dx_ref, db_ref, dc_ref, sums_ref,
        pad_ref, inner_ref, dinner_ref, m_ref, runt_ref,
    ) = refs[chips:]
    for k in range(chips):
        stack_ref[k] = refs[k][...]
    tokens = 2 * BLOCK
    flat0, flat1, run0, run1 = running_logs(step_ref, rate_ref, pad_ref)
    own = jnp.concatenate([run0, run1], axis=0)
    runt_ref[:, :BLOCK] = flat0
    runt_ref[:, tokens : tokens + BLOCK] = flat0 - flat0[:, BLOCK - 1 :]
    runt_ref[:, tokens + BLOCK :] = flat1
    b = b_ref[...]
    c = c_ref[...]
    inner_ref[...] = dot(c, b, 1, 1)
    dinner_ref[...] = jnp.zeros_like(dinner_ref)
    row0 = lax.broadcasted_iota(jnp.int32, (BLOCK, BLOCK), 0)
    col0 = lax.broadcasted_iota(jnp.int32, (BLOCK, BLOCK), 1)
    row1 = lax.broadcasted_iota(jnp.int32, (BLOCK, tokens), 0)
    col1 = lax.broadcasted_iota(jnp.int32, (BLOCK, tokens), 1)
    seen0 = row0 >= col0
    seen1 = row1 + BLOCK >= col1
    m_ref[:BLOCK, BLOCK:] = jnp.zeros((BLOCK, BLOCK), BF16)
    for h in range(HS):
        lanes = head(h)
        x = x_ref[:, lanes]
        g = g_ref[:, lanes]
        xf, gf = x.astype(F32), g.astype(F32)
        gain = skip_ref[h]
        spread0 = jnp.where(seen0, own[:BLOCK, h : h + 1] - runt_ref[h : h + 1, :BLOCK], NEG)
        spread1 = jnp.where(seen1, own[BLOCK:, h : h + 1] - runt_ref[h : h + 1, tokens:], NEG)
        decay0, decay1 = jnp.exp(spread0), jnp.exp(spread1)
        dm = dot(g, x, 1, 1)
        e0, e1 = decay0 * dm[:BLOCK, :BLOCK], decay1 * dm[BLOCK:, :]
        m_ref[:BLOCK, :BLOCK] = (decay0 * inner_ref[:BLOCK, :BLOCK]).astype(BF16)
        m_ref[BLOCK:, :] = (decay1 * inner_ref[BLOCK:, :]).astype(BF16)
        dinner_ref[:BLOCK, :BLOCK] += e0
        dinner_ref[BLOCK:, :] += e1
        w0 = jnp.sum(spread0 * (e0 * inner_ref[:BLOCK, :BLOCK]), axis=0, keepdims=True)
        w1 = jnp.sum(spread1 * (e1 * inner_ref[BLOCK:, :]), axis=0, keepdims=True)
        m = m_ref[...]
        y_ref[:, lanes] = dot(m, x, 1, 0) + gain * xf
        dx_ref[:, lanes] = dot(m, g, 0, 0) + gain * gf
        sums_ref[h : h + 1, :] = w0 + w1[:, :BLOCK] + w1[:, BLOCK:]
        sums_ref[HS + h : HS + h + 1, :] = jnp.sum(gf * xf, axis=0, keepdims=True)
    dinner = dinner_ref[...].astype(BF16)
    dc_ref[...] = dot(dinner, b, 1, 0)
    db_ref[...] = dot(dinner, c, 0, 0)


def outer_kernel(
    x_ref, g_ref, b_ref, c_ref, step_ref, rate_ref, own_ref, other_ref, att_ref,
    inner_y_ref, inner_dx_ref, inner_db_ref, inner_dc_ref, _,
    y_ref, dx_ref, db_ref, dc_ref,
    pad_ref, xt_ref, gt_ref, ent_ref,
):
    _, core = chip_and_core()
    ent_ref[:, pl.ds(pl.multiple_of(core * HALF, HALF), HALF), :] = own_ref[...]
    ent_ref[:, pl.ds(pl.multiple_of((1 - core) * HALF, HALF), HALF), :] = other_ref[...]
    _, _, run0, run1 = running_logs(step_ref, rate_ref, pad_ref)
    enter_log, tail_log, _ = enter_and_tail(run0, run1)
    enter, tail = jnp.exp(enter_log), jnp.exp(tail_log)
    scaled(x_ref, tail, xt_ref)
    scaled(g_ref, enter, gt_ref)
    b = b_ref[...]
    c = c_ref[...]
    for h in range(HS):
        lanes = head(h)
        carried = dot(c, ent_ref[0, :, lanes], 1, 0) * enter[:, h : h + 1]
        back = dot(b, ent_ref[1, :, lanes], 1, 0) * tail[:, h : h + 1]
        y_ref[:, lanes] = (inner_y_ref[:, lanes] + carried + att_ref[:, lanes]).astype(BF16)
        dx_ref[:, lanes] = (inner_dx_ref[:, lanes] + back).astype(BF16)
    dc_ref[...] = (inner_dc_ref[...] + dot(gt_ref[...], ent_ref[0], 1, 1)).astype(BF16)
    db_ref[...] = (inner_db_ref[...] + dot(xt_ref[...], ent_ref[1], 1, 1)).astype(BF16)


def swapped(array):
    return lax.ppermute(array, "seq", [(i, i ^ 1) for i in range(lax.axis_size("seq"))])


def from_chip(array, k):
    n = lax.axis_size("seq")
    return lax.ppermute(array, "seq", [(i, (i + 2 * k) % n) for i in range(n)])


def turned(array, k):
    n = lax.axis_size("dp")
    return lax.ppermute(array, "dp", [(i, (i + k) % n) for i in range(n)])


def call(kernel, outs, ins, scratch, microseconds, name, limit=16):
    return pl.pallas_call(
        kernel,
        out_shape=tuple(jax.ShapeDtypeStruct(*out) for out in outs),
        in_specs=ins,
        out_specs=(VMEM,) * len(outs),
        scratch_shapes=scratch,
        compiler_params=pltpu.CompilerParams(vmem_limit_bytes=limit << 20),
        cost_estimate=cost(microseconds),
        name=name,
    )


def body(query, key, value, ssm_input, in_b, in_c, step, rate_log, skip, block_mask, grad_out):
    n = lax.axis_size("seq")
    chips = n // 2
    replicas = lax.axis_size("dp")
    tokens = query.shape[1]
    blocks = block_mask.shape[1]
    most = 3 * blocks // 8
    every = blocks * BLOCK
    q, g, x = query[0], grad_out[0], ssm_input[0]
    b, c, steps = in_b[0], in_c[0], step[0].T

    half = ((4, HALF, WIDE + LANES), F32)
    keep, give, kv = call(
        local_states_kernel,
        [half, half, ((tokens, 2 * LANES), BF16)],
        [VMEM] * 5 + [SMEM] + [VMEM] * 2,
        [
            pltpu.VMEM((LANES, tokens), F32),
            pltpu.VMEM((tokens, WIDE), BF16),
            pltpu.VMEM((tokens, WIDE), BF16),
            pltpu.VMEM((tokens, WIDE), BF16),
            pltpu.VMEM((4, NS, WIDE), F32),
        ],
        4,
        "local_states",
    )(x, g, b, c, steps, rate_log, key[0], value[0])
    received = swapped(give)
    kv_parts = [kv] + [from_chip(kv, k) for k in range(1, chips)]
    messages = call(
        lambda *refs: combine_kernel(chips, *refs),
        [((HALF, WIDE + LANES), BF16)] * (chips - 1),
        [VMEM] * 2,
        [],
        1,
        "combine_states",
    )(keep, received)
    arrived = [from_chip(messages[k - 1], k) for k in range(1, chips)]

    stack, inner_y, inner_dx, inner_db, inner_dc, sums = call(
        lambda *refs: inner_kernel(chips, *refs),
        [((chips, tokens, 2 * LANES), BF16)]
        + [((tokens, WIDE), F32)] * 2
        + [((tokens, NS), F32)] * 2
        + [((2 * HS, LANES), F32)],
        [VMEM] * 5 + [SMEM] * 2 + [AFTER] + [VMEM] * chips,
        [
            pltpu.VMEM((LANES, tokens), F32),
            pltpu.VMEM((tokens, tokens), F32),
            pltpu.VMEM((tokens, tokens), F32),
            pltpu.VMEM((tokens, tokens), BF16),
            pltpu.VMEM((LANES, 2 * tokens), F32),
        ],
        5,
        "chunk_inner",
    )(x, g, b, c, steps, rate_log, skip, messages[0], *kv_parts)
    other_stack = swapped(stack)

    entering = ((2, HALF, WIDE), BF16)
    own, give, totals = call(
        lambda *refs: chain_kernel(chips, *refs),
        [entering, entering, ((2 * HS, LANES), F32)],
        [VMEM] * (2 + chips),
        [],
        2,
        "chain_states",
    )(keep, received, sums, *arrived)
    other = swapped(give)
    replicated = [turned(totals, k) for k in range(1, replicas)]

    columns = QUERY_HEADS * BLOCK
    attention, dq, keep, give, sums = call(
        lambda *refs: attention_kernel(chips, most, *refs),
        [
            ((tokens, columns), F32),
            ((tokens, columns), BF16),
            ((chips * 2 * LANES, tokens), BF16),
            ((chips * 2 * LANES + 32, tokens), BF16),
            ((2 * HS, LANES), F32),
        ],
        [SMEM] + [VMEM] * 4 + [AFTER] + [VMEM] * replicas,
        [
            pltpu.SMEM((2, most), jnp.int32),
            pltpu.VMEM((every, 2 * LANES), BF16),
            pltpu.VMEM((2 * LANES, every), F32),
            pltpu.VMEM((most * BLOCK, LANES), BF16),
            pltpu.VMEM((most * BLOCK, LANES), BF16),
            pltpu.VMEM((most * BLOCK, 2 * LANES), BF16),
            pltpu.VMEM((LANES, columns), BF16),
            pltpu.VMEM((LANES, columns), BF16),
            pltpu.VMEM((columns, most * BLOCK), BF16),
            pltpu.VMEM((columns, most * BLOCK), BF16),
        ],
        10,
        "attention",
        18 + most,
    )(block_mask[0], q, g, stack, other_stack, other, totals, *replicated)
    partial, summed, *messages = call(
        lambda *refs: pair_sum_kernel(chips, *refs),
        [((2 * LANES, tokens), F32), ((2 * HS, LANES), F32)]
        + [((2 * LANES + 32, tokens), BF16)] * (chips - 1),
        [VMEM] * 3,
        [],
        1,
        "pair_sum",
    )(keep, swapped(give), sums)
    arrived = [from_chip(messages[k - 1], k) for k in range(1, chips)]

    y, dx, db, dc = call(
        outer_kernel,
        [((tokens, WIDE), BF16)] * 2 + [((tokens, NS), BF16)] * 2,
        [VMEM] * 5 + [SMEM] + [VMEM] * 7 + [AFTER],
        [
            pltpu.VMEM((LANES, tokens), F32),
            pltpu.VMEM((tokens, WIDE), BF16),
            pltpu.VMEM((tokens, WIDE), BF16),
            pltpu.VMEM((2, NS, WIDE), BF16),
        ],
        3,
        "chunk_outer",
    )(
        x, g, b, c, steps, rate_log, own, other, attention,
        inner_y, inner_dx, inner_db, inner_dc, messages[0],
    )

    tokens_all = replicas * n * tokens
    dk, dv, grad_rate_log, grad_skip = call(
        lambda *refs: owner_sum_kernel(chips, tokens_all, *refs),
        [((tokens, LANES), BF16)] * 2 + [((1, HS), F32)] * 2,
        [VMEM] * (chips + 1),
        [],
        1,
        "owner_sum",
    )(partial, summed, *arrived)
    return (
        y[None],
        dq[None],
        dk[None],
        dv[None],
        dx[None],
        db[None],
        dc[None],
        grad_rate_log.reshape(HS),
        grad_skip.reshape(HS),
    )


def solution(mesh):
    split = P("dp", "seq", None)
    in_specs = (split,) * 7 + (P(), P(), P("dp", None, None), split)
    out_specs = (split,) * 7 + (P(), P())
    return jax.shard_map(body, mesh=mesh, in_specs=in_specs, out_specs=out_specs, check_vma=False)
```

```python
import jax
import jax.numpy as jnp
from jax import lax
from jax.experimental import pallas as pl
from jax.experimental.pallas import tpu as pltpu
from jax.sharding import PartitionSpec as P

HEAD_WIDTH = 128
QUERY_HEADS = 8
HS = 8
P_SIZE = 128
NS = 128
BLOCK = 128
WIDE = HS * P_SIZE
LANES = 128
FACTOR = HEAD_WIDTH ** (-0.5)
LOG2E = 1.4426950408889634
NEG = -1e30
HALF = NS // 2
HIGH = lax.Precision.HIGHEST
F32 = jnp.float32
BF16 = jnp.bfloat16

VMEM = pl.BlockSpec(memory_space=pltpu.VMEM)
SMEM = pl.BlockSpec(memory_space=pltpu.SMEM)
AFTER = pl.BlockSpec(memory_space=pl.ANY)


def cost(microseconds):
    return pl.CostEstimate(
        flops=int(microseconds * 1.1e9), bytes_accessed=1 << 20, transcendentals=0
    )


def dot(a, b, ca, cb, precision=None):
    return lax.dot_general(
        a, b, (((ca,), (cb,)), ((), ())), preferred_element_type=F32, precision=precision
    )


def head(h):
    return slice(h * LANES, (h + 1) * LANES)


def running_logs(step_ref, rate_ref, pad_ref):
    pad_ref[...] = jnp.zeros_like(pad_ref)
    for h in range(HS):
        rate = jnp.exp(jnp.full((1, 2 * BLOCK), rate_ref[h], F32))
        pad_ref[h : h + 1, :] = -step_ref[h : h + 1, :] * rate
    row = lax.broadcasted_iota(jnp.int32, (BLOCK, BLOCK), 0)
    col = lax.broadcasted_iota(jnp.int32, (BLOCK, BLOCK), 1)
    upper = jnp.where(row <= col, 1.0, 0.0).astype(F32)
    flat0 = dot(pad_ref[:, :BLOCK], upper, 1, 0, HIGH)
    flat1 = dot(pad_ref[:, BLOCK:], upper, 1, 0, HIGH)
    return flat0, flat1, flat0.T, flat1.T


def scaled(x_ref, column, out_ref):
    for h in range(HS):
        out_ref[:, head(h)] = (x_ref[:, head(h)].astype(F32) * column[:, h : h + 1]).astype(BF16)


def chip_and_core():
    me = lax.axis_index("seq")
    return me // 2, me % 2


def fetch(pairs, sems):
    copies = [
        pltpu.make_async_copy(source, target, sems.at[i]) for i, (source, target) in enumerate(pairs)
    ]
    for copy in copies:
        copy.start()
    return copies


def pack_kernel(key_ref, value_ref, out_ref, sems):
    pairs = [(key_ref, out_ref.at[:, :LANES]), (value_ref, out_ref.at[:, LANES:])]
    for copy in fetch(pairs, sems):
        copy.wait()


def stack_kernel(*refs):
    for k, ref in enumerate(refs[:-1]):
        refs[-1][k] = ref[...]


def enter_and_tail(run0, run1):
    t0, t1 = run0[BLOCK - 1 :, :], run1[BLOCK - 1 :, :]
    enter = jnp.concatenate([run0, run1 + t0], axis=0)
    tail = jnp.concatenate([(t0 - run0) + t1, t1 - run1], axis=0)
    return enter, tail, t0 + t1


def local_states_kernel(
    x_hbm, g_hbm, b_hbm, c_hbm, step_hbm, rate_ref, _, keep_ref, give_ref,
    x_ref, g_ref, b_ref, c_ref, step_ref, sems, pad_ref, high_ref, rest_ref, log_ref, state_ref,
):
    _, core = chip_and_core()
    step_copy, b_copy, x_copy, c_copy, g_copy = fetch(
        [(step_hbm, step_ref), (b_hbm, b_ref), (x_hbm, x_ref), (c_hbm, c_ref), (g_hbm, g_ref)], sems
    )
    step_copy.wait()
    _, _, run0, run1 = running_logs(step_ref, rate_ref, pad_ref)
    enter_log, tail_log, total = enter_and_tail(run0, run1)
    enter, tail = jnp.exp(enter_log), jnp.exp(tail_log)
    logs = jnp.broadcast_to(total, (HALF, LANES))
    mine = pl.ds(pl.multiple_of(core * HALF, HALF), HALF)
    other = pl.ds(pl.multiple_of((1 - core) * HALF, HALF), HALF)
    cases = (
        (b_ref, x_ref, tail, tail_log, (b_copy, x_copy)),
        (c_ref, g_ref, enter, enter_log, (c_copy, g_copy)),
    )
    for direction, (left, right, factor, weight, copies) in enumerate(cases):
        for copy in copies:
            copy.wait()
        for h in range(HS):
            product = right[:, head(h)].astype(F32) * factor[:, h : h + 1]
            rounded = product.astype(BF16)
            high_ref[:, head(h)] = rounded
            rest_ref[:, head(h)] = (product - rounded.astype(F32)).astype(BF16)
            log_ref[:, head(h)] = (product * weight[:, h : h + 1]).astype(BF16)
        turned_left = left[...].astype(F32).T.astype(BF16)
        state_ref[direction] = dot(turned_left, high_ref[...], 1, 0) + dot(
            turned_left, rest_ref[...], 1, 0
        )
        state_ref[3 - direction] = dot(turned_left, log_ref[...], 1, 0)
    for kind in range(4):
        keep_ref[kind, :, :WIDE] = state_ref[kind, mine, :]
        keep_ref[kind, :, WIDE:] = logs
        give_ref[kind, :, :WIDE] = state_ref[kind, other, :]
        give_ref[kind, :, WIDE:] = logs


def three_parts(value, rows):
    high = value.astype(BF16).astype(F32)
    middle = (value - high).astype(BF16).astype(F32)
    low = value - high - middle
    index = lax.broadcasted_iota(jnp.int32, (rows, LANES), 0)
    return jnp.where(index == 0, high, jnp.where(index == 1, middle, low)).astype(BF16)


def pair_logs(keep_ref, recv_ref, is0):
    mine, other = keep_ref[0, 0:1, WIDE:], recv_ref[0, 0:1, WIDE:]
    return jnp.where(is0, mine, other), jnp.where(is0, other, mine)


def combine_kernel(chips, keep_ref, recv_ref, _, *message_refs):
    chip, core = chip_and_core()
    is0 = core == 0
    log0, log1 = pair_logs(keep_ref, recv_ref, is0)
    logs = three_parts(log0 + log1, HALF)
    decay0, decay1 = jnp.exp(log0), jnp.exp(log1)
    for h in range(HS):
        mine, other = keep_ref[0, :, head(h)], recv_ref[0, :, head(h)]
        first, second = jnp.where(is0, mine, other), jnp.where(is0, other, mine)
        state = (first * decay1[:, h : h + 1] + second).astype(BF16)
        mine, other = keep_ref[1, :, head(h)], recv_ref[1, :, head(h)]
        first, second = jnp.where(is0, mine, other), jnp.where(is0, other, mine)
        grad = (second * decay0[:, h : h + 1] + first).astype(BF16)
        for k in range(1, chips):
            later = chip + k < chips
            message_refs[k - 1][:, head(h)] = jnp.where(later, state, grad)
    for k in range(1, chips):
        message_refs[k - 1][:, WIDE:] = logs


def chain_kernel(chips, keep_ref, recv_ref, sums_ref, _, *refs):
    message_refs = refs[: chips - 1]
    own_ref, give_ref, total_ref = refs[chips - 1 :]
    chip, core = chip_and_core()
    is0 = core == 0
    log0, log1 = pair_logs(keep_ref, recv_ref, is0)
    decay0, decay1 = jnp.exp(log0), jnp.exp(log1)
    weight0, weight1 = log0 * decay0, log1 * decay1
    factors = [None]
    for ref in message_refs:
        parts = ref[:16, WIDE:].astype(F32)
        factors.append(jnp.exp(parts[0:1, :] + parts[1:2, :] + parts[2:3, :]))
    total_ref[...] = sums_ref[...]
    for h in range(HS):
        column = slice(h, h + 1)
        states = [(keep_ref[kind, :, head(h)], recv_ref[kind, :, head(h)]) for kind in range(4)]
        (s0, s1), (g0, g1), (qs0, qs1), (qg0, qg1) = [
            (jnp.where(is0, mine, other), jnp.where(is0, other, mine)) for mine, other in states
        ]
        state = jnp.zeros((HALF, LANES), F32)
        for k in range(chips - 1, 0, -1):
            new = state * factors[k][:, column] + message_refs[k - 1][:, head(h)].astype(F32)
            state = jnp.where(k <= chip, new, state)
        grad = jnp.zeros((HALF, LANES), F32)
        for k in range(1, chips):
            new = grad * factors[k][:, column] + message_refs[k - 1][:, head(h)].astype(F32)
            grad = jnp.where(k > chip, new, grad)
        h0, l1 = state, grad
        h1 = h0 * decay0[:, column] + s0
        l0 = l1 * decay1[:, column] + g1
        cross = h0 * (l0 * weight0[:, column] + qs0) + h1 * (l1 * weight1[:, column] + qs1)
        cross += l0 * qg0 + l1 * qg1
        total_ref[h : h + 1, :] += jnp.sum(cross, axis=0, keepdims=True)
        h0, h1, l0, l1 = (value.astype(BF16) for value in (h0, h1, l0, l1))
        own_ref[0, :, head(h)] = jnp.where(is0, h0, h1)
        own_ref[1, :, head(h)] = jnp.where(is0, l0, l1)
        give_ref[0, :, head(h)] = jnp.where(is0, h1, h0)
        give_ref[1, :, head(h)] = jnp.where(is0, l1, l0)


def block_attention(
    block, most, mask_ref, q_ref, g_ref, kv_ref, out_ref, dq_ref, acc_ref,
    slot_ref, k_ref, k_live_ref, v_ref, q_turned_ref, g_turned_ref, ds_ref, wb_ref,
):
    count = mask_ref.shape[0]
    scale = FACTOR * LOG2E
    lower, upper = slice(0, LANES), slice(LANES, 2 * LANES)
    own = slice(block * BLOCK, (block + 1) * BLOCK)
    at = slice(block * BLOCK, (block + 1) * BLOCK)
    row = lax.axis_index("seq") * (q_ref.shape[0] // BLOCK) + block
    slots = []
    for slot in range(most):
        slot_ref[slot] = row

    def note(j, seen):
        hit = mask_ref[row, j]

        @pl.when(hit == 1)
        def _():
            slot_ref[seen] = j

        return seen + hit

    allowed = lax.fori_loop(0, count, note, 0)
    for slot in range(most):
        index, live = slot_ref[slot], slot < allowed
        slots.append((index, live))
        source = pl.ds(pl.multiple_of(index * BLOCK, BLOCK), BLOCK)
        target = slice(slot * BLOCK, (slot + 1) * BLOCK)
        k_tile, v_tile = kv_ref[source, lower], kv_ref[source, upper]
        k_ref[target, :] = k_tile
        k_live_ref[target, :] = jnp.where(live, k_tile, jnp.zeros_like(k_tile))
        v_ref[target, lower] = jnp.where(live, v_tile, jnp.zeros_like(v_tile))
        v_ref[target, upper] = jnp.full((BLOCK, LANES), jnp.where(live, 1.0, 0.0), F32).astype(BF16)
    group = 2
    for first in range(0, QUERY_HEADS, group):
        heads = range(first, first + group)
        rows = slice(first * BLOCK, (first + group) * BLOCK)
        q = jnp.concatenate([q_ref[at, head(h)] for h in heads], axis=0)
        g = jnp.concatenate([g_ref[at, head(h)] for h in heads], axis=0)
        scores = dot(q, k_ref[...], 1, 1)
        best = jnp.max(scores, axis=1, keepdims=True)
        weights = jnp.exp2((scores - best) * scale)
        wb_ref[rows, :] = weights.astype(BF16)
        both = dot(wb_ref[rows, :], v_ref[...], 1, 0)
        inverse = 1.0 / both[:, upper]
        out = both[:, lower] * inverse
        delta = jnp.sum(out * g.astype(F32), axis=1, keepdims=True)
        dprobs = dot(g, v_ref[:, lower], 1, 1)
        ds_ref[rows, :] = (weights * (dprobs - delta)).astype(BF16)
        dq = (dot(ds_ref[rows, :], k_live_ref[...], 1, 0) * (inverse * FACTOR)).astype(BF16)
        q_turned_ref[:, rows] = (q.astype(F32) * inverse).astype(BF16).T
        g_turned_ref[:, rows] = (g.astype(F32) * inverse).astype(BF16).T
        for place, h in enumerate(heads):
            part = slice(place * BLOCK, (place + 1) * BLOCK)
            out_ref[:, head(h)] = out[part]
            dq_ref[own, head(h)] = dq[part]
    dk = dot(q_turned_ref[...], ds_ref[...], 1, 0)
    dv = dot(g_turned_ref[...], wb_ref[...], 1, 0)
    for slot, (index, live) in enumerate(slots):
        source = slice(slot * BLOCK, (slot + 1) * BLOCK)

        @pl.when(live)
        def _():
            target = pl.ds(pl.multiple_of(index * BLOCK, BLOCK), BLOCK)
            acc_ref[lower, target] += dk[:, source]
            acc_ref[upper, target] += dv[:, source]


def first_attention_kernel(
    chips, most, mask_ref, q_ref, g_ref, stack_ref, other_stack_ref, _, out_ref, dq_ref, acc_ref, kv_ref, *scratch
):
    tokens = q_ref.shape[0]
    chip, core = chip_and_core()
    acc_ref[...] = jnp.zeros_like(acc_ref)
    for k in range(chips):
        for other, ref in enumerate((stack_ref, other_stack_ref)):
            source = 2 * lax.rem(chip + chips - k, chips) + lax.rem(core + other, 2)
            at = pl.ds(pl.multiple_of(source * tokens, tokens), tokens)
            kv_ref[at, :] = ref[k]
    block_attention(0, most, mask_ref, q_ref, g_ref, kv_ref, out_ref, dq_ref, acc_ref, *scratch)


def second_attention_kernel(
    most, mask_ref, q_ref, g_ref, kv_ref, first_dq_ref, first_acc_ref, _, out_ref, dq_ref, acc_ref, *scratch
):
    acc_ref[...] = first_acc_ref[...]
    dq_ref[:BLOCK, :] = first_dq_ref[...]
    block_attention(1, most, mask_ref, q_ref, g_ref, kv_ref, out_ref, dq_ref, acc_ref, *scratch)


def share_kernel(chips, acc_ref, *refs):
    keep_ref, give_ref, sums_ref = refs[-3:]
    tokens = keep_ref.shape[1]
    _, core = chip_and_core()
    sums = refs[0][...]
    for ref in refs[1:-3]:
        sums += ref[...]
    sums_ref[...] = sums
    high = sums.astype(BF16)
    middle = (sums - high.astype(F32)).astype(BF16)
    low = (sums - high.astype(F32) - middle.astype(F32)).astype(BF16)
    give_ref[chips * tokens : chips * tokens + 16, :] = jnp.concatenate([high, middle], axis=1)
    give_ref[chips * tokens + 16 :, :] = jnp.concatenate([low, jnp.zeros_like(low)], axis=1)
    for k in range(chips):
        mine = pl.multiple_of((2 * k + core) * tokens, tokens)
        other = pl.multiple_of((2 * k + 1 - core) * tokens, tokens)
        rows = slice(k * tokens, (k + 1) * tokens)
        keep_ref[rows, :] = acc_ref[:, pl.ds(mine, tokens)].astype(BF16)
        give_ref[rows, :] = acc_ref[:, pl.ds(other, tokens)].astype(BF16)


def pair_sum_kernel(chips, keep_ref, recv_ref, sums_ref, own_ref, total_ref, *message_refs):
    chip, _ = chip_and_core()
    rows = own_ref.shape[0]
    at = pl.ds(pl.multiple_of(chip * rows, rows), rows)
    own_ref[...] = keep_ref[at, :].astype(F32) + recv_ref[at, :].astype(F32)
    total = sums_ref[...] + whole_sums(recv_ref[chips * rows :, :])
    total_ref[...] = total
    high = total.astype(BF16)
    middle = (total - high.astype(F32)).astype(BF16)
    low = (total - high.astype(F32) - middle.astype(F32)).astype(BF16)
    for k in range(1, chips):
        target = pl.ds(pl.multiple_of(lax.rem(chip + k, chips) * rows, rows), rows)
        both = keep_ref[target, :].astype(F32) + recv_ref[target, :].astype(F32)
        message_refs[k - 1][:rows, :] = both.astype(BF16)
        message_refs[k - 1][rows : rows + 16, :] = jnp.concatenate([high, middle], axis=1)
        message_refs[k - 1][rows + 16 :, :] = jnp.concatenate([low, jnp.zeros_like(low)], axis=1)


def whole_sums(tail):
    tail = tail.astype(F32)
    return tail[:16, :LANES] + tail[:16, LANES:] + tail[16:, :LANES]


def owner_sum_kernel(chips, tokens_all, own_ref, sums_ref, *refs):
    parts, (dk_ref, dv_ref, rate_ref, skip_ref) = refs[: chips - 1], refs[chips - 1 :]
    rows = own_ref.shape[0]
    total = own_ref[...]
    sums = sums_ref[...]
    for part in parts:
        total += part[:rows, :].astype(F32)
        sums += whole_sums(part[rows:, :])
    dk_ref[...] = (total[:LANES].T * FACTOR).astype(BF16)
    dv_ref[...] = total[LANES:].T.astype(BF16)
    ones = jnp.ones((8, LANES), F32)
    rate = dot(ones, sums[:HS], 1, 1, HIGH) * (1.0 / tokens_all)
    skip = dot(ones, sums[HS:], 1, 1, HIGH) * (1.0 / (tokens_all * P_SIZE))
    rate_ref[...] = rate[0:1, :]
    skip_ref[...] = skip[0:1, :]


def inner_kernel(
    x_ref, g_ref, b_ref, c_ref, step_ref, rate_ref, skip_ref, _,
    y_ref, dx_ref, db_ref, dc_ref, sums_ref,
    pad_ref, inner_ref, dinner_ref, m_ref, runt_ref,
):
    tokens = 2 * BLOCK
    flat0, flat1, run0, run1 = running_logs(step_ref, rate_ref, pad_ref)
    own = jnp.concatenate([run0, run1], axis=0)
    runt_ref[:, :BLOCK] = flat0
    runt_ref[:, tokens : tokens + BLOCK] = flat0 - flat0[:, BLOCK - 1 :]
    runt_ref[:, tokens + BLOCK :] = flat1
    b = b_ref[...]
    c = c_ref[...]
    inner_ref[...] = dot(c, b, 1, 1)
    dinner_ref[...] = jnp.zeros_like(dinner_ref)
    row0 = lax.broadcasted_iota(jnp.int32, (BLOCK, BLOCK), 0)
    col0 = lax.broadcasted_iota(jnp.int32, (BLOCK, BLOCK), 1)
    row1 = lax.broadcasted_iota(jnp.int32, (BLOCK, tokens), 0)
    col1 = lax.broadcasted_iota(jnp.int32, (BLOCK, tokens), 1)
    seen0 = row0 >= col0
    seen1 = row1 + BLOCK >= col1
    m_ref[:BLOCK, BLOCK:] = jnp.zeros((BLOCK, BLOCK), BF16)
    for h in range(HS):
        lanes = head(h)
        x = x_ref[:, lanes]
        g = g_ref[:, lanes]
        xf, gf = x.astype(F32), g.astype(F32)
        gain = skip_ref[h]
        spread0 = jnp.where(seen0, own[:BLOCK, h : h + 1] - runt_ref[h : h + 1, :BLOCK], NEG)
        spread1 = jnp.where(seen1, own[BLOCK:, h : h + 1] - runt_ref[h : h + 1, tokens:], NEG)
        decay0, decay1 = jnp.exp(spread0), jnp.exp(spread1)
        dm = dot(g, x, 1, 1)
        e0, e1 = decay0 * dm[:BLOCK, :BLOCK], decay1 * dm[BLOCK:, :]
        m_ref[:BLOCK, :BLOCK] = (decay0 * inner_ref[:BLOCK, :BLOCK]).astype(BF16)
        m_ref[BLOCK:, :] = (decay1 * inner_ref[BLOCK:, :]).astype(BF16)
        dinner_ref[:BLOCK, :BLOCK] += e0
        dinner_ref[BLOCK:, :] += e1
        w0 = jnp.sum(spread0 * (e0 * inner_ref[:BLOCK, :BLOCK]), axis=0, keepdims=True)
        w1 = jnp.sum(spread1 * (e1 * inner_ref[BLOCK:, :]), axis=0, keepdims=True)
        m = m_ref[...]
        y_ref[:, lanes] = dot(m, x, 1, 0) + gain * xf
        dx_ref[:, lanes] = dot(m, g, 0, 0) + gain * gf
        sums_ref[h : h + 1, :] = w0 + w1[:, :BLOCK] + w1[:, BLOCK:]
        sums_ref[HS + h : HS + h + 1, :] = jnp.sum(gf * xf, axis=0, keepdims=True)
    dinner = dinner_ref[...].astype(BF16)
    dc_ref[...] = dot(dinner, b, 1, 0)
    db_ref[...] = dot(dinner, c, 0, 0)


def outer_kernel(
    x_ref, g_ref, b_ref, c_ref, step_ref, rate_ref, own_ref, other_ref, first_ref, second_ref,
    inner_y_ref, inner_dx_ref, inner_db_ref, inner_dc_ref, _,
    y_ref, dx_ref, db_ref, dc_ref,
    pad_ref, xt_ref, gt_ref, ent_ref,
):
    _, core = chip_and_core()
    ent_ref[:, pl.ds(pl.multiple_of(core * HALF, HALF), HALF), :] = own_ref[...]
    ent_ref[:, pl.ds(pl.multiple_of((1 - core) * HALF, HALF), HALF), :] = other_ref[...]
    _, _, run0, run1 = running_logs(step_ref, rate_ref, pad_ref)
    enter_log, tail_log, _ = enter_and_tail(run0, run1)
    enter, tail = jnp.exp(enter_log), jnp.exp(tail_log)
    scaled(x_ref, tail, xt_ref)
    scaled(g_ref, enter, gt_ref)
    b = b_ref[...]
    c = c_ref[...]
    for h in range(HS):
        lanes = head(h)
        carried = dot(c, ent_ref[0, :, lanes], 1, 0) * enter[:, h : h + 1]
        back = dot(b, ent_ref[1, :, lanes], 1, 0) * tail[:, h : h + 1]
        y = inner_y_ref[:, lanes] + carried
        y_ref[:BLOCK, lanes] = (y[:BLOCK] + first_ref[:, lanes]).astype(BF16)
        y_ref[BLOCK:, lanes] = (y[BLOCK:] + second_ref[:, lanes]).astype(BF16)
        dx_ref[:, lanes] = (inner_dx_ref[:, lanes] + back).astype(BF16)
    dc_ref[...] = (inner_dc_ref[...] + dot(gt_ref[...], ent_ref[0], 1, 1)).astype(BF16)
    db_ref[...] = (inner_db_ref[...] + dot(xt_ref[...], ent_ref[1], 1, 1)).astype(BF16)


def swapped(array):
    return lax.ppermute(array, "seq", [(i, i ^ 1) for i in range(lax.axis_size("seq"))])


def from_chip(array, k):
    n = lax.axis_size("seq")
    return lax.ppermute(array, "seq", [(i, (i + 2 * k) % n) for i in range(n)])


def turned(array, k):
    n = lax.axis_size("dp")
    return lax.ppermute(array, "dp", [(i, (i + k) % n) for i in range(n)])


def call(kernel, outs, ins, scratch, microseconds, name, limit=16):
    return pl.pallas_call(
        kernel,
        out_shape=tuple(jax.ShapeDtypeStruct(*out) for out in outs),
        in_specs=ins,
        out_specs=(VMEM,) * len(outs),
        scratch_shapes=scratch,
        compiler_params=pltpu.CompilerParams(vmem_limit_bytes=limit << 20),
        cost_estimate=cost(microseconds),
        name=name,
    )


def body(query, key, value, ssm_input, in_b, in_c, step, rate_log, skip, block_mask, grad_out):
    n = lax.axis_size("seq")
    chips = n // 2
    replicas = lax.axis_size("dp")
    tokens = query.shape[1]
    blocks = block_mask.shape[1]
    most = 3 * blocks // 8
    every = blocks * BLOCK
    q, g, x = query[0], grad_out[0], ssm_input[0]
    b, c, steps = in_b[0], in_c[0], step[0].T

    (kv,) = call(
        pack_kernel,
        [((tokens, 2 * LANES), BF16)],
        [AFTER] * 2,
        [pltpu.SemaphoreType.DMA((2,))],
        1,
        "pack_kv",
        60,
    )(key[0], value[0])
    kv_parts = [kv] + [from_chip(kv, k) for k in range(1, chips)]

    half = ((4, HALF, WIDE + LANES), F32)
    keep, give = call(
        local_states_kernel,
        [half, half],
        [AFTER] * 5 + [SMEM, AFTER],
        [
            pltpu.VMEM((tokens, WIDE), BF16),
            pltpu.VMEM((tokens, WIDE), BF16),
            pltpu.VMEM((tokens, NS), BF16),
            pltpu.VMEM((tokens, NS), BF16),
            pltpu.VMEM((HS, tokens), F32),
            pltpu.SemaphoreType.DMA((5,)),
            pltpu.VMEM((LANES, tokens), F32),
            pltpu.VMEM((tokens, WIDE), BF16),
            pltpu.VMEM((tokens, WIDE), BF16),
            pltpu.VMEM((tokens, WIDE), BF16),
            pltpu.VMEM((4, NS, WIDE), F32),
        ],
        20,
        "local_states",
        60,
    )(x, g, b, c, steps, rate_log, kv)
    received = swapped(give)

    inner_y, inner_dx, inner_db, inner_dc, sums = call(
        inner_kernel,
        [((tokens, WIDE), F32)] * 2 + [((tokens, NS), F32)] * 2 + [((2 * HS, LANES), F32)],
        [VMEM] * 5 + [SMEM] * 2 + [AFTER],
        [
            pltpu.VMEM((LANES, tokens), F32),
            pltpu.VMEM((tokens, tokens), F32),
            pltpu.VMEM((tokens, tokens), F32),
            pltpu.VMEM((tokens, tokens), BF16),
            pltpu.VMEM((LANES, 2 * tokens), F32),
        ],
        0.3,
        "chunk_inner",
    )(x, g, b, c, steps, rate_log, skip, keep)

    messages = call(
        lambda *refs: combine_kernel(chips, *refs),
        [((HALF, WIDE + LANES), BF16)] * (chips - 1),
        [VMEM] * 2 + [AFTER],
        [],
        1,
        "combine_states",
    )(keep, received, sums)
    arrived = [from_chip(messages[k - 1], k) for k in range(1, chips)]
    (stack,) = call(
        lambda _, *refs: stack_kernel(*refs),
        [((chips, tokens, 2 * LANES), BF16)],
        [AFTER] + [VMEM] * chips,
        [],
        1,
        "stack_kv",
    )(messages[0], *kv_parts)
    other_stack = swapped(stack)

    columns = QUERY_HEADS * BLOCK
    scratch = [
        pltpu.SMEM((most,), jnp.int32),
        pltpu.VMEM((most * BLOCK, LANES), BF16),
        pltpu.VMEM((most * BLOCK, LANES), BF16),
        pltpu.VMEM((most * BLOCK, 2 * LANES), BF16),
        pltpu.VMEM((LANES, columns), BF16),
        pltpu.VMEM((LANES, columns), BF16),
        pltpu.VMEM((columns, most * BLOCK), BF16),
        pltpu.VMEM((columns, most * BLOCK), BF16),
    ]
    first_out, first_dq, first_acc, kv_all = call(
        lambda *refs: first_attention_kernel(chips, most, *refs),
        [
            ((BLOCK, columns), F32),
            ((BLOCK, columns), BF16),
            ((2 * LANES, every), F32),
            ((every, 2 * LANES), BF16),
        ],
        [SMEM] + [VMEM] * 4 + [AFTER],
        scratch,
        5,
        "first_attention",
        18 + most,
    )(block_mask[0], q, g, stack, other_stack, messages[0])
    entering = ((2, HALF, WIDE), BF16)
    own, give, totals = call(
        lambda *refs: chain_kernel(chips, *refs),
        [entering, entering, ((2 * HS, LANES), F32)],
        [VMEM] * 3 + [AFTER] + [VMEM] * (chips - 1),
        [],
        2,
        "chain_states",
    )(keep, received, sums, first_dq, *arrived)
    other = swapped(give)
    replicated = [turned(totals, k) for k in range(1, replicas)]

    second_out, dq, acc = call(
        lambda *refs: second_attention_kernel(most, *refs),
        [((BLOCK, columns), F32), ((tokens, columns), BF16), ((2 * LANES, every), F32)],
        [SMEM] + [VMEM] * 5 + [AFTER],
        scratch,
        5,
        "second_attention",
        18 + most,
    )(block_mask[0], q, g, kv_all, first_dq, first_acc, totals)
    keep, give, sums = call(
        lambda *refs: share_kernel(chips, *refs),
        [
            ((chips * 2 * LANES, tokens), BF16),
            ((chips * 2 * LANES + 32, tokens), BF16),
            ((2 * HS, LANES), F32),
        ],
        [VMEM] * (1 + replicas),
        [],
        1,
        "share_key_gradients",
    )(acc, totals, *replicated)
    partial, summed, *messages = call(
        lambda *refs: pair_sum_kernel(chips, *refs),
        [((2 * LANES, tokens), F32), ((2 * HS, LANES), F32)]
        + [((2 * LANES + 32, tokens), BF16)] * (chips - 1),
        [VMEM] * 3,
        [],
        1,
        "pair_sum",
    )(keep, swapped(give), sums)
    arrived = [from_chip(messages[k - 1], k) for k in range(1, chips)]

    y, dx, db, dc = call(
        outer_kernel,
        [((tokens, WIDE), BF16)] * 2 + [((tokens, NS), BF16)] * 2,
        [VMEM] * 5 + [SMEM] + [VMEM] * 8 + [AFTER],
        [
            pltpu.VMEM((LANES, tokens), F32),
            pltpu.VMEM((tokens, WIDE), BF16),
            pltpu.VMEM((tokens, WIDE), BF16),
            pltpu.VMEM((2, NS, WIDE), BF16),
        ],
        3,
        "chunk_outer",
    )(
        x, g, b, c, steps, rate_log, own, other, first_out, second_out,
        inner_y, inner_dx, inner_db, inner_dc, messages[0],
    )

    tokens_all = replicas * n * tokens
    dk, dv, grad_rate_log, grad_skip = call(
        lambda *refs: owner_sum_kernel(chips, tokens_all, *refs),
        [((tokens, LANES), BF16)] * 2 + [((1, HS), F32)] * 2,
        [VMEM] * (chips + 1),
        [],
        1,
        "owner_sum",
    )(partial, summed, *arrived)
    return (
        y[None],
        dq[None],
        dk[None],
        dv[None],
        dx[None],
        db[None],
        dc[None],
        grad_rate_log.reshape(HS),
        grad_skip.reshape(HS),
    )


def solution(mesh):
    split = P("dp", "seq", None)
    in_specs = (split,) * 7 + (P(), P(), P("dp", None, None), split)
    out_specs = (split,) * 7 + (P(), P())
    return jax.shard_map(body, mesh=mesh, in_specs=in_specs, out_specs=out_specs, check_vma=False)
```

```python
import jax
import jax.numpy as jnp
from jax import lax
from jax.experimental import pallas as pl
from jax.experimental.pallas import tpu as pltpu
from jax.sharding import PartitionSpec as P

HEAD_WIDTH = 128
QUERY_HEADS = 8
HS = 8
P_SIZE = 128
NS = 128
BLOCK = 128
WIDE = HS * P_SIZE
LANES = 128
FACTOR = HEAD_WIDTH ** (-0.5)
LOG2E = 1.4426950408889634
NEG = -1e30
HALF = NS // 2
HIGH = lax.Precision.HIGHEST
F32 = jnp.float32
BF16 = jnp.bfloat16

VMEM = pl.BlockSpec(memory_space=pltpu.VMEM)
SMEM = pl.BlockSpec(memory_space=pltpu.SMEM)
AFTER = pl.BlockSpec(memory_space=pl.ANY)


def cost(microseconds):
    return pl.CostEstimate(
        flops=int(microseconds * 1.1e9), bytes_accessed=1 << 20, transcendentals=0
    )


def dot(a, b, ca, cb, precision=None):
    return lax.dot_general(
        a, b, (((ca,), (cb,)), ((), ())), preferred_element_type=F32, precision=precision
    )


def head(h):
    return slice(h * LANES, (h + 1) * LANES)


def running_logs(step_ref, rate_ref, pad_ref):
    pad_ref[...] = jnp.zeros_like(pad_ref)
    for h in range(HS):
        rate = jnp.exp(jnp.full((1, 2 * BLOCK), rate_ref[h], F32))
        pad_ref[h : h + 1, :] = -step_ref[h : h + 1, :] * rate
    row = lax.broadcasted_iota(jnp.int32, (BLOCK, BLOCK), 0)
    col = lax.broadcasted_iota(jnp.int32, (BLOCK, BLOCK), 1)
    upper = jnp.where(row <= col, 1.0, 0.0).astype(F32)
    flat0 = dot(pad_ref[:, :BLOCK], upper, 1, 0, HIGH)
    flat1 = dot(pad_ref[:, BLOCK:], upper, 1, 0, HIGH)
    return flat0, flat1, flat0.T, flat1.T


def scaled(x_ref, column, out_ref):
    for h in range(HS):
        out_ref[:, head(h)] = (x_ref[:, head(h)].astype(F32) * column[:, h : h + 1]).astype(BF16)


def chip_and_core():
    me = lax.axis_index("seq")
    return me // 2, me % 2


def fetch(pairs, sems):
    copies = [
        pltpu.make_async_copy(source, target, sems.at[i]) for i, (source, target) in enumerate(pairs)
    ]
    for copy in copies:
        copy.start()
    return copies


def pack_kernel(key_ref, value_ref, out_ref, sems):
    pairs = [(key_ref, out_ref.at[:, :LANES]), (value_ref, out_ref.at[:, LANES:])]
    for copy in fetch(pairs, sems):
        copy.wait()


def split_kernel(states_ref, *refs):
    keep_ref, give_ref, stack_ref = refs[-3:]
    _, core = chip_and_core()
    keep_ref[...] = states_ref[:, pl.ds(pl.multiple_of(core * HALF, HALF), HALF), :]
    give_ref[...] = states_ref[:, pl.ds(pl.multiple_of((1 - core) * HALF, HALF), HALF), :]
    for k, ref in enumerate(refs[:-3]):
        stack_ref[k] = ref[...]


def enter_and_tail(run0, run1):
    t0, t1 = run0[BLOCK - 1 :, :], run1[BLOCK - 1 :, :]
    enter = jnp.concatenate([run0, run1 + t0], axis=0)
    tail = jnp.concatenate([(t0 - run0) + t1, t1 - run1], axis=0)
    return enter, tail, t0 + t1


def local_states_kernel(
    x_ref, g_ref, b_ref, c_ref, step_ref, rate_ref, state_ref, pad_ref, high_ref, rest_ref, log_ref
):
    _, _, run0, run1 = running_logs(step_ref, rate_ref, pad_ref)
    enter_log, tail_log, total = enter_and_tail(run0, run1)
    enter, tail = jnp.exp(enter_log), jnp.exp(tail_log)
    state_ref[:, :, WIDE:] = jnp.broadcast_to(total, (4, NS, LANES))
    cases = ((b_ref, x_ref, tail, tail_log), (c_ref, g_ref, enter, enter_log))
    for direction, (left, right, factor, weight) in enumerate(cases):
        for h in range(HS):
            product = right[:, head(h)].astype(F32) * factor[:, h : h + 1]
            rounded = product.astype(BF16)
            high_ref[:, head(h)] = rounded
            rest_ref[:, head(h)] = (product - rounded.astype(F32)).astype(BF16)
            log_ref[:, head(h)] = (product * weight[:, h : h + 1]).astype(BF16)
        turned_left = left[...].astype(F32).T.astype(BF16)
        state_ref[direction, :, :WIDE] = dot(turned_left, high_ref[...], 1, 0) + dot(
            turned_left, rest_ref[...], 1, 0
        )
        state_ref[3 - direction, :, :WIDE] = dot(turned_left, log_ref[...], 1, 0)


def three_parts(value, rows):
    high = value.astype(BF16).astype(F32)
    middle = (value - high).astype(BF16).astype(F32)
    low = value - high - middle
    index = lax.broadcasted_iota(jnp.int32, (rows, LANES), 0)
    return jnp.where(index == 0, high, jnp.where(index == 1, middle, low)).astype(BF16)


def pair_logs(keep_ref, recv_ref, is0):
    mine, other = keep_ref[0, 0:1, WIDE:], recv_ref[0, 0:1, WIDE:]
    return jnp.where(is0, mine, other), jnp.where(is0, other, mine)


def combine_kernel(chips, keep_ref, recv_ref, _, *message_refs):
    chip, core = chip_and_core()
    is0 = core == 0
    log0, log1 = pair_logs(keep_ref, recv_ref, is0)
    logs = three_parts(log0 + log1, HALF)
    decay0, decay1 = jnp.exp(log0), jnp.exp(log1)
    for h in range(HS):
        mine, other = keep_ref[0, :, head(h)], recv_ref[0, :, head(h)]
        first, second = jnp.where(is0, mine, other), jnp.where(is0, other, mine)
        state = (first * decay1[:, h : h + 1] + second).astype(BF16)
        mine, other = keep_ref[1, :, head(h)], recv_ref[1, :, head(h)]
        first, second = jnp.where(is0, mine, other), jnp.where(is0, other, mine)
        grad = (second * decay0[:, h : h + 1] + first).astype(BF16)
        for k in range(1, chips):
            later = chip + k < chips
            message_refs[k - 1][:, head(h)] = jnp.where(later, state, grad)
    for k in range(1, chips):
        message_refs[k - 1][:, WIDE:] = logs


def chain_kernel(chips, keep_ref, recv_ref, sums_ref, _, *refs):
    message_refs = refs[: chips - 1]
    own_ref, give_ref, total_ref = refs[chips - 1 :]
    chip, core = chip_and_core()
    is0 = core == 0
    log0, log1 = pair_logs(keep_ref, recv_ref, is0)
    decay0, decay1 = jnp.exp(log0), jnp.exp(log1)
    weight0, weight1 = log0 * decay0, log1 * decay1
    factors = [None]
    for ref in message_refs:
        parts = ref[:16, WIDE:].astype(F32)
        factors.append(jnp.exp(parts[0:1, :] + parts[1:2, :] + parts[2:3, :]))
    total_ref[...] = sums_ref[...]
    for h in range(HS):
        column = slice(h, h + 1)
        states = [(keep_ref[kind, :, head(h)], recv_ref[kind, :, head(h)]) for kind in range(4)]
        (s0, s1), (g0, g1), (qs0, qs1), (qg0, qg1) = [
            (jnp.where(is0, mine, other), jnp.where(is0, other, mine)) for mine, other in states
        ]
        state = jnp.zeros((HALF, LANES), F32)
        for k in range(chips - 1, 0, -1):
            new = state * factors[k][:, column] + message_refs[k - 1][:, head(h)].astype(F32)
            state = jnp.where(k <= chip, new, state)
        grad = jnp.zeros((HALF, LANES), F32)
        for k in range(1, chips):
            new = grad * factors[k][:, column] + message_refs[k - 1][:, head(h)].astype(F32)
            grad = jnp.where(k > chip, new, grad)
        h0, l1 = state, grad
        h1 = h0 * decay0[:, column] + s0
        l0 = l1 * decay1[:, column] + g1
        cross = h0 * (l0 * weight0[:, column] + qs0) + h1 * (l1 * weight1[:, column] + qs1)
        cross += l0 * qg0 + l1 * qg1
        total_ref[h : h + 1, :] += jnp.sum(cross, axis=0, keepdims=True)
        h0, h1, l0, l1 = (value.astype(BF16) for value in (h0, h1, l0, l1))
        own_ref[0, :, head(h)] = jnp.where(is0, h0, h1)
        own_ref[1, :, head(h)] = jnp.where(is0, l0, l1)
        give_ref[0, :, head(h)] = jnp.where(is0, h1, h0)
        give_ref[1, :, head(h)] = jnp.where(is0, l1, l0)


def block_attention(
    block, most, mask_ref, q_ref, g_ref, kv_ref, out_ref, dq_ref, acc_ref,
    slot_ref, k_ref, k_live_ref, v_ref, q_turned_ref, g_turned_ref, ds_ref, wb_ref,
):
    count = mask_ref.shape[0]
    scale = FACTOR * LOG2E
    lower, upper = slice(0, LANES), slice(LANES, 2 * LANES)
    own = slice(block * BLOCK, (block + 1) * BLOCK)
    at = slice(block * BLOCK, (block + 1) * BLOCK)
    row = lax.axis_index("seq") * (q_ref.shape[0] // BLOCK) + block
    slots = []
    for slot in range(most):
        slot_ref[slot] = row

    def note(j, seen):
        hit = mask_ref[row, j]

        @pl.when(hit == 1)
        def _():
            slot_ref[seen] = j

        return seen + hit

    allowed = lax.fori_loop(0, count, note, 0)
    for slot in range(most):
        index, live = slot_ref[slot], slot < allowed
        slots.append((index, live))
        source = pl.ds(pl.multiple_of(index * BLOCK, BLOCK), BLOCK)
        target = slice(slot * BLOCK, (slot + 1) * BLOCK)
        k_tile, v_tile = kv_ref[source, lower], kv_ref[source, upper]
        k_ref[target, :] = k_tile
        k_live_ref[target, :] = jnp.where(live, k_tile, jnp.zeros_like(k_tile))
        v_ref[target, lower] = jnp.where(live, v_tile, jnp.zeros_like(v_tile))
        v_ref[target, upper] = jnp.full((BLOCK, LANES), jnp.where(live, 1.0, 0.0), F32).astype(BF16)
    group = 2
    firsts = range(0, QUERY_HEADS, group)

    def stacked(ref, first):
        return jnp.concatenate([ref[at, head(h)] for h in range(first, first + group)], axis=0)

    upcoming = dot(stacked(q_ref, 0), k_ref[...], 1, 1)
    for first in firsts:
        heads = range(first, first + group)
        rows = slice(first * BLOCK, (first + group) * BLOCK)
        q, g = stacked(q_ref, first), stacked(g_ref, first)
        scores = upcoming
        dprobs = dot(g, v_ref[:, lower], 1, 1)
        if first + group < QUERY_HEADS:
            upcoming = dot(stacked(q_ref, first + group), k_ref[...], 1, 1)
        best = jnp.max(scores, axis=1, keepdims=True)
        weights = jnp.exp2((scores - best) * scale)
        wb_ref[rows, :] = weights.astype(BF16)
        both = dot(wb_ref[rows, :], v_ref[...], 1, 0)
        inverse = 1.0 / both[:, upper]
        out = both[:, lower] * inverse
        delta = jnp.sum(out * g.astype(F32), axis=1, keepdims=True)
        ds_ref[rows, :] = (weights * (dprobs - delta)).astype(BF16)
        dq = (dot(ds_ref[rows, :], k_live_ref[...], 1, 0) * (inverse * FACTOR)).astype(BF16)
        q_turned_ref[:, rows] = (q.astype(F32) * inverse).astype(BF16).T
        g_turned_ref[:, rows] = (g.astype(F32) * inverse).astype(BF16).T
        for place, h in enumerate(heads):
            part = slice(place * BLOCK, (place + 1) * BLOCK)
            out_ref[:, head(h)] = out[part]
            dq_ref[own, head(h)] = dq[part]
    dk = dot(q_turned_ref[...], ds_ref[...], 1, 0)
    dv = dot(g_turned_ref[...], wb_ref[...], 1, 0)
    for slot, (index, live) in enumerate(slots):
        source = slice(slot * BLOCK, (slot + 1) * BLOCK)

        @pl.when(live)
        def _():
            target = pl.ds(pl.multiple_of(index * BLOCK, BLOCK), BLOCK)
            acc_ref[lower, target] += dk[:, source]
            acc_ref[upper, target] += dv[:, source]


def first_attention_kernel(
    chips, most, mask_ref, q_ref, g_ref, stack_ref, other_stack_ref, _, out_ref, dq_ref, acc_ref, kv_ref, *scratch
):
    tokens = q_ref.shape[0]
    chip, core = chip_and_core()
    acc_ref[...] = jnp.zeros_like(acc_ref)
    for k in range(chips):
        for other, ref in enumerate((stack_ref, other_stack_ref)):
            source = 2 * lax.rem(chip + chips - k, chips) + lax.rem(core + other, 2)
            at = pl.ds(pl.multiple_of(source * tokens, tokens), tokens)
            kv_ref[at, :] = ref[k]
    block_attention(0, most, mask_ref, q_ref, g_ref, kv_ref, out_ref, dq_ref, acc_ref, *scratch)


def second_attention_kernel(
    most, mask_ref, q_ref, g_ref, kv_ref, first_dq_ref, first_acc_ref, _, out_ref, dq_ref, acc_ref, *scratch
):
    acc_ref[...] = first_acc_ref[...]
    dq_ref[:BLOCK, :] = first_dq_ref[...]
    block_attention(1, most, mask_ref, q_ref, g_ref, kv_ref, out_ref, dq_ref, acc_ref, *scratch)


def share_kernel(chips, acc_ref, *refs):
    keep_ref, give_ref, sums_ref = refs[-3:]
    tokens = keep_ref.shape[1]
    _, core = chip_and_core()
    sums = refs[0][...]
    for ref in refs[1:-3]:
        sums += ref[...]
    sums_ref[...] = sums
    high = sums.astype(BF16)
    middle = (sums - high.astype(F32)).astype(BF16)
    low = (sums - high.astype(F32) - middle.astype(F32)).astype(BF16)
    give_ref[chips * tokens : chips * tokens + 16, :] = jnp.concatenate([high, middle], axis=1)
    give_ref[chips * tokens + 16 :, :] = jnp.concatenate([low, jnp.zeros_like(low)], axis=1)
    for k in range(chips):
        mine = pl.multiple_of((2 * k + core) * tokens, tokens)
        other = pl.multiple_of((2 * k + 1 - core) * tokens, tokens)
        rows = slice(k * tokens, (k + 1) * tokens)
        keep_ref[rows, :] = acc_ref[:, pl.ds(mine, tokens)].astype(BF16)
        give_ref[rows, :] = acc_ref[:, pl.ds(other, tokens)].astype(BF16)


def pair_sum_kernel(chips, keep_ref, recv_ref, sums_ref, own_ref, total_ref, *message_refs):
    chip, _ = chip_and_core()
    rows = own_ref.shape[0]
    at = pl.ds(pl.multiple_of(chip * rows, rows), rows)
    own_ref[...] = keep_ref[at, :].astype(F32) + recv_ref[at, :].astype(F32)
    total = sums_ref[...] + whole_sums(recv_ref[chips * rows :, :])
    total_ref[...] = total
    high = total.astype(BF16)
    middle = (total - high.astype(F32)).astype(BF16)
    low = (total - high.astype(F32) - middle.astype(F32)).astype(BF16)
    for k in range(1, chips):
        target = pl.ds(pl.multiple_of(lax.rem(chip + k, chips) * rows, rows), rows)
        both = keep_ref[target, :].astype(F32) + recv_ref[target, :].astype(F32)
        message_refs[k - 1][:rows, :] = both.astype(BF16)
        message_refs[k - 1][rows : rows + 16, :] = jnp.concatenate([high, middle], axis=1)
        message_refs[k - 1][rows + 16 :, :] = jnp.concatenate([low, jnp.zeros_like(low)], axis=1)


def whole_sums(tail):
    tail = tail.astype(F32)
    return tail[:16, :LANES] + tail[:16, LANES:] + tail[16:, :LANES]


def owner_sum_kernel(chips, tokens_all, own_ref, sums_ref, *refs):
    parts, (dk_ref, dv_ref, rate_ref, skip_ref) = refs[: chips - 1], refs[chips - 1 :]
    rows = own_ref.shape[0]
    total = own_ref[...]
    sums = sums_ref[...]
    for part in parts:
        total += part[:rows, :].astype(F32)
        sums += whole_sums(part[rows:, :])
    dk_ref[...] = (total[:LANES].T * FACTOR).astype(BF16)
    dv_ref[...] = total[LANES:].T.astype(BF16)
    ones = jnp.ones((8, LANES), F32)
    rate = dot(ones, sums[:HS], 1, 1, HIGH) * (1.0 / tokens_all)
    skip = dot(ones, sums[HS:], 1, 1, HIGH) * (1.0 / (tokens_all * P_SIZE))
    rate_ref[...] = rate[0:1, :]
    skip_ref[...] = skip[0:1, :]


def inner_kernel(
    x_ref, g_ref, b_ref, c_ref, step_ref, rate_ref, skip_ref,
    y_ref, dx_ref, db_ref, dc_ref, sums_ref,
    pad_ref, inner_ref, dinner_ref, m_ref, runt_ref,
):
    tokens = 2 * BLOCK
    flat0, flat1, run0, run1 = running_logs(step_ref, rate_ref, pad_ref)
    own = jnp.concatenate([run0, run1], axis=0)
    runt_ref[:, :BLOCK] = flat0
    runt_ref[:, tokens : tokens + BLOCK] = flat0 - flat0[:, BLOCK - 1 :]
    runt_ref[:, tokens + BLOCK :] = flat1
    b = b_ref[...]
    c = c_ref[...]
    inner_ref[...] = dot(c, b, 1, 1)
    dinner_ref[...] = jnp.zeros_like(dinner_ref)
    row0 = lax.broadcasted_iota(jnp.int32, (BLOCK, BLOCK), 0)
    col0 = lax.broadcasted_iota(jnp.int32, (BLOCK, BLOCK), 1)
    row1 = lax.broadcasted_iota(jnp.int32, (BLOCK, tokens), 0)
    col1 = lax.broadcasted_iota(jnp.int32, (BLOCK, tokens), 1)
    seen0 = row0 >= col0
    seen1 = row1 + BLOCK >= col1
    m_ref[:BLOCK, BLOCK:] = jnp.zeros((BLOCK, BLOCK), BF16)
    for h in range(HS):
        lanes = head(h)
        x = x_ref[:, lanes]
        g = g_ref[:, lanes]
        xf, gf = x.astype(F32), g.astype(F32)
        gain = skip_ref[h]
        spread0 = jnp.where(seen0, own[:BLOCK, h : h + 1] - runt_ref[h : h + 1, :BLOCK], NEG)
        spread1 = jnp.where(seen1, own[BLOCK:, h : h + 1] - runt_ref[h : h + 1, tokens:], NEG)
        decay0, decay1 = jnp.exp(spread0), jnp.exp(spread1)
        dm = dot(g, x, 1, 1)
        e0, e1 = decay0 * dm[:BLOCK, :BLOCK], decay1 * dm[BLOCK:, :]
        m_ref[:BLOCK, :BLOCK] = (decay0 * inner_ref[:BLOCK, :BLOCK]).astype(BF16)
        m_ref[BLOCK:, :] = (decay1 * inner_ref[BLOCK:, :]).astype(BF16)
        dinner_ref[:BLOCK, :BLOCK] += e0
        dinner_ref[BLOCK:, :] += e1
        w0 = jnp.sum(spread0 * (e0 * inner_ref[:BLOCK, :BLOCK]), axis=0, keepdims=True)
        w1 = jnp.sum(spread1 * (e1 * inner_ref[BLOCK:, :]), axis=0, keepdims=True)
        m = m_ref[...]
        y_ref[:, lanes] = dot(m, x, 1, 0) + gain * xf
        dx_ref[:, lanes] = dot(m, g, 0, 0) + gain * gf
        sums_ref[h : h + 1, :] = w0 + w1[:, :BLOCK] + w1[:, BLOCK:]
        sums_ref[HS + h : HS + h + 1, :] = jnp.sum(gf * xf, axis=0, keepdims=True)
    dinner = dinner_ref[...].astype(BF16)
    dc_ref[...] = dot(dinner, b, 1, 0)
    db_ref[...] = dot(dinner, c, 0, 0)


def chunk_kernel(
    x_ref, g_ref, b_ref, c_ref, step_ref, rate_ref, skip_ref, _,
    state_ref, y_ref, dx_ref, db_ref, dc_ref, sums_ref, pad_ref, *scratch
):
    operands = (x_ref, g_ref, b_ref, c_ref, step_ref, rate_ref)
    local_states_kernel(*operands, state_ref, pad_ref, *scratch[:3])
    inner_kernel(*operands, skip_ref, y_ref, dx_ref, db_ref, dc_ref, sums_ref, pad_ref, *scratch[3:])


def outer_kernel(
    x_ref, g_ref, b_ref, c_ref, step_ref, rate_ref, own_ref, other_ref, first_ref, second_ref,
    inner_y_ref, inner_dx_ref, inner_db_ref, inner_dc_ref, _,
    y_ref, dx_ref, db_ref, dc_ref,
    pad_ref, xt_ref, gt_ref, ent_ref,
):
    _, core = chip_and_core()
    ent_ref[:, pl.ds(pl.multiple_of(core * HALF, HALF), HALF), :] = own_ref[...]
    ent_ref[:, pl.ds(pl.multiple_of((1 - core) * HALF, HALF), HALF), :] = other_ref[...]
    _, _, run0, run1 = running_logs(step_ref, rate_ref, pad_ref)
    enter_log, tail_log, _ = enter_and_tail(run0, run1)
    enter, tail = jnp.exp(enter_log), jnp.exp(tail_log)
    scaled(x_ref, tail, xt_ref)
    scaled(g_ref, enter, gt_ref)
    b = b_ref[...]
    c = c_ref[...]
    for h in range(HS):
        lanes = head(h)
        carried = dot(c, ent_ref[0, :, lanes], 1, 0) * enter[:, h : h + 1]
        back = dot(b, ent_ref[1, :, lanes], 1, 0) * tail[:, h : h + 1]
        y = inner_y_ref[:, lanes] + carried
        y_ref[:BLOCK, lanes] = (y[:BLOCK] + first_ref[:, lanes]).astype(BF16)
        y_ref[BLOCK:, lanes] = (y[BLOCK:] + second_ref[:, lanes]).astype(BF16)
        dx_ref[:, lanes] = (inner_dx_ref[:, lanes] + back).astype(BF16)
    dc_ref[...] = (inner_dc_ref[...] + dot(gt_ref[...], ent_ref[0], 1, 1)).astype(BF16)
    db_ref[...] = (inner_db_ref[...] + dot(xt_ref[...], ent_ref[1], 1, 1)).astype(BF16)


def swapped(array):
    return lax.ppermute(array, "seq", [(i, i ^ 1) for i in range(lax.axis_size("seq"))])


def from_chip(array, k):
    n = lax.axis_size("seq")
    return lax.ppermute(array, "seq", [(i, (i + 2 * k) % n) for i in range(n)])


def turned(array, k):
    n = lax.axis_size("dp")
    return lax.ppermute(array, "dp", [(i, (i + k) % n) for i in range(n)])


def call(kernel, outs, ins, scratch, microseconds, name, limit=16):
    return pl.pallas_call(
        kernel,
        out_shape=tuple(jax.ShapeDtypeStruct(*out) for out in outs),
        in_specs=ins,
        out_specs=(VMEM,) * len(outs),
        scratch_shapes=scratch,
        compiler_params=pltpu.CompilerParams(vmem_limit_bytes=limit << 20),
        cost_estimate=cost(microseconds),
        name=name,
    )


def body(query, key, value, ssm_input, in_b, in_c, step, rate_log, skip, block_mask, grad_out):
    n = lax.axis_size("seq")
    chips = n // 2
    replicas = lax.axis_size("dp")
    tokens = query.shape[1]
    blocks = block_mask.shape[1]
    most = 3 * blocks // 8
    every = blocks * BLOCK
    q, g, x = query[0], grad_out[0], ssm_input[0]
    b, c, steps = in_b[0], in_c[0], step[0].T

    (kv,) = call(
        pack_kernel,
        [((tokens, 2 * LANES), BF16)],
        [AFTER] * 2,
        [pltpu.SemaphoreType.DMA((2,))],
        1,
        "pack_kv",
        60,
    )(key[0], value[0])
    kv_parts = [kv] + [from_chip(kv, k) for k in range(1, chips)]

    states, inner_y, inner_dx, inner_db, inner_dc, sums = call(
        chunk_kernel,
        [((4, NS, WIDE + LANES), F32)]
        + [((tokens, WIDE), F32)] * 2
        + [((tokens, NS), F32)] * 2
        + [((2 * HS, LANES), F32)],
        [VMEM] * 5 + [SMEM] * 2 + [AFTER],
        [
            pltpu.VMEM((LANES, tokens), F32),
            pltpu.VMEM((tokens, WIDE), BF16),
            pltpu.VMEM((tokens, WIDE), BF16),
            pltpu.VMEM((tokens, WIDE), BF16),
            pltpu.VMEM((tokens, tokens), F32),
            pltpu.VMEM((tokens, tokens), F32),
            pltpu.VMEM((tokens, tokens), BF16),
            pltpu.VMEM((LANES, 2 * tokens), F32),
        ],
        6,
        "chunk_alone",
        20,
    )(x, g, b, c, steps, rate_log, skip, kv)
    half = ((4, HALF, WIDE + LANES), F32)
    keep, give, stack = call(
        split_kernel,
        [half, half, ((chips, tokens, 2 * LANES), BF16)],
        [VMEM] * (1 + chips),
        [],
        1,
        "split_states",
    )(states, *kv_parts)
    received = swapped(give)
    other_stack = swapped(stack)

    messages = call(
        lambda *refs: combine_kernel(chips, *refs),
        [((HALF, WIDE + LANES), BF16)] * (chips - 1),
        [VMEM] * 2 + [AFTER],
        [],
        1,
        "combine_states",
    )(keep, received, sums)
    arrived = [from_chip(messages[k - 1], k) for k in range(1, chips)]

    columns = QUERY_HEADS * BLOCK
    scratch = [
        pltpu.SMEM((most,), jnp.int32),
        pltpu.VMEM((most * BLOCK, LANES), BF16),
        pltpu.VMEM((most * BLOCK, LANES), BF16),
        pltpu.VMEM((most * BLOCK, 2 * LANES), BF16),
        pltpu.VMEM((LANES, columns), BF16),
        pltpu.VMEM((LANES, columns), BF16),
        pltpu.VMEM((columns, most * BLOCK), BF16),
        pltpu.VMEM((columns, most * BLOCK), BF16),
    ]
    first_out, first_dq, first_acc, kv_all = call(
        lambda *refs: first_attention_kernel(chips, most, *refs),
        [
            ((BLOCK, columns), F32),
            ((BLOCK, columns), BF16),
            ((2 * LANES, every), F32),
            ((every, 2 * LANES), BF16),
        ],
        [SMEM] + [VMEM] * 4 + [AFTER],
        scratch,
        5,
        "first_attention",
        18 + most,
    )(block_mask[0], q, g, stack, other_stack, messages[0])
    entering = ((2, HALF, WIDE), BF16)
    own, give, totals = call(
        lambda *refs: chain_kernel(chips, *refs),
        [entering, entering, ((2 * HS, LANES), F32)],
        [VMEM] * 3 + [AFTER] + [VMEM] * (chips - 1),
        [],
        2,
        "chain_states",
    )(keep, received, sums, first_dq, *arrived)
    other = swapped(give)
    replicated = [turned(totals, k) for k in range(1, replicas)]

    second_out, dq, acc = call(
        lambda *refs: second_attention_kernel(most, *refs),
        [((BLOCK, columns), F32), ((tokens, columns), BF16), ((2 * LANES, every), F32)],
        [SMEM] + [VMEM] * 5 + [AFTER],
        scratch,
        5,
        "second_attention",
        18 + most,
    )(block_mask[0], q, g, kv_all, first_dq, first_acc, totals)
    keep, give, sums = call(
        lambda *refs: share_kernel(chips, *refs),
        [
            ((chips * 2 * LANES, tokens), BF16),
            ((chips * 2 * LANES + 32, tokens), BF16),
            ((2 * HS, LANES), F32),
        ],
        [VMEM] * (1 + replicas),
        [],
        1,
        "share_key_gradients",
    )(acc, totals, *replicated)
    partial, summed, *messages = call(
        lambda *refs: pair_sum_kernel(chips, *refs),
        [((2 * LANES, tokens), F32), ((2 * HS, LANES), F32)]
        + [((2 * LANES + 32, tokens), BF16)] * (chips - 1),
        [VMEM] * 3,
        [],
        1,
        "pair_sum",
    )(keep, swapped(give), sums)
    arrived = [from_chip(messages[k - 1], k) for k in range(1, chips)]

    y, dx, db, dc = call(
        outer_kernel,
        [((tokens, WIDE), BF16)] * 2 + [((tokens, NS), BF16)] * 2,
        [VMEM] * 5 + [SMEM] + [VMEM] * 8 + [AFTER],
        [
            pltpu.VMEM((LANES, tokens), F32),
            pltpu.VMEM((tokens, WIDE), BF16),
            pltpu.VMEM((tokens, WIDE), BF16),
            pltpu.VMEM((2, NS, WIDE), BF16),
        ],
        3,
        "chunk_outer",
    )(
        x, g, b, c, steps, rate_log, own, other, first_out, second_out,
        inner_y, inner_dx, inner_db, inner_dc, messages[0],
    )

    tokens_all = replicas * n * tokens
    dk, dv, grad_rate_log, grad_skip = call(
        lambda *refs: owner_sum_kernel(chips, tokens_all, *refs),
        [((tokens, LANES), BF16)] * 2 + [((1, HS), F32)] * 2,
        [VMEM] * (chips + 1),
        [],
        1,
        "owner_sum",
    )(partial, summed, *arrived)
    return (
        y[None],
        dq[None],
        dk[None],
        dv[None],
        dx[None],
        db[None],
        dc[None],
        grad_rate_log.reshape(HS),
        grad_skip.reshape(HS),
    )


def solution(mesh):
    split = P("dp", "seq", None)
    in_specs = (split,) * 7 + (P(), P(), P("dp", None, None), split)
    out_specs = (split,) * 7 + (P(), P())
    return jax.shard_map(body, mesh=mesh, in_specs=in_specs, out_specs=out_specs, check_vma=False)
```

```python
import jax
import jax.numpy as jnp
from jax import lax
from jax.experimental import pallas as pl
from jax.experimental.pallas import tpu as pltpu
from jax.sharding import PartitionSpec as P

HEAD_WIDTH = 128
QUERY_HEADS = 8
HS = 8
P_SIZE = 128
NS = 128
BLOCK = 128
WIDE = HS * P_SIZE
LANES = 128
FACTOR = HEAD_WIDTH ** (-0.5)
LOG2E = 1.4426950408889634
NEG = -1e30
HALF = NS // 2
EARLY_HEADS = 4
HIGH = lax.Precision.HIGHEST
F32 = jnp.float32
BF16 = jnp.bfloat16

VMEM = pl.BlockSpec(memory_space=pltpu.VMEM)
SMEM = pl.BlockSpec(memory_space=pltpu.SMEM)
AFTER = pl.BlockSpec(memory_space=pl.ANY)


def cost(microseconds):
    return pl.CostEstimate(
        flops=int(microseconds * 1.1e9), bytes_accessed=1 << 20, transcendentals=0
    )


def dot(a, b, ca, cb, precision=None):
    return lax.dot_general(
        a, b, (((ca,), (cb,)), ((), ())), preferred_element_type=F32, precision=precision
    )


def head(h):
    return slice(h * LANES, (h + 1) * LANES)


def running_logs(step_ref, rate_ref, pad_ref):
    pad_ref[...] = jnp.zeros_like(pad_ref)
    for h in range(HS):
        rate = jnp.exp(jnp.full((1, 2 * BLOCK), rate_ref[h], F32))
        pad_ref[h : h + 1, :] = -step_ref[h : h + 1, :] * rate
    row = lax.broadcasted_iota(jnp.int32, (BLOCK, BLOCK), 0)
    col = lax.broadcasted_iota(jnp.int32, (BLOCK, BLOCK), 1)
    upper = jnp.where(row <= col, 1.0, 0.0).astype(F32)
    flat0 = dot(pad_ref[:, :BLOCK], upper, 1, 0, HIGH)
    flat1 = dot(pad_ref[:, BLOCK:], upper, 1, 0, HIGH)
    return flat0, flat1, flat0.T, flat1.T


def scaled(x_ref, column, out_ref):
    for h in range(HS):
        out_ref[:, head(h)] = (x_ref[:, head(h)].astype(F32) * column[:, h : h + 1]).astype(BF16)


def chip_and_core():
    me = lax.axis_index("seq")
    return me // 2, me % 2


def fetch(pairs, sems):
    copies = [
        pltpu.make_async_copy(source, target, sems.at[i]) for i, (source, target) in enumerate(pairs)
    ]
    for copy in copies:
        copy.start()
    return copies


def pack_kernel(key_ref, value_ref, out_ref, sems):
    pairs = [(key_ref, out_ref.at[:, :LANES]), (value_ref, out_ref.at[:, LANES:])]
    for copy in fetch(pairs, sems):
        copy.wait()


def split_kernel(states_ref, *refs):
    keep_ref, give_ref, stack_ref = refs[-3:]
    _, core = chip_and_core()
    keep_ref[...] = states_ref[:, pl.ds(pl.multiple_of(core * HALF, HALF), HALF), :]
    give_ref[...] = states_ref[:, pl.ds(pl.multiple_of((1 - core) * HALF, HALF), HALF), :]
    for k, ref in enumerate(refs[:-3]):
        stack_ref[k] = ref[...]


def enter_and_tail(run0, run1):
    t0, t1 = run0[BLOCK - 1 :, :], run1[BLOCK - 1 :, :]
    enter = jnp.concatenate([run0, run1 + t0], axis=0)
    tail = jnp.concatenate([(t0 - run0) + t1, t1 - run1], axis=0)
    return enter, tail, t0 + t1


def local_states_kernel(
    x_ref, g_ref, b_ref, c_ref, step_ref, rate_ref, state_ref, pad_ref, high_ref, rest_ref, log_ref
):
    _, _, run0, run1 = running_logs(step_ref, rate_ref, pad_ref)
    enter_log, tail_log, total = enter_and_tail(run0, run1)
    enter, tail = jnp.exp(enter_log), jnp.exp(tail_log)
    state_ref[:, :, WIDE:] = jnp.broadcast_to(total, (4, NS, LANES))
    cases = ((b_ref, x_ref, tail, tail_log), (c_ref, g_ref, enter, enter_log))
    for direction, (left, right, factor, weight) in enumerate(cases):
        for h in range(HS):
            product = right[:, head(h)].astype(F32) * factor[:, h : h + 1]
            rounded = product.astype(BF16)
            high_ref[:, head(h)] = rounded
            rest_ref[:, head(h)] = (product - rounded.astype(F32)).astype(BF16)
            log_ref[:, head(h)] = (product * weight[:, h : h + 1]).astype(BF16)
        turned_left = left[...].astype(F32).T.astype(BF16)
        state_ref[direction, :, :WIDE] = dot(turned_left, high_ref[...], 1, 0) + dot(
            turned_left, rest_ref[...], 1, 0
        )
        state_ref[3 - direction, :, :WIDE] = dot(turned_left, log_ref[...], 1, 0)


def three_parts(value, rows):
    high = value.astype(BF16).astype(F32)
    middle = (value - high).astype(BF16).astype(F32)
    low = value - high - middle
    index = lax.broadcasted_iota(jnp.int32, (rows, LANES), 0)
    return jnp.where(index == 0, high, jnp.where(index == 1, middle, low)).astype(BF16)


def pair_logs(keep_ref, recv_ref, is0):
    mine, other = keep_ref[0, 0:1, WIDE:], recv_ref[0, 0:1, WIDE:]
    return jnp.where(is0, mine, other), jnp.where(is0, other, mine)


def combine_kernel(chips, keep_ref, recv_ref, _, *message_refs):
    chip, core = chip_and_core()
    is0 = core == 0
    log0, log1 = pair_logs(keep_ref, recv_ref, is0)
    logs = three_parts(log0 + log1, HALF)
    decay0, decay1 = jnp.exp(log0), jnp.exp(log1)
    for h in range(HS):
        mine, other = keep_ref[0, :, head(h)], recv_ref[0, :, head(h)]
        first, second = jnp.where(is0, mine, other), jnp.where(is0, other, mine)
        state = (first * decay1[:, h : h + 1] + second).astype(BF16)
        mine, other = keep_ref[1, :, head(h)], recv_ref[1, :, head(h)]
        first, second = jnp.where(is0, mine, other), jnp.where(is0, other, mine)
        grad = (second * decay0[:, h : h + 1] + first).astype(BF16)
        for k in range(1, chips):
            later = chip + k < chips
            message_refs[k - 1][:, head(h)] = jnp.where(later, state, grad)
    for k in range(1, chips):
        message_refs[k - 1][:, WIDE:] = logs


def chain_kernel(chips, keep_ref, recv_ref, sums_ref, _, *refs):
    message_refs = refs[: chips - 1]
    own_ref, give_ref, total_ref = refs[chips - 1 :]
    chip, core = chip_and_core()
    is0 = core == 0
    log0, log1 = pair_logs(keep_ref, recv_ref, is0)
    decay0, decay1 = jnp.exp(log0), jnp.exp(log1)
    weight0, weight1 = log0 * decay0, log1 * decay1
    factors = [None]
    for ref in message_refs:
        parts = ref[:16, WIDE:].astype(F32)
        factors.append(jnp.exp(parts[0:1, :] + parts[1:2, :] + parts[2:3, :]))
    total_ref[...] = sums_ref[...]
    for h in range(HS):
        column = slice(h, h + 1)
        states = [(keep_ref[kind, :, head(h)], recv_ref[kind, :, head(h)]) for kind in range(4)]
        (s0, s1), (g0, g1), (qs0, qs1), (qg0, qg1) = [
            (jnp.where(is0, mine, other), jnp.where(is0, other, mine)) for mine, other in states
        ]
        state = jnp.zeros((HALF, LANES), F32)
        for k in range(chips - 1, 0, -1):
            new = state * factors[k][:, column] + message_refs[k - 1][:, head(h)].astype(F32)
            state = jnp.where(k <= chip, new, state)
        grad = jnp.zeros((HALF, LANES), F32)
        for k in range(1, chips):
            new = grad * factors[k][:, column] + message_refs[k - 1][:, head(h)].astype(F32)
            grad = jnp.where(k > chip, new, grad)
        h0, l1 = state, grad
        h1 = h0 * decay0[:, column] + s0
        l0 = l1 * decay1[:, column] + g1
        cross = h0 * (l0 * weight0[:, column] + qs0) + h1 * (l1 * weight1[:, column] + qs1)
        cross += l0 * qg0 + l1 * qg1
        total_ref[h : h + 1, :] += jnp.sum(cross, axis=0, keepdims=True)
        h0, h1, l0, l1 = (value.astype(BF16) for value in (h0, h1, l0, l1))
        own_ref[0, :, head(h)] = jnp.where(is0, h0, h1)
        own_ref[1, :, head(h)] = jnp.where(is0, l0, l1)
        give_ref[0, :, head(h)] = jnp.where(is0, h1, h0)
        give_ref[1, :, head(h)] = jnp.where(is0, l1, l0)


def block_attention(
    block, chosen, most, mask_ref, q_ref, g_ref, kv_ref, out_ref, dq_ref, acc_ref,
    slot_ref, k_ref, k_live_ref, v_ref, q_turned_ref, g_turned_ref, ds_ref, wb_ref,
):
    count = mask_ref.shape[0]
    scale = FACTOR * LOG2E
    lower, upper = slice(0, LANES), slice(LANES, 2 * LANES)
    own = slice(block * BLOCK, (block + 1) * BLOCK)
    at = slice(block * BLOCK, (block + 1) * BLOCK)
    row = lax.axis_index("seq") * (q_ref.shape[0] // BLOCK) + block
    slots = []
    for slot in range(most):
        slot_ref[slot] = row

    def note(j, seen):
        hit = mask_ref[row, j]

        @pl.when(hit == 1)
        def _():
            slot_ref[seen] = j

        return seen + hit

    allowed = lax.fori_loop(0, count, note, 0)
    for slot in range(most):
        index, live = slot_ref[slot], slot < allowed
        slots.append((index, live))
        source = pl.ds(pl.multiple_of(index * BLOCK, BLOCK), BLOCK)
        target = slice(slot * BLOCK, (slot + 1) * BLOCK)
        k_tile, v_tile = kv_ref[source, lower], kv_ref[source, upper]
        k_ref[target, :] = k_tile
        k_live_ref[target, :] = jnp.where(live, k_tile, jnp.zeros_like(k_tile))
        v_ref[target, lower] = jnp.where(live, v_tile, jnp.zeros_like(v_tile))
        v_ref[target, upper] = jnp.full((BLOCK, LANES), jnp.where(live, 1.0, 0.0), F32).astype(BF16)
    group = 2
    firsts = range(chosen[0], chosen[1], group)
    used = slice(chosen[0] * BLOCK, chosen[1] * BLOCK)

    def stacked(ref, first):
        return jnp.concatenate([ref[at, head(h)] for h in range(first, first + group)], axis=0)

    upcoming = dot(stacked(q_ref, chosen[0]), k_ref[...], 1, 1)
    for first in firsts:
        heads = range(first, first + group)
        rows = slice(first * BLOCK, (first + group) * BLOCK)
        q, g = stacked(q_ref, first), stacked(g_ref, first)
        scores = upcoming
        dprobs = dot(g, v_ref[:, lower], 1, 1)
        if first + group < chosen[1]:
            upcoming = dot(stacked(q_ref, first + group), k_ref[...], 1, 1)
        best = jnp.max(scores, axis=1, keepdims=True)
        weights = jnp.exp2((scores - best) * scale)
        wb_ref[rows, :] = weights.astype(BF16)
        both = dot(wb_ref[rows, :], v_ref[...], 1, 0)
        inverse = 1.0 / both[:, upper]
        out = both[:, lower] * inverse
        delta = jnp.sum(out * g.astype(F32), axis=1, keepdims=True)
        ds_ref[rows, :] = (weights * (dprobs - delta)).astype(BF16)
        dq = (dot(ds_ref[rows, :], k_live_ref[...], 1, 0) * (inverse * FACTOR)).astype(BF16)
        q_turned_ref[:, rows] = (q.astype(F32) * inverse).astype(BF16).T
        g_turned_ref[:, rows] = (g.astype(F32) * inverse).astype(BF16).T
        for place, h in enumerate(heads):
            part = slice(place * BLOCK, (place + 1) * BLOCK)
            out_ref[own, head(h)] = out[part]
            dq_ref[own, head(h)] = dq[part]
    dk = dot(q_turned_ref[:, used], ds_ref[used, :], 1, 0)
    dv = dot(g_turned_ref[:, used], wb_ref[used, :], 1, 0)
    for slot, (index, live) in enumerate(slots):
        source = slice(slot * BLOCK, (slot + 1) * BLOCK)

        @pl.when(live)
        def _():
            target = pl.ds(pl.multiple_of(index * BLOCK, BLOCK), BLOCK)
            acc_ref[lower, target] += dk[:, source]
            acc_ref[upper, target] += dv[:, source]


def first_attention_kernel(
    chips, most, mask_ref, q_ref, g_ref, stack_ref, other_stack_ref, _, out_ref, dq_ref, acc_ref, kv_ref, *scratch
):
    tokens = q_ref.shape[0]
    chip, core = chip_and_core()
    acc_ref[...] = jnp.zeros_like(acc_ref)
    for k in range(chips):
        for other, ref in enumerate((stack_ref, other_stack_ref)):
            source = 2 * lax.rem(chip + chips - k, chips) + lax.rem(core + other, 2)
            at = pl.ds(pl.multiple_of(source * tokens, tokens), tokens)
            kv_ref[at, :] = ref[k]
    shared = (most, mask_ref, q_ref, g_ref, kv_ref, out_ref, dq_ref, acc_ref, *scratch)
    block_attention(0, (0, QUERY_HEADS), *shared)
    block_attention(1, (0, EARLY_HEADS), *shared)


def second_attention_kernel(
    most, mask_ref, q_ref, g_ref, kv_ref, first_out_ref, first_dq_ref, first_acc_ref, _,
    out_ref, dq_ref, acc_ref, *scratch
):
    acc_ref[...] = first_acc_ref[...]
    early = EARLY_HEADS * HEAD_WIDTH
    dq_ref[:BLOCK, :] = first_dq_ref[:BLOCK, :]
    dq_ref[BLOCK:, :early] = first_dq_ref[BLOCK:, :early]
    out_ref[:BLOCK, :] = first_out_ref[:BLOCK, :]
    out_ref[BLOCK:, :early] = first_out_ref[BLOCK:, :early]
    shared = (most, mask_ref, q_ref, g_ref, kv_ref, out_ref, dq_ref, acc_ref, *scratch)
    block_attention(1, (EARLY_HEADS, QUERY_HEADS), *shared)


def share_kernel(chips, acc_ref, *refs):
    keep_ref, give_ref, sums_ref = refs[-3:]
    tokens = keep_ref.shape[1]
    _, core = chip_and_core()
    sums = refs[0][...]
    for ref in refs[1:-3]:
        sums += ref[...]
    sums_ref[...] = sums
    high = sums.astype(BF16)
    middle = (sums - high.astype(F32)).astype(BF16)
    low = (sums - high.astype(F32) - middle.astype(F32)).astype(BF16)
    give_ref[chips * tokens : chips * tokens + 16, :] = jnp.concatenate([high, middle], axis=1)
    give_ref[chips * tokens + 16 :, :] = jnp.concatenate([low, jnp.zeros_like(low)], axis=1)
    for k in range(chips):
        mine = pl.multiple_of((2 * k + core) * tokens, tokens)
        other = pl.multiple_of((2 * k + 1 - core) * tokens, tokens)
        rows = slice(k * tokens, (k + 1) * tokens)
        keep_ref[rows, :] = acc_ref[:, pl.ds(mine, tokens)].astype(BF16)
        give_ref[rows, :] = acc_ref[:, pl.ds(other, tokens)].astype(BF16)


def pair_sum_kernel(chips, keep_ref, recv_ref, sums_ref, *refs):
    farther_refs, (own_ref, total_ref), message_refs = (
        refs[: -chips - 1], refs[-chips - 1 : -chips + 1], refs[-chips + 1 :]
    )
    chip, _ = chip_and_core()
    rows = own_ref.shape[0]
    at = pl.ds(pl.multiple_of(chip * rows, rows), rows)
    own_ref[...] = keep_ref[at, :].astype(F32) + recv_ref[at, :].astype(F32)
    total = sums_ref[...] + whole_sums(recv_ref[chips * rows :, :])
    for ref in farther_refs:
        total += ref[...]
    total_ref[...] = total
    high = total.astype(BF16)
    middle = (total - high.astype(F32)).astype(BF16)
    low = (total - high.astype(F32) - middle.astype(F32)).astype(BF16)
    for k in range(1, chips):
        target = pl.ds(pl.multiple_of(lax.rem(chip + k, chips) * rows, rows), rows)
        both = keep_ref[target, :].astype(F32) + recv_ref[target, :].astype(F32)
        message_refs[k - 1][:rows, :] = both.astype(BF16)
        message_refs[k - 1][rows : rows + 16, :] = jnp.concatenate([high, middle], axis=1)
        message_refs[k - 1][rows + 16 :, :] = jnp.concatenate([low, jnp.zeros_like(low)], axis=1)


def whole_sums(tail):
    tail = tail.astype(F32)
    return tail[:16, :LANES] + tail[:16, LANES:] + tail[16:, :LANES]


def owner_sum_kernel(chips, tokens_all, own_ref, sums_ref, *refs):
    parts, (dk_ref, dv_ref, rate_ref, skip_ref) = refs[: chips - 1], refs[chips - 1 :]
    rows = own_ref.shape[0]
    total = own_ref[...]
    sums = sums_ref[...]
    for part in parts:
        total += part[:rows, :].astype(F32)
        sums += whole_sums(part[rows:, :])
    dk_ref[...] = (total[:LANES].T * FACTOR).astype(BF16)
    dv_ref[...] = total[LANES:].T.astype(BF16)
    ones = jnp.ones((8, LANES), F32)
    rate = dot(ones, sums[:HS], 1, 1, HIGH) * (1.0 / tokens_all)
    skip = dot(ones, sums[HS:], 1, 1, HIGH) * (1.0 / (tokens_all * P_SIZE))
    rate_ref[...] = rate[0:1, :]
    skip_ref[...] = skip[0:1, :]


def inner_kernel(
    x_ref, g_ref, b_ref, c_ref, step_ref, rate_ref, skip_ref,
    y_ref, dx_ref, db_ref, dc_ref, sums_ref,
    pad_ref, inner_ref, dinner_ref, m_ref, runt_ref,
):
    tokens = 2 * BLOCK
    flat0, flat1, run0, run1 = running_logs(step_ref, rate_ref, pad_ref)
    own = jnp.concatenate([run0, run1], axis=0)
    runt_ref[:, :BLOCK] = flat0
    runt_ref[:, tokens : tokens + BLOCK] = flat0 - flat0[:, BLOCK - 1 :]
    runt_ref[:, tokens + BLOCK :] = flat1
    b = b_ref[...]
    c = c_ref[...]
    inner_ref[...] = dot(c, b, 1, 1)
    dinner_ref[...] = jnp.zeros_like(dinner_ref)
    row0 = lax.broadcasted_iota(jnp.int32, (BLOCK, BLOCK), 0)
    col0 = lax.broadcasted_iota(jnp.int32, (BLOCK, BLOCK), 1)
    row1 = lax.broadcasted_iota(jnp.int32, (BLOCK, tokens), 0)
    col1 = lax.broadcasted_iota(jnp.int32, (BLOCK, tokens), 1)
    seen0 = row0 >= col0
    seen1 = row1 + BLOCK >= col1
    m_ref[:BLOCK, BLOCK:] = jnp.zeros((BLOCK, BLOCK), BF16)
    for h in range(HS):
        lanes = head(h)
        x = x_ref[:, lanes]
        g = g_ref[:, lanes]
        xf, gf = x.astype(F32), g.astype(F32)
        gain = skip_ref[h]
        spread0 = jnp.where(seen0, own[:BLOCK, h : h + 1] - runt_ref[h : h + 1, :BLOCK], NEG)
        spread1 = jnp.where(seen1, own[BLOCK:, h : h + 1] - runt_ref[h : h + 1, tokens:], NEG)
        decay0, decay1 = jnp.exp(spread0), jnp.exp(spread1)
        dm = dot(g, x, 1, 1)
        e0, e1 = decay0 * dm[:BLOCK, :BLOCK], decay1 * dm[BLOCK:, :]
        m_ref[:BLOCK, :BLOCK] = (decay0 * inner_ref[:BLOCK, :BLOCK]).astype(BF16)
        m_ref[BLOCK:, :] = (decay1 * inner_ref[BLOCK:, :]).astype(BF16)
        dinner_ref[:BLOCK, :BLOCK] += e0
        dinner_ref[BLOCK:, :] += e1
        w0 = jnp.sum(spread0 * (e0 * inner_ref[:BLOCK, :BLOCK]), axis=0, keepdims=True)
        w1 = jnp.sum(spread1 * (e1 * inner_ref[BLOCK:, :]), axis=0, keepdims=True)
        m = m_ref[...]
        y_ref[:, lanes] = dot(m, x, 1, 0) + gain * xf
        dx_ref[:, lanes] = dot(m, g, 0, 0) + gain * gf
        sums_ref[h : h + 1, :] = w0 + w1[:, :BLOCK] + w1[:, BLOCK:]
        sums_ref[HS + h : HS + h + 1, :] = jnp.sum(gf * xf, axis=0, keepdims=True)
    dinner = dinner_ref[...].astype(BF16)
    dc_ref[...] = dot(dinner, b, 1, 0)
    db_ref[...] = dot(dinner, c, 0, 0)


def chunk_kernel(
    x_ref, g_ref, b_ref, c_ref, step_ref, rate_ref, skip_ref,
    state_ref, y_ref, dx_ref, db_ref, dc_ref, sums_ref, pad_ref, *scratch
):
    operands = (x_ref, g_ref, b_ref, c_ref, step_ref, rate_ref)
    local_states_kernel(*operands, state_ref, pad_ref, *scratch[:3])
    inner_kernel(*operands, skip_ref, y_ref, dx_ref, db_ref, dc_ref, sums_ref, pad_ref, *scratch[3:])


def outer_kernel(
    x_ref, g_ref, b_ref, c_ref, step_ref, rate_ref, own_ref, other_ref, att_ref,
    inner_y_ref, inner_dx_ref, inner_db_ref, inner_dc_ref, _,
    y_ref, dx_ref, db_ref, dc_ref,
    pad_ref, xt_ref, gt_ref, ent_ref,
):
    _, core = chip_and_core()
    ent_ref[:, pl.ds(pl.multiple_of(core * HALF, HALF), HALF), :] = own_ref[...]
    ent_ref[:, pl.ds(pl.multiple_of((1 - core) * HALF, HALF), HALF), :] = other_ref[...]
    _, _, run0, run1 = running_logs(step_ref, rate_ref, pad_ref)
    enter_log, tail_log, _ = enter_and_tail(run0, run1)
    enter, tail = jnp.exp(enter_log), jnp.exp(tail_log)
    scaled(x_ref, tail, xt_ref)
    scaled(g_ref, enter, gt_ref)
    b = b_ref[...]
    c = c_ref[...]
    for h in range(HS):
        lanes = head(h)
        carried = dot(c, ent_ref[0, :, lanes], 1, 0) * enter[:, h : h + 1]
        back = dot(b, ent_ref[1, :, lanes], 1, 0) * tail[:, h : h + 1]
        y_ref[:, lanes] = (inner_y_ref[:, lanes] + carried + att_ref[:, lanes]).astype(BF16)
        dx_ref[:, lanes] = (inner_dx_ref[:, lanes] + back).astype(BF16)
    dc_ref[...] = (inner_dc_ref[...] + dot(gt_ref[...], ent_ref[0], 1, 1)).astype(BF16)
    db_ref[...] = (inner_db_ref[...] + dot(xt_ref[...], ent_ref[1], 1, 1)).astype(BF16)


def swapped(array):
    return lax.ppermute(array, "seq", [(i, i ^ 1) for i in range(lax.axis_size("seq"))])


def from_chip(array, k):
    n = lax.axis_size("seq")
    return lax.ppermute(array, "seq", [(i, (i + 2 * k) % n) for i in range(n)])


def from_replica(array, distance, flip):
    replicas, n = lax.axis_size("dp"), lax.axis_size("seq")
    pairs = [
        (r * n + i, (r ^ distance) * n + (i ^ flip)) for r in range(replicas) for i in range(n)
    ]
    return lax.ppermute(array, ("dp", "seq"), pairs)


def call(kernel, outs, ins, scratch, microseconds, name, limit=16):
    return pl.pallas_call(
        kernel,
        out_shape=tuple(jax.ShapeDtypeStruct(*out) for out in outs),
        in_specs=ins,
        out_specs=(VMEM,) * len(outs),
        scratch_shapes=scratch,
        compiler_params=pltpu.CompilerParams(vmem_limit_bytes=limit << 20),
        cost_estimate=cost(microseconds),
        name=name,
    )


def body(query, key, value, ssm_input, in_b, in_c, step, rate_log, skip, block_mask, grad_out):
    n = lax.axis_size("seq")
    chips = n // 2
    replicas = lax.axis_size("dp")
    tokens = query.shape[1]
    blocks = block_mask.shape[1]
    most = 3 * blocks // 8
    every = blocks * BLOCK
    q, g, x = query[0], grad_out[0], ssm_input[0]
    b, c, steps = in_b[0], in_c[0], step[0].T

    (kv,) = call(
        pack_kernel,
        [((tokens, 2 * LANES), BF16)],
        [AFTER] * 2,
        [pltpu.SemaphoreType.DMA((2,))],
        1,
        "pack_kv",
        60,
    )(key[0], value[0])
    kv_parts = [kv] + [from_chip(kv, k) for k in range(1, chips)]

    states, inner_y, inner_dx, inner_db, inner_dc, sums = call(
        chunk_kernel,
        [((4, NS, WIDE + LANES), F32)]
        + [((tokens, WIDE), F32)] * 2
        + [((tokens, NS), F32)] * 2
        + [((2 * HS, LANES), F32)],
        [VMEM] * 5 + [SMEM] * 2,
        [
            pltpu.VMEM((LANES, tokens), F32),
            pltpu.VMEM((tokens, WIDE), BF16),
            pltpu.VMEM((tokens, WIDE), BF16),
            pltpu.VMEM((tokens, WIDE), BF16),
            pltpu.VMEM((tokens, tokens), F32),
            pltpu.VMEM((tokens, tokens), F32),
            pltpu.VMEM((tokens, tokens), BF16),
            pltpu.VMEM((LANES, 2 * tokens), F32),
        ],
        6,
        "chunk_alone",
        20,
    )(x, g, b, c, steps, rate_log, skip)
    half = ((4, HALF, WIDE + LANES), F32)
    keep, give, stack = call(
        split_kernel,
        [half, half, ((chips, tokens, 2 * LANES), BF16)],
        [VMEM] * (1 + chips),
        [],
        1,
        "split_states",
    )(states, *kv_parts)
    received = swapped(give)
    other_stack = swapped(stack)

    messages = call(
        lambda *refs: combine_kernel(chips, *refs),
        [((HALF, WIDE + LANES), BF16)] * (chips - 1),
        [VMEM] * 2 + [AFTER],
        [],
        1,
        "combine_states",
    )(keep, received, sums)
    arrived = [from_chip(messages[k - 1], k) for k in range(1, chips)]

    columns = QUERY_HEADS * BLOCK
    scratch = [
        pltpu.SMEM((most,), jnp.int32),
        pltpu.VMEM((most * BLOCK, LANES), BF16),
        pltpu.VMEM((most * BLOCK, LANES), BF16),
        pltpu.VMEM((most * BLOCK, 2 * LANES), BF16),
        pltpu.VMEM((LANES, columns), BF16),
        pltpu.VMEM((LANES, columns), BF16),
        pltpu.VMEM((columns, most * BLOCK), BF16),
        pltpu.VMEM((columns, most * BLOCK), BF16),
    ]
    first_out, first_dq, first_acc, kv_all = call(
        lambda *refs: first_attention_kernel(chips, most, *refs),
        [
            ((tokens, columns), F32),
            ((tokens, columns), BF16),
            ((2 * LANES, every), F32),
            ((every, 2 * LANES), BF16),
        ],
        [SMEM] + [VMEM] * 4 + [AFTER],
        scratch,
        5,
        "first_attention",
        18 + most,
    )(block_mask[0], q, g, stack, other_stack, messages[0])
    entering = ((2, HALF, WIDE), BF16)
    own, give, totals = call(
        lambda *refs: chain_kernel(chips, *refs),
        [entering, entering, ((2 * HS, LANES), F32)],
        [VMEM] * 3 + [AFTER] + [VMEM] * (chips - 1),
        [],
        2,
        "chain_states",
    )(keep, received, sums, first_dq, *arrived)
    other = swapped(give)
    neighbour = from_replica(totals, 1, 0)

    attention, dq, acc = call(
        lambda *refs: second_attention_kernel(most, *refs),
        [((tokens, columns), F32), ((tokens, columns), BF16), ((2 * LANES, every), F32)],
        [SMEM] + [VMEM] * 6 + [AFTER],
        scratch,
        5,
        "second_attention",
        18 + most,
    )(block_mask[0], q, g, kv_all, first_out, first_dq, first_acc, totals)
    keep, give, sums = call(
        lambda *refs: share_kernel(chips, *refs),
        [
            ((chips * 2 * LANES, tokens), BF16),
            ((chips * 2 * LANES + 32, tokens), BF16),
            ((2 * HS, LANES), F32),
        ],
        [VMEM] * 3,
        [],
        1,
        "share_key_gradients",
    )(acc, totals, neighbour)
    farther = [from_replica(sums, d, flip) for d in range(2, replicas, 2) for flip in (0, 1)]
    partial, summed, *messages = call(
        lambda *refs: pair_sum_kernel(chips, *refs),
        [((2 * LANES, tokens), F32), ((2 * HS, LANES), F32)]
        + [((2 * LANES + 32, tokens), BF16)] * (chips - 1),
        [VMEM] * (3 + len(farther)),
        [],
        1,
        "pair_sum",
    )(keep, swapped(give), sums, *farther)
    arrived = [from_chip(messages[k - 1], k) for k in range(1, chips)]

    y, dx, db, dc = call(
        outer_kernel,
        [((tokens, WIDE), BF16)] * 2 + [((tokens, NS), BF16)] * 2,
        [VMEM] * 5 + [SMEM] + [VMEM] * 7 + [AFTER],
        [
            pltpu.VMEM((LANES, tokens), F32),
            pltpu.VMEM((tokens, WIDE), BF16),
            pltpu.VMEM((tokens, WIDE), BF16),
            pltpu.VMEM((2, NS, WIDE), BF16),
        ],
        3,
        "chunk_outer",
    )(
        x, g, b, c, steps, rate_log, own, other, attention,
        inner_y, inner_dx, inner_db, inner_dc, messages[0],
    )

    tokens_all = replicas * n * tokens
    dk, dv, grad_rate_log, grad_skip = call(
        lambda *refs: owner_sum_kernel(chips, tokens_all, *refs),
        [((tokens, LANES), BF16)] * 2 + [((1, HS), F32)] * 2,
        [VMEM] * (chips + 1),
        [],
        1,
        "owner_sum",
    )(partial, summed, *arrived)
    return (
        y[None],
        dq[None],
        dk[None],
        dv[None],
        dx[None],
        db[None],
        dc[None],
        grad_rate_log.reshape(HS),
        grad_skip.reshape(HS),
    )


def solution(mesh):
    split = P("dp", "seq", None)
    in_specs = (split,) * 7 + (P(), P(), P("dp", None, None), split)
    out_specs = (split,) * 7 + (P(), P())
    return jax.shard_map(body, mesh=mesh, in_specs=in_specs, out_specs=out_specs, check_vma=False)
```

```python
import jax
import jax.numpy as jnp
from jax import lax
from jax.experimental import pallas as pl
from jax.experimental.pallas import tpu as pltpu
from jax.sharding import PartitionSpec as P

HEAD_WIDTH = 128
QUERY_HEADS = 8
HS = 8
P_SIZE = 128
NS = 128
BLOCK = 128
WIDE = HS * P_SIZE
LANES = 128
FACTOR = HEAD_WIDTH ** (-0.5)
LOG2E = 1.4426950408889634
NEG = -1e30
HALF = NS // 2
HIGH = lax.Precision.HIGHEST
F32 = jnp.float32
BF16 = jnp.bfloat16

VMEM = pl.BlockSpec(memory_space=pltpu.VMEM)
SMEM = pl.BlockSpec(memory_space=pltpu.SMEM)
AFTER = pl.BlockSpec(memory_space=pl.ANY)


def cost(microseconds):
    return pl.CostEstimate(
        flops=int(microseconds * 1.1e9), bytes_accessed=1 << 20, transcendentals=0
    )


def dot(a, b, ca, cb, precision=None):
    return lax.dot_general(
        a, b, (((ca,), (cb,)), ((), ())), preferred_element_type=F32, precision=precision
    )


def head(h):
    return slice(h * LANES, (h + 1) * LANES)


def running_logs(step_ref, rate_ref, pad_ref):
    pad_ref[...] = jnp.zeros_like(pad_ref)
    for h in range(HS):
        rate = jnp.exp(jnp.full((1, 2 * BLOCK), rate_ref[h], F32))
        pad_ref[h : h + 1, :] = -step_ref[h : h + 1, :] * rate
    row = lax.broadcasted_iota(jnp.int32, (BLOCK, BLOCK), 0)
    col = lax.broadcasted_iota(jnp.int32, (BLOCK, BLOCK), 1)
    upper = jnp.where(row <= col, 1.0, 0.0).astype(F32)
    flat0 = dot(pad_ref[:, :BLOCK], upper, 1, 0, HIGH)
    flat1 = dot(pad_ref[:, BLOCK:], upper, 1, 0, HIGH)
    return flat0, flat1, flat0.T, flat1.T


def scaled(x_ref, column, out_ref):
    for h in range(HS):
        out_ref[:, head(h)] = (x_ref[:, head(h)].astype(F32) * column[:, h : h + 1]).astype(BF16)


def chip_and_core():
    me = lax.axis_index("seq")
    return me // 2, me % 2


def fetch(pairs, sems):
    copies = [
        pltpu.make_async_copy(source, target, sems.at[i]) for i, (source, target) in enumerate(pairs)
    ]
    for copy in copies:
        copy.start()
    return copies


def pack_kernel(key_ref, value_ref, out_ref, sems):
    pairs = [(key_ref, out_ref.at[:, :LANES]), (value_ref, out_ref.at[:, LANES:])]
    for copy in fetch(pairs, sems):
        copy.wait()


def split_kernel(states_ref, *refs):
    keep_ref, give_ref, stack_ref = refs[-3:]
    _, core = chip_and_core()
    keep_ref[...] = states_ref[:, pl.ds(pl.multiple_of(core * HALF, HALF), HALF), :]
    give_ref[...] = states_ref[:, pl.ds(pl.multiple_of((1 - core) * HALF, HALF), HALF), :]
    for k, ref in enumerate(refs[:-3]):
        stack_ref[k] = ref[...]


def enter_and_tail(run0, run1):
    t0, t1 = run0[BLOCK - 1 :, :], run1[BLOCK - 1 :, :]
    enter = jnp.concatenate([run0, run1 + t0], axis=0)
    tail = jnp.concatenate([(t0 - run0) + t1, t1 - run1], axis=0)
    return enter, tail, t0 + t1


def local_states_kernel(
    x_ref, g_ref, b_ref, c_ref, step_ref, rate_ref, state_ref, pad_ref, high_ref, rest_ref, log_ref
):
    _, _, run0, run1 = running_logs(step_ref, rate_ref, pad_ref)
    enter_log, tail_log, total = enter_and_tail(run0, run1)
    enter, tail = jnp.exp(enter_log), jnp.exp(tail_log)
    state_ref[:, :, WIDE:] = jnp.broadcast_to(total, (4, NS, LANES))
    cases = ((b_ref, x_ref, tail, tail_log), (c_ref, g_ref, enter, enter_log))
    for direction, (left, right, factor, weight) in enumerate(cases):
        for h in range(HS):
            product = right[:, head(h)].astype(F32) * factor[:, h : h + 1]
            rounded = product.astype(BF16)
            high_ref[:, head(h)] = rounded
            rest_ref[:, head(h)] = (product - rounded.astype(F32)).astype(BF16)
            log_ref[:, head(h)] = (product * weight[:, h : h + 1]).astype(BF16)
        turned_left = left[...].astype(F32).T.astype(BF16)
        state_ref[direction, :, :WIDE] = dot(turned_left, high_ref[...], 1, 0) + dot(
            turned_left, rest_ref[...], 1, 0
        )
        state_ref[3 - direction, :, :WIDE] = dot(turned_left, log_ref[...], 1, 0)


def three_parts(value, rows):
    high = value.astype(BF16).astype(F32)
    middle = (value - high).astype(BF16).astype(F32)
    low = value - high - middle
    index = lax.broadcasted_iota(jnp.int32, (rows, LANES), 0)
    return jnp.where(index == 0, high, jnp.where(index == 1, middle, low)).astype(BF16)


def pair_logs(keep_ref, recv_ref, is0):
    mine, other = keep_ref[0, 0:1, WIDE:], recv_ref[0, 0:1, WIDE:]
    return jnp.where(is0, mine, other), jnp.where(is0, other, mine)


def combine_kernel(chips, keep_ref, recv_ref, _, *message_refs):
    chip, core = chip_and_core()
    is0 = core == 0
    log0, log1 = pair_logs(keep_ref, recv_ref, is0)
    logs = three_parts(log0 + log1, HALF)
    decay0, decay1 = jnp.exp(log0), jnp.exp(log1)
    for h in range(HS):
        mine, other = keep_ref[0, :, head(h)], recv_ref[0, :, head(h)]
        first, second = jnp.where(is0, mine, other), jnp.where(is0, other, mine)
        state = (first * decay1[:, h : h + 1] + second).astype(BF16)
        mine, other = keep_ref[1, :, head(h)], recv_ref[1, :, head(h)]
        first, second = jnp.where(is0, mine, other), jnp.where(is0, other, mine)
        grad = (second * decay0[:, h : h + 1] + first).astype(BF16)
        for k in range(1, chips):
            later = chip + k < chips
            message_refs[k - 1][:, head(h)] = jnp.where(later, state, grad)
    for k in range(1, chips):
        message_refs[k - 1][:, WIDE:] = logs


def chain_kernel(chips, keep_ref, recv_ref, sums_ref, _, *refs):
    message_refs = refs[: chips - 1]
    own_ref, give_ref, total_ref = refs[chips - 1 :]
    chip, core = chip_and_core()
    is0 = core == 0
    log0, log1 = pair_logs(keep_ref, recv_ref, is0)
    decay0, decay1 = jnp.exp(log0), jnp.exp(log1)
    weight0, weight1 = log0 * decay0, log1 * decay1
    factors = [None]
    for ref in message_refs:
        parts = ref[:16, WIDE:].astype(F32)
        factors.append(jnp.exp(parts[0:1, :] + parts[1:2, :] + parts[2:3, :]))
    total_ref[...] = sums_ref[...]
    for h in range(HS):
        column = slice(h, h + 1)
        states = [(keep_ref[kind, :, head(h)], recv_ref[kind, :, head(h)]) for kind in range(4)]
        (s0, s1), (g0, g1), (qs0, qs1), (qg0, qg1) = [
            (jnp.where(is0, mine, other), jnp.where(is0, other, mine)) for mine, other in states
        ]
        state = jnp.zeros((HALF, LANES), F32)
        for k in range(chips - 1, 0, -1):
            new = state * factors[k][:, column] + message_refs[k - 1][:, head(h)].astype(F32)
            state = jnp.where(k <= chip, new, state)
        grad = jnp.zeros((HALF, LANES), F32)
        for k in range(1, chips):
            new = grad * factors[k][:, column] + message_refs[k - 1][:, head(h)].astype(F32)
            grad = jnp.where(k > chip, new, grad)
        h0, l1 = state, grad
        h1 = h0 * decay0[:, column] + s0
        l0 = l1 * decay1[:, column] + g1
        cross = h0 * (l0 * weight0[:, column] + qs0) + h1 * (l1 * weight1[:, column] + qs1)
        cross += l0 * qg0 + l1 * qg1
        total_ref[h : h + 1, :] += jnp.sum(cross, axis=0, keepdims=True)
        h0, h1, l0, l1 = (value.astype(BF16) for value in (h0, h1, l0, l1))
        own_ref[0, :, head(h)] = jnp.where(is0, h0, h1)
        own_ref[1, :, head(h)] = jnp.where(is0, l0, l1)
        give_ref[0, :, head(h)] = jnp.where(is0, h1, h0)
        give_ref[1, :, head(h)] = jnp.where(is0, l1, l0)


def block_attention(
    block, most, mask_ref, q_ref, g_ref, kv_ref, out_ref, dq_ref, acc_ref,
    slot_ref, k_ref, k_live_ref, v_ref, q_turned_ref, g_turned_ref, ds_ref, wb_ref,
):
    count = mask_ref.shape[0]
    scale = FACTOR * LOG2E
    lower, upper = slice(0, LANES), slice(LANES, 2 * LANES)
    own = slice(block * BLOCK, (block + 1) * BLOCK)
    at = slice(block * BLOCK, (block + 1) * BLOCK)
    row = lax.axis_index("seq") * (q_ref.shape[0] // BLOCK) + block
    slots = []
    for slot in range(most):
        slot_ref[slot] = row

    def note(j, seen):
        hit = mask_ref[row, j]

        @pl.when(hit == 1)
        def _():
            slot_ref[seen] = j

        return seen + hit

    allowed = lax.fori_loop(0, count, note, 0)
    for slot in range(most):
        index, live = slot_ref[slot], slot < allowed
        slots.append((index, live))
        source = pl.ds(pl.multiple_of(index * BLOCK, BLOCK), BLOCK)
        target = slice(slot * BLOCK, (slot + 1) * BLOCK)
        k_tile, v_tile = kv_ref[source, lower], kv_ref[source, upper]
        k_ref[target, :] = k_tile
        k_live_ref[target, :] = jnp.where(live, k_tile, jnp.zeros_like(k_tile))
        v_ref[target, lower] = jnp.where(live, v_tile, jnp.zeros_like(v_tile))
        v_ref[target, upper] = jnp.full((BLOCK, LANES), jnp.where(live, 1.0, 0.0), F32).astype(BF16)
    group = 2
    firsts = range(0, QUERY_HEADS, group)

    def stacked(ref, first):
        return jnp.concatenate([ref[at, head(h)] for h in range(first, first + group)], axis=0)

    upcoming = dot(stacked(q_ref, 0), k_ref[...], 1, 1)
    for first in firsts:
        heads = range(first, first + group)
        rows = slice(first * BLOCK, (first + group) * BLOCK)
        q, g = stacked(q_ref, first), stacked(g_ref, first)
        scores = upcoming
        dprobs = dot(g, v_ref[:, lower], 1, 1)
        if first + group < QUERY_HEADS:
            upcoming = dot(stacked(q_ref, first + group), k_ref[...], 1, 1)
        best = jnp.max(scores, axis=1, keepdims=True)
        weights = jnp.exp2((scores - best) * scale)
        wb_ref[rows, :] = weights.astype(BF16)
        both = dot(wb_ref[rows, :], v_ref[...], 1, 0)
        inverse = 1.0 / both[:, upper]
        out = both[:, lower] * inverse
        delta = jnp.sum(out * g.astype(F32), axis=1, keepdims=True)
        ds_ref[rows, :] = (weights * (dprobs - delta)).astype(BF16)
        dq = (dot(ds_ref[rows, :], k_live_ref[...], 1, 0) * (inverse * FACTOR)).astype(BF16)
        q_turned_ref[:, rows] = (q.astype(F32) * inverse).astype(BF16).T
        g_turned_ref[:, rows] = (g.astype(F32) * inverse).astype(BF16).T
        for place, h in enumerate(heads):
            part = slice(place * BLOCK, (place + 1) * BLOCK)
            out_ref[:, head(h)] = out[part]
            dq_ref[own, head(h)] = dq[part]
    dk = dot(q_turned_ref[...], ds_ref[...], 1, 0)
    dv = dot(g_turned_ref[...], wb_ref[...], 1, 0)
    for slot, (index, live) in enumerate(slots):
        source = slice(slot * BLOCK, (slot + 1) * BLOCK)

        @pl.when(live)
        def _():
            target = pl.ds(pl.multiple_of(index * BLOCK, BLOCK), BLOCK)
            acc_ref[lower, target] += dk[:, source]
            acc_ref[upper, target] += dv[:, source]


def first_attention_kernel(
    chips, most, mask_ref, q_ref, g_ref, stack_ref, other_stack_ref, _, out_ref, dq_ref, acc_ref, kv_ref, *scratch
):
    tokens = q_ref.shape[0]
    chip, core = chip_and_core()
    acc_ref[...] = jnp.zeros_like(acc_ref)
    for k in range(chips):
        for other, ref in enumerate((stack_ref, other_stack_ref)):
            source = 2 * lax.rem(chip + chips - k, chips) + lax.rem(core + other, 2)
            at = pl.ds(pl.multiple_of(source * tokens, tokens), tokens)
            kv_ref[at, :] = ref[k]
    block_attention(0, most, mask_ref, q_ref, g_ref, kv_ref, out_ref, dq_ref, acc_ref, *scratch)


def second_attention_kernel(
    most, mask_ref, q_ref, g_ref, kv_ref, first_dq_ref, first_acc_ref, _, out_ref, dq_ref, acc_ref, *scratch
):
    acc_ref[...] = first_acc_ref[...]
    dq_ref[:BLOCK, :] = first_dq_ref[...]
    block_attention(1, most, mask_ref, q_ref, g_ref, kv_ref, out_ref, dq_ref, acc_ref, *scratch)


def share_kernel(chips, acc_ref, *refs):
    keep_ref, give_ref, sums_ref = refs[-3:]
    tokens = keep_ref.shape[1]
    _, core = chip_and_core()
    sums = refs[0][...]
    for ref in refs[1:-3]:
        sums += ref[...]
    sums_ref[...] = sums
    high = sums.astype(BF16)
    middle = (sums - high.astype(F32)).astype(BF16)
    low = (sums - high.astype(F32) - middle.astype(F32)).astype(BF16)
    give_ref[chips * tokens : chips * tokens + 16, :] = jnp.concatenate([high, middle], axis=1)
    give_ref[chips * tokens + 16 :, :] = jnp.concatenate([low, jnp.zeros_like(low)], axis=1)
    for k in range(chips):
        mine = pl.multiple_of((2 * k + core) * tokens, tokens)
        other = pl.multiple_of((2 * k + 1 - core) * tokens, tokens)
        rows = slice(k * tokens, (k + 1) * tokens)
        keep_ref[rows, :] = acc_ref[:, pl.ds(mine, tokens)].astype(BF16)
        give_ref[rows, :] = acc_ref[:, pl.ds(other, tokens)].astype(BF16)


def pair_sum_kernel(chips, keep_ref, recv_ref, sums_ref, own_ref, total_ref, *message_refs):
    chip, _ = chip_and_core()
    rows = own_ref.shape[0]
    at = pl.ds(pl.multiple_of(chip * rows, rows), rows)
    own_ref[...] = keep_ref[at, :].astype(F32) + recv_ref[at, :].astype(F32)
    total = sums_ref[...] + whole_sums(recv_ref[chips * rows :, :])
    total_ref[...] = total
    high = total.astype(BF16)
    middle = (total - high.astype(F32)).astype(BF16)
    low = (total - high.astype(F32) - middle.astype(F32)).astype(BF16)
    for k in range(1, chips):
        target = pl.ds(pl.multiple_of(lax.rem(chip + k, chips) * rows, rows), rows)
        both = keep_ref[target, :].astype(F32) + recv_ref[target, :].astype(F32)
        message_refs[k - 1][:rows, :] = both.astype(BF16)
        message_refs[k - 1][rows : rows + 16, :] = jnp.concatenate([high, middle], axis=1)
        message_refs[k - 1][rows + 16 :, :] = jnp.concatenate([low, jnp.zeros_like(low)], axis=1)


def whole_sums(tail):
    tail = tail.astype(F32)
    return tail[:16, :LANES] + tail[:16, LANES:] + tail[16:, :LANES]


def owner_sum_kernel(chips, tokens_all, own_ref, sums_ref, *refs):
    parts, farther_refs, (dk_ref, dv_ref, rate_ref, skip_ref) = (
        refs[: chips - 1], refs[chips - 1 : -4], refs[-4:]
    )
    rows = own_ref.shape[0]
    total = own_ref[...]
    sums = sums_ref[...]
    for part in parts:
        total += part[:rows, :].astype(F32)
        sums += whole_sums(part[rows:, :])
    for ref in farther_refs:
        sums += ref[...]
    dk_ref[...] = (total[:LANES].T * FACTOR).astype(BF16)
    dv_ref[...] = total[LANES:].T.astype(BF16)
    ones = jnp.ones((8, LANES), F32)
    rate = dot(ones, sums[:HS], 1, 1, HIGH) * (1.0 / tokens_all)
    skip = dot(ones, sums[HS:], 1, 1, HIGH) * (1.0 / (tokens_all * P_SIZE))
    rate_ref[...] = rate[0:1, :]
    skip_ref[...] = skip[0:1, :]


def inner_kernel(
    x_ref, g_ref, b_ref, c_ref, step_ref, rate_ref, skip_ref,
    y_ref, dx_ref, db_ref, dc_ref, sums_ref,
    pad_ref, inner_ref, dinner_ref, m_ref, runt_ref,
):
    tokens = 2 * BLOCK
    flat0, flat1, run0, run1 = running_logs(step_ref, rate_ref, pad_ref)
    own = jnp.concatenate([run0, run1], axis=0)
    runt_ref[:, :BLOCK] = flat0
    runt_ref[:, tokens : tokens + BLOCK] = flat0 - flat0[:, BLOCK - 1 :]
    runt_ref[:, tokens + BLOCK :] = flat1
    b = b_ref[...]
    c = c_ref[...]
    inner_ref[...] = dot(c, b, 1, 1)
    dinner_ref[...] = jnp.zeros_like(dinner_ref)
    row0 = lax.broadcasted_iota(jnp.int32, (BLOCK, BLOCK), 0)
    col0 = lax.broadcasted_iota(jnp.int32, (BLOCK, BLOCK), 1)
    row1 = lax.broadcasted_iota(jnp.int32, (BLOCK, tokens), 0)
    col1 = lax.broadcasted_iota(jnp.int32, (BLOCK, tokens), 1)
    seen0 = row0 >= col0
    seen1 = row1 + BLOCK >= col1
    m_ref[:BLOCK, BLOCK:] = jnp.zeros((BLOCK, BLOCK), BF16)
    for h in range(HS):
        lanes = head(h)
        x = x_ref[:, lanes]
        g = g_ref[:, lanes]
        xf, gf = x.astype(F32), g.astype(F32)
        gain = skip_ref[h]
        spread0 = jnp.where(seen0, own[:BLOCK, h : h + 1] - runt_ref[h : h + 1, :BLOCK], NEG)
        spread1 = jnp.where(seen1, own[BLOCK:, h : h + 1] - runt_ref[h : h + 1, tokens:], NEG)
        decay0, decay1 = jnp.exp(spread0), jnp.exp(spread1)
        dm = dot(g, x, 1, 1)
        e0, e1 = decay0 * dm[:BLOCK, :BLOCK], decay1 * dm[BLOCK:, :]
        m_ref[:BLOCK, :BLOCK] = (decay0 * inner_ref[:BLOCK, :BLOCK]).astype(BF16)
        m_ref[BLOCK:, :] = (decay1 * inner_ref[BLOCK:, :]).astype(BF16)
        dinner_ref[:BLOCK, :BLOCK] += e0
        dinner_ref[BLOCK:, :] += e1
        w0 = jnp.sum(spread0 * (e0 * inner_ref[:BLOCK, :BLOCK]), axis=0, keepdims=True)
        w1 = jnp.sum(spread1 * (e1 * inner_ref[BLOCK:, :]), axis=0, keepdims=True)
        m = m_ref[...]
        y_ref[:, lanes] = dot(m, x, 1, 0) + gain * xf
        dx_ref[:, lanes] = dot(m, g, 0, 0) + gain * gf
        sums_ref[h : h + 1, :] = w0 + w1[:, :BLOCK] + w1[:, BLOCK:]
        sums_ref[HS + h : HS + h + 1, :] = jnp.sum(gf * xf, axis=0, keepdims=True)
    dinner = dinner_ref[...].astype(BF16)
    dc_ref[...] = dot(dinner, b, 1, 0)
    db_ref[...] = dot(dinner, c, 0, 0)


def chunk_kernel(
    x_ref, g_ref, b_ref, c_ref, step_ref, rate_ref, skip_ref,
    state_ref, y_ref, dx_ref, db_ref, dc_ref, sums_ref, pad_ref, *scratch
):
    operands = (x_ref, g_ref, b_ref, c_ref, step_ref, rate_ref)
    local_states_kernel(*operands, state_ref, pad_ref, *scratch[:3])
    inner_kernel(*operands, skip_ref, y_ref, dx_ref, db_ref, dc_ref, sums_ref, pad_ref, *scratch[3:])


def outer_kernel(
    x_ref, g_ref, b_ref, c_ref, step_ref, rate_ref, own_ref, other_ref, first_ref, second_ref,
    inner_y_ref, inner_dx_ref, inner_db_ref, inner_dc_ref, sums_ref,
    y_ref, dx_ref, db_ref, dc_ref, passed_ref,
    pad_ref, xt_ref, gt_ref, ent_ref,
):
    passed_ref[...] = sums_ref[...]
    _, core = chip_and_core()
    ent_ref[:, pl.ds(pl.multiple_of(core * HALF, HALF), HALF), :] = own_ref[...]
    ent_ref[:, pl.ds(pl.multiple_of((1 - core) * HALF, HALF), HALF), :] = other_ref[...]
    _, _, run0, run1 = running_logs(step_ref, rate_ref, pad_ref)
    enter_log, tail_log, _ = enter_and_tail(run0, run1)
    enter, tail = jnp.exp(enter_log), jnp.exp(tail_log)
    scaled(x_ref, tail, xt_ref)
    scaled(g_ref, enter, gt_ref)
    b = b_ref[...]
    c = c_ref[...]
    for h in range(HS):
        lanes = head(h)
        carried = dot(c, ent_ref[0, :, lanes], 1, 0) * enter[:, h : h + 1]
        back = dot(b, ent_ref[1, :, lanes], 1, 0) * tail[:, h : h + 1]
        y = inner_y_ref[:, lanes] + carried
        y_ref[:BLOCK, lanes] = (y[:BLOCK] + first_ref[:, lanes]).astype(BF16)
        y_ref[BLOCK:, lanes] = (y[BLOCK:] + second_ref[:, lanes]).astype(BF16)
        dx_ref[:, lanes] = (inner_dx_ref[:, lanes] + back).astype(BF16)
    dc_ref[...] = (inner_dc_ref[...] + dot(gt_ref[...], ent_ref[0], 1, 1)).astype(BF16)
    db_ref[...] = (inner_db_ref[...] + dot(xt_ref[...], ent_ref[1], 1, 1)).astype(BF16)


def swapped(array):
    return lax.ppermute(array, "seq", [(i, i ^ 1) for i in range(lax.axis_size("seq"))])


def from_chip(array, k):
    n = lax.axis_size("seq")
    return lax.ppermute(array, "seq", [(i, (i + 2 * k) % n) for i in range(n)])


def from_replica(array, distance, k):
    replicas, n = lax.axis_size("dp"), lax.axis_size("seq")
    pairs = [
        (r * n + i, (r ^ distance) * n + (i + 2 * k) % n) for r in range(replicas) for i in range(n)
    ]
    return lax.ppermute(array, ("dp", "seq"), pairs)


def call(kernel, outs, ins, scratch, microseconds, name, limit=16):
    return pl.pallas_call(
        kernel,
        out_shape=tuple(jax.ShapeDtypeStruct(*out) for out in outs),
        in_specs=ins,
        out_specs=(VMEM,) * len(outs),
        scratch_shapes=scratch,
        compiler_params=pltpu.CompilerParams(vmem_limit_bytes=limit << 20),
        cost_estimate=cost(microseconds),
        name=name,
    )


def body(query, key, value, ssm_input, in_b, in_c, step, rate_log, skip, block_mask, grad_out):
    n = lax.axis_size("seq")
    chips = n // 2
    replicas = lax.axis_size("dp")
    tokens = query.shape[1]
    blocks = block_mask.shape[1]
    most = 3 * blocks // 8
    every = blocks * BLOCK
    q, g, x = query[0], grad_out[0], ssm_input[0]
    b, c, steps = in_b[0], in_c[0], step[0].T

    (kv,) = call(
        pack_kernel,
        [((tokens, 2 * LANES), BF16)],
        [AFTER] * 2,
        [pltpu.SemaphoreType.DMA((2,))],
        1,
        "pack_kv",
        60,
    )(key[0], value[0])
    kv_parts = [kv] + [from_chip(kv, k) for k in range(1, chips)]

    states, inner_y, inner_dx, inner_db, inner_dc, sums = call(
        chunk_kernel,
        [((4, NS, WIDE + LANES), F32)]
        + [((tokens, WIDE), F32)] * 2
        + [((tokens, NS), F32)] * 2
        + [((2 * HS, LANES), F32)],
        [VMEM] * 5 + [SMEM] * 2,
        [
            pltpu.VMEM((LANES, tokens), F32),
            pltpu.VMEM((tokens, WIDE), BF16),
            pltpu.VMEM((tokens, WIDE), BF16),
            pltpu.VMEM((tokens, WIDE), BF16),
            pltpu.VMEM((tokens, tokens), F32),
            pltpu.VMEM((tokens, tokens), F32),
            pltpu.VMEM((tokens, tokens), BF16),
            pltpu.VMEM((LANES, 2 * tokens), F32),
        ],
        6,
        "chunk_alone",
        20,
    )(x, g, b, c, steps, rate_log, skip)
    half = ((4, HALF, WIDE + LANES), F32)
    keep, give, stack = call(
        split_kernel,
        [half, half, ((chips, tokens, 2 * LANES), BF16)],
        [VMEM] * (1 + chips),
        [],
        1,
        "split_states",
    )(states, *kv_parts)
    received = swapped(give)
    other_stack = swapped(stack)

    messages = call(
        lambda *refs: combine_kernel(chips, *refs),
        [((HALF, WIDE + LANES), BF16)] * (chips - 1),
        [VMEM] * 2 + [AFTER],
        [],
        1,
        "combine_states",
    )(keep, received, sums)
    arrived = [from_chip(messages[k - 1], k) for k in range(1, chips)]

    columns = QUERY_HEADS * BLOCK
    scratch = [
        pltpu.SMEM((most,), jnp.int32),
        pltpu.VMEM((most * BLOCK, LANES), BF16),
        pltpu.VMEM((most * BLOCK, LANES), BF16),
        pltpu.VMEM((most * BLOCK, 2 * LANES), BF16),
        pltpu.VMEM((LANES, columns), BF16),
        pltpu.VMEM((LANES, columns), BF16),
        pltpu.VMEM((columns, most * BLOCK), BF16),
        pltpu.VMEM((columns, most * BLOCK), BF16),
    ]
    first_out, first_dq, first_acc, kv_all = call(
        lambda *refs: first_attention_kernel(chips, most, *refs),
        [
            ((BLOCK, columns), F32),
            ((BLOCK, columns), BF16),
            ((2 * LANES, every), F32),
            ((every, 2 * LANES), BF16),
        ],
        [SMEM] + [VMEM] * 4 + [AFTER],
        scratch,
        5,
        "first_attention",
        18 + most,
    )(block_mask[0], q, g, stack, other_stack, messages[0])
    entering = ((2, HALF, WIDE), BF16)
    own, give, totals = call(
        lambda *refs: chain_kernel(chips, *refs),
        [entering, entering, ((2 * HS, LANES), F32)],
        [VMEM] * 3 + [AFTER] + [VMEM] * (chips - 1),
        [],
        2,
        "chain_states",
    )(keep, received, sums, first_dq, *arrived)
    other = swapped(give)
    neighbour = from_replica(totals, 1, 0)

    second_out, dq, acc = call(
        lambda *refs: second_attention_kernel(most, *refs),
        [((BLOCK, columns), F32), ((tokens, columns), BF16), ((2 * LANES, every), F32)],
        [SMEM] + [VMEM] * 5 + [AFTER],
        scratch,
        5,
        "second_attention",
        18 + most,
    )(block_mask[0], q, g, kv_all, first_dq, first_acc, totals)
    keep, give, sums = call(
        lambda *refs: share_kernel(chips, *refs),
        [
            ((chips * 2 * LANES, tokens), BF16),
            ((chips * 2 * LANES + 32, tokens), BF16),
            ((2 * HS, LANES), F32),
        ],
        [VMEM] * 3,
        [],
        1,
        "share_key_gradients",
    )(acc, totals, neighbour)
    partial, summed, *messages = call(
        lambda *refs: pair_sum_kernel(chips, *refs),
        [((2 * LANES, tokens), F32), ((2 * HS, LANES), F32)]
        + [((2 * LANES + 32, tokens), BF16)] * (chips - 1),
        [VMEM] * 3,
        [],
        1,
        "pair_sum",
    )(keep, swapped(give), sums)
    arrived = [from_chip(messages[k - 1], k) for k in range(1, chips)]
    y, dx, db, dc, passed = call(
        outer_kernel,
        [((tokens, WIDE), BF16)] * 2 + [((tokens, NS), BF16)] * 2 + [((2 * HS, LANES), F32)],
        [VMEM] * 5 + [SMEM] + [VMEM] * 9,
        [
            pltpu.VMEM((LANES, tokens), F32),
            pltpu.VMEM((tokens, WIDE), BF16),
            pltpu.VMEM((tokens, WIDE), BF16),
            pltpu.VMEM((2, NS, WIDE), BF16),
        ],
        3,
        "chunk_outer",
    )(
        x, g, b, c, steps, rate_log, own, other, first_out, second_out,
        inner_y, inner_dx, inner_db, inner_dc, summed,
    )
    farther = [from_replica(passed, d, k) for d in range(2, replicas, 2) for k in range(chips)]

    tokens_all = replicas * n * tokens
    dk, dv, grad_rate_log, grad_skip = call(
        lambda *refs: owner_sum_kernel(chips, tokens_all, *refs),
        [((tokens, LANES), BF16)] * 2 + [((1, HS), F32)] * 2,
        [VMEM] * (chips + 1 + len(farther)),
        [],
        1,
        "owner_sum",
    )(partial, summed, *arrived, *farther)
    return (
        y[None],
        dq[None],
        dk[None],
        dv[None],
        dx[None],
        db[None],
        dc[None],
        grad_rate_log.reshape(HS),
        grad_skip.reshape(HS),
    )


def solution(mesh):
    split = P("dp", "seq", None)
    in_specs = (split,) * 7 + (P(), P(), P("dp", None, None), split)
    out_specs = (split,) * 7 + (P(), P())
    return jax.shard_map(body, mesh=mesh, in_specs=in_specs, out_specs=out_specs, check_vma=False)
```

```python
import jax
import jax.numpy as jnp
from jax import lax
from jax.experimental import pallas as pl
from jax.experimental.pallas import tpu as pltpu
from jax.sharding import PartitionSpec as P

HEAD_WIDTH = 128
QUERY_HEADS = 8
HS = 8
P_SIZE = 128
NS = 128
BLOCK = 128
WIDE = HS * P_SIZE
LANES = 128
FACTOR = HEAD_WIDTH ** (-0.5)
LOG2E = 1.4426950408889634
NEG = -1e30
HALF = NS // 2
HIGH = lax.Precision.HIGHEST
F32 = jnp.float32
BF16 = jnp.bfloat16

VMEM = pl.BlockSpec(memory_space=pltpu.VMEM)
SMEM = pl.BlockSpec(memory_space=pltpu.SMEM)
AFTER = pl.BlockSpec(memory_space=pl.ANY)


def cost(microseconds):
    return pl.CostEstimate(
        flops=int(microseconds * 1.1e9), bytes_accessed=1 << 20, transcendentals=0
    )


def dot(a, b, ca, cb, precision=None):
    return lax.dot_general(
        a, b, (((ca,), (cb,)), ((), ())), preferred_element_type=F32, precision=precision
    )


def head(h):
    return slice(h * LANES, (h + 1) * LANES)


def running_logs(step_ref, rate_ref, pad_ref):
    pad_ref[...] = jnp.zeros_like(pad_ref)
    for h in range(HS):
        rate = jnp.exp(jnp.full((1, 2 * BLOCK), rate_ref[h], F32))
        pad_ref[h : h + 1, :] = -step_ref[h : h + 1, :] * rate
    row = lax.broadcasted_iota(jnp.int32, (BLOCK, BLOCK), 0)
    col = lax.broadcasted_iota(jnp.int32, (BLOCK, BLOCK), 1)
    upper = jnp.where(row <= col, 1.0, 0.0).astype(F32)
    flat0 = dot(pad_ref[:, :BLOCK], upper, 1, 0, HIGH)
    flat1 = dot(pad_ref[:, BLOCK:], upper, 1, 0, HIGH)
    return flat0, flat1, flat0.T, flat1.T


def scaled(x_ref, column, out_ref):
    for h in range(HS):
        out_ref[:, head(h)] = (x_ref[:, head(h)].astype(F32) * column[:, h : h + 1]).astype(BF16)


def chip_and_core():
    me = lax.axis_index("seq")
    return me // 2, me % 2


def fetch(pairs, sems):
    copies = [
        pltpu.make_async_copy(source, target, sems.at[i]) for i, (source, target) in enumerate(pairs)
    ]
    for copy in copies:
        copy.start()
    return copies


def pack_kernel(key_ref, value_ref, out_ref, sems):
    pairs = [(key_ref, out_ref.at[:, :LANES]), (value_ref, out_ref.at[:, LANES:])]
    for copy in fetch(pairs, sems):
        copy.wait()


def split_kernel(states_ref, *refs):
    keep_ref, give_ref, stack_ref = refs[-3:]
    _, core = chip_and_core()
    keep_ref[...] = states_ref[:, pl.ds(pl.multiple_of(core * HALF, HALF), HALF), :]
    give_ref[...] = states_ref[:, pl.ds(pl.multiple_of((1 - core) * HALF, HALF), HALF), :]
    for k, ref in enumerate(refs[:-3]):
        stack_ref[k] = ref[...]


def enter_and_tail(run0, run1):
    t0, t1 = run0[BLOCK - 1 :, :], run1[BLOCK - 1 :, :]
    enter = jnp.concatenate([run0, run1 + t0], axis=0)
    tail = jnp.concatenate([(t0 - run0) + t1, t1 - run1], axis=0)
    return enter, tail, t0 + t1


def local_states_kernel(
    x_ref, g_ref, b_ref, c_ref, step_ref, rate_ref, state_ref, pad_ref, high_ref, rest_ref, log_ref
):
    _, _, run0, run1 = running_logs(step_ref, rate_ref, pad_ref)
    enter_log, tail_log, total = enter_and_tail(run0, run1)
    enter, tail = jnp.exp(enter_log), jnp.exp(tail_log)
    state_ref[:, :, WIDE:] = jnp.broadcast_to(total, (4, NS, LANES))
    cases = ((b_ref, x_ref, tail, tail_log), (c_ref, g_ref, enter, enter_log))
    for direction, (left, right, factor, weight) in enumerate(cases):
        for h in range(HS):
            product = right[:, head(h)].astype(F32) * factor[:, h : h + 1]
            rounded = product.astype(BF16)
            high_ref[:, head(h)] = rounded
            rest_ref[:, head(h)] = (product - rounded.astype(F32)).astype(BF16)
            log_ref[:, head(h)] = (product * weight[:, h : h + 1]).astype(BF16)
        turned_left = left[...].astype(F32).T.astype(BF16)
        state_ref[direction, :, :WIDE] = dot(turned_left, high_ref[...], 1, 0) + dot(
            turned_left, rest_ref[...], 1, 0
        )
        state_ref[3 - direction, :, :WIDE] = dot(turned_left, log_ref[...], 1, 0)


def three_parts(value, rows):
    high = value.astype(BF16).astype(F32)
    middle = (value - high).astype(BF16).astype(F32)
    low = value - high - middle
    index = lax.broadcasted_iota(jnp.int32, (rows, LANES), 0)
    return jnp.where(index == 0, high, jnp.where(index == 1, middle, low)).astype(BF16)


def pair_logs(keep_ref, recv_ref, is0):
    mine, other = keep_ref[0, 0:1, WIDE:], recv_ref[0, 0:1, WIDE:]
    return jnp.where(is0, mine, other), jnp.where(is0, other, mine)


def combine_kernel(chips, keep_ref, recv_ref, _, *message_refs):
    chip, core = chip_and_core()
    is0 = core == 0
    log0, log1 = pair_logs(keep_ref, recv_ref, is0)
    logs = three_parts(log0 + log1, HALF)
    decay0, decay1 = jnp.exp(log0), jnp.exp(log1)
    for h in range(HS):
        mine, other = keep_ref[0, :, head(h)], recv_ref[0, :, head(h)]
        first, second = jnp.where(is0, mine, other), jnp.where(is0, other, mine)
        state = (first * decay1[:, h : h + 1] + second).astype(BF16)
        mine, other = keep_ref[1, :, head(h)], recv_ref[1, :, head(h)]
        first, second = jnp.where(is0, mine, other), jnp.where(is0, other, mine)
        grad = (second * decay0[:, h : h + 1] + first).astype(BF16)
        for k in range(1, chips):
            later = chip + k < chips
            message_refs[k - 1][:, head(h)] = jnp.where(later, state, grad)
    for k in range(1, chips):
        message_refs[k - 1][:, WIDE:] = logs


def chain_kernel(chips, keep_ref, recv_ref, sums_ref, _, *refs):
    message_refs = refs[: chips - 1]
    own_ref, give_ref, total_ref = refs[chips - 1 :]
    chip, core = chip_and_core()
    is0 = core == 0
    log0, log1 = pair_logs(keep_ref, recv_ref, is0)
    decay0, decay1 = jnp.exp(log0), jnp.exp(log1)
    weight0, weight1 = log0 * decay0, log1 * decay1
    factors = [None]
    for ref in message_refs:
        parts = ref[:16, WIDE:].astype(F32)
        factors.append(jnp.exp(parts[0:1, :] + parts[1:2, :] + parts[2:3, :]))
    total_ref[...] = sums_ref[...]
    for h in range(HS):
        column = slice(h, h + 1)
        states = [(keep_ref[kind, :, head(h)], recv_ref[kind, :, head(h)]) for kind in range(4)]
        (s0, s1), (g0, g1), (qs0, qs1), (qg0, qg1) = [
            (jnp.where(is0, mine, other), jnp.where(is0, other, mine)) for mine, other in states
        ]
        state = jnp.zeros((HALF, LANES), F32)
        for k in range(chips - 1, 0, -1):
            new = state * factors[k][:, column] + message_refs[k - 1][:, head(h)].astype(F32)
            state = jnp.where(k <= chip, new, state)
        grad = jnp.zeros((HALF, LANES), F32)
        for k in range(1, chips):
            new = grad * factors[k][:, column] + message_refs[k - 1][:, head(h)].astype(F32)
            grad = jnp.where(k > chip, new, grad)
        h0, l1 = state, grad
        h1 = h0 * decay0[:, column] + s0
        l0 = l1 * decay1[:, column] + g1
        cross = h0 * (l0 * weight0[:, column] + qs0) + h1 * (l1 * weight1[:, column] + qs1)
        cross += l0 * qg0 + l1 * qg1
        total_ref[h : h + 1, :] += jnp.sum(cross, axis=0, keepdims=True)
        h0, h1, l0, l1 = (value.astype(BF16) for value in (h0, h1, l0, l1))
        own_ref[0, :, head(h)] = jnp.where(is0, h0, h1)
        own_ref[1, :, head(h)] = jnp.where(is0, l0, l1)
        give_ref[0, :, head(h)] = jnp.where(is0, h1, h0)
        give_ref[1, :, head(h)] = jnp.where(is0, l1, l0)


def find_slots(row, most, mask_ref, slot_ref):
    for slot in range(most):
        slot_ref[slot] = row

    def note(j, seen):
        hit = mask_ref[row, j]

        @pl.when(hit == 1)
        def _():
            slot_ref[seen] = j

        return seen + hit

    allowed = lax.fori_loop(0, mask_ref.shape[0], note, 0)
    return [(slot_ref[slot], slot < allowed) for slot in range(most)]


def block_attention(
    block, slots, q_ref, g_ref, kv_ref, out_ref, dq_ref,
    k_ref, k_live_ref, v_ref, q_turned_ref, g_turned_ref, ds_ref, wb_ref,
):
    scale = FACTOR * LOG2E
    lower, upper = slice(0, LANES), slice(LANES, 2 * LANES)
    own = slice(block * BLOCK, (block + 1) * BLOCK)
    at = slice(block * BLOCK, (block + 1) * BLOCK)
    for slot, (index, live) in enumerate(slots):
        source = pl.ds(pl.multiple_of(index * BLOCK, BLOCK), BLOCK)
        target = slice(slot * BLOCK, (slot + 1) * BLOCK)
        k_tile, v_tile = kv_ref[source, lower], kv_ref[source, upper]
        k_ref[target, :] = k_tile
        k_live_ref[target, :] = jnp.where(live, k_tile, jnp.zeros_like(k_tile))
        v_ref[target, lower] = jnp.where(live, v_tile, jnp.zeros_like(v_tile))
        v_ref[target, upper] = jnp.full((BLOCK, LANES), jnp.where(live, 1.0, 0.0), F32).astype(BF16)
    group = 2
    firsts = range(0, QUERY_HEADS, group)

    def stacked(ref, first):
        return jnp.concatenate([ref[at, head(h)] for h in range(first, first + group)], axis=0)

    upcoming = dot(stacked(q_ref, 0), k_ref[...], 1, 1)
    for first in firsts:
        heads = range(first, first + group)
        rows = slice(first * BLOCK, (first + group) * BLOCK)
        q, g = stacked(q_ref, first), stacked(g_ref, first)
        scores = upcoming
        dprobs = dot(g, v_ref[:, lower], 1, 1)
        if first + group < QUERY_HEADS:
            upcoming = dot(stacked(q_ref, first + group), k_ref[...], 1, 1)
        best = jnp.max(scores, axis=1, keepdims=True)
        weights = jnp.exp2((scores - best) * scale)
        wb_ref[rows, :] = weights.astype(BF16)
        both = dot(wb_ref[rows, :], v_ref[...], 1, 0)
        inverse = 1.0 / both[:, upper]
        out = both[:, lower] * inverse
        delta = jnp.sum(out * g.astype(F32), axis=1, keepdims=True)
        ds_ref[rows, :] = (weights * (dprobs - delta)).astype(BF16)
        dq = (dot(ds_ref[rows, :], k_live_ref[...], 1, 0) * (inverse * FACTOR)).astype(BF16)
        q_turned_ref[:, rows] = (q.astype(F32) * inverse).astype(BF16).T
        g_turned_ref[:, rows] = (g.astype(F32) * inverse).astype(BF16).T
        for place, h in enumerate(heads):
            part = slice(place * BLOCK, (place + 1) * BLOCK)
            out_ref[:, head(h)] = out[part]
            dq_ref[own, head(h)] = dq[part]


def add_key_terms(slots, acc_ref, q_turned_ref, g_turned_ref, ds_ref, wb_ref):
    lower, upper = slice(0, LANES), slice(LANES, 2 * LANES)
    dk = dot(q_turned_ref[...], ds_ref[...], 1, 0)
    dv = dot(g_turned_ref[...], wb_ref[...], 1, 0)
    for slot, (index, live) in enumerate(slots):
        source = slice(slot * BLOCK, (slot + 1) * BLOCK)

        @pl.when(live)
        def _():
            target = pl.ds(pl.multiple_of(index * BLOCK, BLOCK), BLOCK)
            acc_ref[lower, target] += dk[:, source]
            acc_ref[upper, target] += dv[:, source]


def first_attention_kernel(
    chips, most, mask_ref, q_ref, g_ref, stack_ref, other_stack_ref, _, out_ref, dq_ref, acc_ref, kv_ref, slot_ref, *scratch
):
    tokens = q_ref.shape[0]
    chip, core = chip_and_core()
    acc_ref[...] = jnp.zeros_like(acc_ref)
    for k in range(chips):
        for other, ref in enumerate((stack_ref, other_stack_ref)):
            source = 2 * lax.rem(chip + chips - k, chips) + lax.rem(core + other, 2)
            at = pl.ds(pl.multiple_of(source * tokens, tokens), tokens)
            kv_ref[at, :] = ref[k]
    slots = find_slots(2 * lax.axis_index("seq"), most, mask_ref, slot_ref)
    block_attention(0, slots, q_ref, g_ref, kv_ref, out_ref, dq_ref, *scratch)
    add_key_terms(slots, acc_ref, *scratch[3:])


def second_attention_kernel(
    most, mask_ref, q_ref, g_ref, kv_ref, first_dq_ref, _, out_ref, dq_ref,
    q_turned_ref, g_turned_ref, ds_ref, wb_ref, slot_ref, *scratch
):
    dq_ref[:BLOCK, :] = first_dq_ref[...]
    slots = find_slots(2 * lax.axis_index("seq") + 1, most, mask_ref, slot_ref)
    products = (q_turned_ref, g_turned_ref, ds_ref, wb_ref)
    block_attention(1, slots, q_ref, g_ref, kv_ref, out_ref, dq_ref, *scratch, *products)


def key_terms_kernel(most, mask_ref, first_acc_ref, *refs):
    products, acc_ref, slot_ref = refs[:4], refs[4], refs[5]
    acc_ref[...] = first_acc_ref[...]
    slots = find_slots(2 * lax.axis_index("seq") + 1, most, mask_ref, slot_ref)
    add_key_terms(slots, acc_ref, *products)


def share_kernel(chips, acc_ref, *refs):
    keep_ref, give_ref, sums_ref = refs[-3:]
    tokens = keep_ref.shape[1]
    _, core = chip_and_core()
    sums = refs[0][...]
    for ref in refs[1:-3]:
        sums += ref[...]
    sums_ref[...] = sums
    high = sums.astype(BF16)
    middle = (sums - high.astype(F32)).astype(BF16)
    low = (sums - high.astype(F32) - middle.astype(F32)).astype(BF16)
    give_ref[chips * tokens : chips * tokens + 16, :] = jnp.concatenate([high, middle], axis=1)
    give_ref[chips * tokens + 16 :, :] = jnp.concatenate([low, jnp.zeros_like(low)], axis=1)
    for k in range(chips):
        mine = pl.multiple_of((2 * k + core) * tokens, tokens)
        other = pl.multiple_of((2 * k + 1 - core) * tokens, tokens)
        rows = slice(k * tokens, (k + 1) * tokens)
        keep_ref[rows, :] = acc_ref[:, pl.ds(mine, tokens)].astype(BF16)
        give_ref[rows, :] = acc_ref[:, pl.ds(other, tokens)].astype(BF16)


def pair_sum_kernel(chips, keep_ref, recv_ref, sums_ref, own_ref, total_ref, *message_refs):
    chip, _ = chip_and_core()
    rows = own_ref.shape[0]
    at = pl.ds(pl.multiple_of(chip * rows, rows), rows)
    own_ref[...] = keep_ref[at, :].astype(F32) + recv_ref[at, :].astype(F32)
    total = sums_ref[...] + whole_sums(recv_ref[chips * rows :, :])
    total_ref[...] = total
    high = total.astype(BF16)
    middle = (total - high.astype(F32)).astype(BF16)
    low = (total - high.astype(F32) - middle.astype(F32)).astype(BF16)
    for k in range(1, chips):
        target = pl.ds(pl.multiple_of(lax.rem(chip + k, chips) * rows, rows), rows)
        both = keep_ref[target, :].astype(F32) + recv_ref[target, :].astype(F32)
        message_refs[k - 1][:rows, :] = both.astype(BF16)
        message_refs[k - 1][rows : rows + 16, :] = jnp.concatenate([high, middle], axis=1)
        message_refs[k - 1][rows + 16 :, :] = jnp.concatenate([low, jnp.zeros_like(low)], axis=1)


def whole_sums(tail):
    tail = tail.astype(F32)
    return tail[:16, :LANES] + tail[:16, LANES:] + tail[16:, :LANES]


def owner_sum_kernel(chips, tokens_all, own_ref, sums_ref, *refs):
    parts, (dk_ref, dv_ref, rate_ref, skip_ref) = refs[: chips - 1], refs[chips - 1 :]
    rows = own_ref.shape[0]
    total = own_ref[...]
    sums = sums_ref[...]
    for part in parts:
        total += part[:rows, :].astype(F32)
        sums += whole_sums(part[rows:, :])
    dk_ref[...] = (total[:LANES].T * FACTOR).astype(BF16)
    dv_ref[...] = total[LANES:].T.astype(BF16)
    ones = jnp.ones((8, LANES), F32)
    rate = dot(ones, sums[:HS], 1, 1, HIGH) * (1.0 / tokens_all)
    skip = dot(ones, sums[HS:], 1, 1, HIGH) * (1.0 / (tokens_all * P_SIZE))
    rate_ref[...] = rate[0:1, :]
    skip_ref[...] = skip[0:1, :]


def inner_kernel(
    x_ref, g_ref, b_ref, c_ref, step_ref, rate_ref, skip_ref,
    y_ref, dx_ref, db_ref, dc_ref, sums_ref,
    pad_ref, inner_ref, dinner_ref, m_ref, runt_ref,
):
    tokens = 2 * BLOCK
    flat0, flat1, run0, run1 = running_logs(step_ref, rate_ref, pad_ref)
    own = jnp.concatenate([run0, run1], axis=0)
    runt_ref[:, :BLOCK] = flat0
    runt_ref[:, tokens : tokens + BLOCK] = flat0 - flat0[:, BLOCK - 1 :]
    runt_ref[:, tokens + BLOCK :] = flat1
    b = b_ref[...]
    c = c_ref[...]
    inner_ref[...] = dot(c, b, 1, 1)
    dinner_ref[...] = jnp.zeros_like(dinner_ref)
    row0 = lax.broadcasted_iota(jnp.int32, (BLOCK, BLOCK), 0)
    col0 = lax.broadcasted_iota(jnp.int32, (BLOCK, BLOCK), 1)
    row1 = lax.broadcasted_iota(jnp.int32, (BLOCK, tokens), 0)
    col1 = lax.broadcasted_iota(jnp.int32, (BLOCK, tokens), 1)
    seen0 = row0 >= col0
    seen1 = row1 + BLOCK >= col1
    m_ref[:BLOCK, BLOCK:] = jnp.zeros((BLOCK, BLOCK), BF16)
    for h in range(HS):
        lanes = head(h)
        x = x_ref[:, lanes]
        g = g_ref[:, lanes]
        xf, gf = x.astype(F32), g.astype(F32)
        gain = skip_ref[h]
        spread0 = jnp.where(seen0, own[:BLOCK, h : h + 1] - runt_ref[h : h + 1, :BLOCK], NEG)
        spread1 = jnp.where(seen1, own[BLOCK:, h : h + 1] - runt_ref[h : h + 1, tokens:], NEG)
        decay0, decay1 = jnp.exp(spread0), jnp.exp(spread1)
        dm = dot(g, x, 1, 1)
        e0, e1 = decay0 * dm[:BLOCK, :BLOCK], decay1 * dm[BLOCK:, :]
        m_ref[:BLOCK, :BLOCK] = (decay0 * inner_ref[:BLOCK, :BLOCK]).astype(BF16)
        m_ref[BLOCK:, :] = (decay1 * inner_ref[BLOCK:, :]).astype(BF16)
        dinner_ref[:BLOCK, :BLOCK] += e0
        dinner_ref[BLOCK:, :] += e1
        w0 = jnp.sum(spread0 * (e0 * inner_ref[:BLOCK, :BLOCK]), axis=0, keepdims=True)
        w1 = jnp.sum(spread1 * (e1 * inner_ref[BLOCK:, :]), axis=0, keepdims=True)
        m = m_ref[...]
        y_ref[:, lanes] = dot(m, x, 1, 0) + gain * xf
        dx_ref[:, lanes] = dot(m, g, 0, 0) + gain * gf
        sums_ref[h : h + 1, :] = w0 + w1[:, :BLOCK] + w1[:, BLOCK:]
        sums_ref[HS + h : HS + h + 1, :] = jnp.sum(gf * xf, axis=0, keepdims=True)
    dinner = dinner_ref[...].astype(BF16)
    dc_ref[...] = dot(dinner, b, 1, 0)
    db_ref[...] = dot(dinner, c, 0, 0)


def chunk_kernel(
    x_ref, g_ref, b_ref, c_ref, step_ref, rate_ref, skip_ref,
    state_ref, y_ref, dx_ref, db_ref, dc_ref, sums_ref, pad_ref, *scratch
):
    operands = (x_ref, g_ref, b_ref, c_ref, step_ref, rate_ref)
    local_states_kernel(*operands, state_ref, pad_ref, *scratch[:3])
    inner_kernel(*operands, skip_ref, y_ref, dx_ref, db_ref, dc_ref, sums_ref, pad_ref, *scratch[3:])


def outer_kernel(
    x_ref, g_ref, b_ref, c_ref, step_ref, rate_ref, own_ref, other_ref, first_ref, second_ref,
    inner_y_ref, inner_dx_ref, inner_db_ref, inner_dc_ref, _,
    y_ref, dx_ref, db_ref, dc_ref,
    pad_ref, xt_ref, gt_ref, ent_ref,
):
    _, core = chip_and_core()
    ent_ref[:, pl.ds(pl.multiple_of(core * HALF, HALF), HALF), :] = own_ref[...]
    ent_ref[:, pl.ds(pl.multiple_of((1 - core) * HALF, HALF), HALF), :] = other_ref[...]
    _, _, run0, run1 = running_logs(step_ref, rate_ref, pad_ref)
    enter_log, tail_log, _ = enter_and_tail(run0, run1)
    enter, tail = jnp.exp(enter_log), jnp.exp(tail_log)
    scaled(x_ref, tail, xt_ref)
    scaled(g_ref, enter, gt_ref)
    b = b_ref[...]
    c = c_ref[...]
    for h in range(HS):
        lanes = head(h)
        carried = dot(c, ent_ref[0, :, lanes], 1, 0) * enter[:, h : h + 1]
        back = dot(b, ent_ref[1, :, lanes], 1, 0) * tail[:, h : h + 1]
        y = inner_y_ref[:, lanes] + carried
        y_ref[:BLOCK, lanes] = (y[:BLOCK] + first_ref[:, lanes]).astype(BF16)
        y_ref[BLOCK:, lanes] = (y[BLOCK:] + second_ref[:, lanes]).astype(BF16)
        dx_ref[:, lanes] = (inner_dx_ref[:, lanes] + back).astype(BF16)
    dc_ref[...] = (inner_dc_ref[...] + dot(gt_ref[...], ent_ref[0], 1, 1)).astype(BF16)
    db_ref[...] = (inner_db_ref[...] + dot(xt_ref[...], ent_ref[1], 1, 1)).astype(BF16)


def swapped(array):
    return lax.ppermute(array, "seq", [(i, i ^ 1) for i in range(lax.axis_size("seq"))])


def from_chip(array, k):
    n = lax.axis_size("seq")
    return lax.ppermute(array, "seq", [(i, (i + 2 * k) % n) for i in range(n)])


def from_replica(array, distance):
    pairs = [(r, r ^ distance) for r in range(lax.axis_size("dp"))]
    return lax.ppermute(array, "dp", pairs)


def call(kernel, outs, ins, scratch, microseconds, name, limit=16):
    return pl.pallas_call(
        kernel,
        out_shape=tuple(jax.ShapeDtypeStruct(*out) for out in outs),
        in_specs=ins,
        out_specs=(VMEM,) * len(outs),
        scratch_shapes=scratch,
        compiler_params=pltpu.CompilerParams(vmem_limit_bytes=limit << 20),
        cost_estimate=cost(microseconds),
        name=name,
    )


def body(query, key, value, ssm_input, in_b, in_c, step, rate_log, skip, block_mask, grad_out):
    n = lax.axis_size("seq")
    chips = n // 2
    replicas = lax.axis_size("dp")
    tokens = query.shape[1]
    blocks = block_mask.shape[1]
    most = 3 * blocks // 8
    every = blocks * BLOCK
    q, g, x = query[0], grad_out[0], ssm_input[0]
    b, c, steps = in_b[0], in_c[0], step[0].T

    (kv,) = call(
        pack_kernel,
        [((tokens, 2 * LANES), BF16)],
        [AFTER] * 2,
        [pltpu.SemaphoreType.DMA((2,))],
        1,
        "pack_kv",
        60,
    )(key[0], value[0])
    kv_parts = [kv] + [from_chip(kv, k) for k in range(1, chips)]

    states, inner_y, inner_dx, inner_db, inner_dc, sums = call(
        chunk_kernel,
        [((4, NS, WIDE + LANES), F32)]
        + [((tokens, WIDE), F32)] * 2
        + [((tokens, NS), F32)] * 2
        + [((2 * HS, LANES), F32)],
        [VMEM] * 5 + [SMEM] * 2,
        [
            pltpu.VMEM((LANES, tokens), F32),
            pltpu.VMEM((tokens, WIDE), BF16),
            pltpu.VMEM((tokens, WIDE), BF16),
            pltpu.VMEM((tokens, WIDE), BF16),
            pltpu.VMEM((tokens, tokens), F32),
            pltpu.VMEM((tokens, tokens), F32),
            pltpu.VMEM((tokens, tokens), BF16),
            pltpu.VMEM((LANES, 2 * tokens), F32),
        ],
        6,
        "chunk_alone",
        20,
    )(x, g, b, c, steps, rate_log, skip)
    half = ((4, HALF, WIDE + LANES), F32)
    keep, give, stack = call(
        split_kernel,
        [half, half, ((chips, tokens, 2 * LANES), BF16)],
        [VMEM] * (1 + chips),
        [],
        1,
        "split_states",
    )(states, *kv_parts)
    received = swapped(give)
    other_stack = swapped(stack)

    messages = call(
        lambda *refs: combine_kernel(chips, *refs),
        [((HALF, WIDE + LANES), BF16)] * (chips - 1),
        [VMEM] * 2 + [AFTER],
        [],
        1,
        "combine_states",
    )(keep, received, sums)
    arrived = [from_chip(messages[k - 1], k) for k in range(1, chips)]

    columns = QUERY_HEADS * BLOCK
    scratch = [
        pltpu.SMEM((most,), jnp.int32),
        pltpu.VMEM((most * BLOCK, LANES), BF16),
        pltpu.VMEM((most * BLOCK, LANES), BF16),
        pltpu.VMEM((most * BLOCK, 2 * LANES), BF16),
        pltpu.VMEM((LANES, columns), BF16),
        pltpu.VMEM((LANES, columns), BF16),
        pltpu.VMEM((columns, most * BLOCK), BF16),
        pltpu.VMEM((columns, most * BLOCK), BF16),
    ]
    first_out, first_dq, first_acc, kv_all = call(
        lambda *refs: first_attention_kernel(chips, most, *refs),
        [
            ((BLOCK, columns), F32),
            ((BLOCK, columns), BF16),
            ((2 * LANES, every), F32),
            ((every, 2 * LANES), BF16),
        ],
        [SMEM] + [VMEM] * 4 + [AFTER],
        scratch,
        5,
        "first_attention",
        18 + most,
    )(block_mask[0], q, g, stack, other_stack, messages[0])
    entering = ((2, HALF, WIDE), BF16)
    own, give, totals = call(
        lambda *refs: chain_kernel(chips, *refs),
        [entering, entering, ((2 * HS, LANES), F32)],
        [VMEM] * 3 + [AFTER] + [VMEM] * (chips - 1),
        [],
        2,
        "chain_states",
    )(keep, received, sums, first_dq, *arrived)
    other = swapped(give)
    rounds = [1 << bit for bit in range((replicas - 1).bit_length())]
    replicated = totals
    for distance in rounds[:-1]:
        replicated = replicated + from_replica(replicated, distance)
    last_round = from_replica(replicated, rounds[-1])

    second_out, dq, *products = call(
        lambda *refs: second_attention_kernel(most, *refs),
        [
            ((BLOCK, columns), F32),
            ((tokens, columns), BF16),
            ((LANES, columns), BF16),
            ((LANES, columns), BF16),
            ((columns, most * BLOCK), BF16),
            ((columns, most * BLOCK), BF16),
        ],
        [SMEM] + [VMEM] * 4 + [AFTER],
        scratch[:4],
        4,
        "second_attention",
        18 + most,
    )(block_mask[0], q, g, kv_all, first_dq, totals)
    (acc,) = call(
        lambda *refs: key_terms_kernel(most, *refs),
        [((2 * LANES, every), F32)],
        [SMEM] + [VMEM] * 5,
        scratch[:1],
        2,
        "key_terms",
        18 + most,
    )(block_mask[0], first_acc, *products)
    keep, give, sums = call(
        lambda *refs: share_kernel(chips, *refs),
        [
            ((chips * 2 * LANES, tokens), BF16),
            ((chips * 2 * LANES + 32, tokens), BF16),
            ((2 * HS, LANES), F32),
        ],
        [VMEM] * 3,
        [],
        1,
        "share_key_gradients",
    )(acc, replicated, last_round)
    partial, summed, *messages = call(
        lambda *refs: pair_sum_kernel(chips, *refs),
        [((2 * LANES, tokens), F32), ((2 * HS, LANES), F32)]
        + [((2 * LANES + 32, tokens), BF16)] * (chips - 1),
        [VMEM] * 3,
        [],
        1,
        "pair_sum",
    )(keep, swapped(give), sums)
    arrived = [from_chip(messages[k - 1], k) for k in range(1, chips)]

    y, dx, db, dc = call(
        outer_kernel,
        [((tokens, WIDE), BF16)] * 2 + [((tokens, NS), BF16)] * 2,
        [VMEM] * 5 + [SMEM] + [VMEM] * 8 + [AFTER],
        [
            pltpu.VMEM((LANES, tokens), F32),
            pltpu.VMEM((tokens, WIDE), BF16),
            pltpu.VMEM((tokens, WIDE), BF16),
            pltpu.VMEM((2, NS, WIDE), BF16),
        ],
        3,
        "chunk_outer",
    )(
        x, g, b, c, steps, rate_log, own, other, first_out, second_out,
        inner_y, inner_dx, inner_db, inner_dc, messages[0],
    )

    tokens_all = replicas * n * tokens
    dk, dv, grad_rate_log, grad_skip = call(
        lambda *refs: owner_sum_kernel(chips, tokens_all, *refs),
        [((tokens, LANES), BF16)] * 2 + [((1, HS), F32)] * 2,
        [VMEM] * (chips + 1),
        [],
        1,
        "owner_sum",
    )(partial, summed, *arrived)
    return (
        y[None],
        dq[None],
        dk[None],
        dv[None],
        dx[None],
        db[None],
        dc[None],
        grad_rate_log.reshape(HS),
        grad_skip.reshape(HS),
    )


def solution(mesh):
    split = P("dp", "seq", None)
    in_specs = (split,) * 7 + (P(), P(), P("dp", None, None), split)
    out_specs = (split,) * 7 + (P(), P())
    return jax.shard_map(body, mesh=mesh, in_specs=in_specs, out_specs=out_specs, check_vma=False)
```

```python
import jax
import jax.numpy as jnp
from jax import lax
from jax.experimental import pallas as pl
from jax.experimental.pallas import tpu as pltpu
from jax.sharding import PartitionSpec as P

HEAD_WIDTH = 128
QUERY_HEADS = 8
HS = 8
P_SIZE = 128
NS = 128
BLOCK = 128
WIDE = HS * P_SIZE
LANES = 128
FACTOR = HEAD_WIDTH ** (-0.5)
LOG2E = 1.4426950408889634
NEG = -1e30
HALF = NS // 2
HALF_HEADS = QUERY_HEADS // 2
HIGH = lax.Precision.HIGHEST
F32 = jnp.float32
BF16 = jnp.bfloat16

VMEM = pl.BlockSpec(memory_space=pltpu.VMEM)
SMEM = pl.BlockSpec(memory_space=pltpu.SMEM)
AFTER = pl.BlockSpec(memory_space=pl.ANY)


def cost(microseconds):
    return pl.CostEstimate(
        flops=int(microseconds * 1.1e9), bytes_accessed=1 << 20, transcendentals=0
    )


def dot(a, b, ca, cb, precision=None):
    return lax.dot_general(
        a, b, (((ca,), (cb,)), ((), ())), preferred_element_type=F32, precision=precision
    )


def head(h):
    return slice(h * LANES, (h + 1) * LANES)


def running_logs(step_ref, rate_ref, pad_ref):
    pad_ref[...] = jnp.zeros_like(pad_ref)
    for h in range(HS):
        rate = jnp.exp(jnp.full((1, 2 * BLOCK), rate_ref[h], F32))
        pad_ref[h : h + 1, :] = -step_ref[h : h + 1, :] * rate
    row = lax.broadcasted_iota(jnp.int32, (BLOCK, BLOCK), 0)
    col = lax.broadcasted_iota(jnp.int32, (BLOCK, BLOCK), 1)
    upper = jnp.where(row <= col, 1.0, 0.0).astype(F32)
    flat0 = dot(pad_ref[:, :BLOCK], upper, 1, 0, HIGH)
    flat1 = dot(pad_ref[:, BLOCK:], upper, 1, 0, HIGH)
    return flat0, flat1, flat0.T, flat1.T


def scaled(x_ref, column, out_ref):
    for h in range(HS):
        out_ref[:, head(h)] = (x_ref[:, head(h)].astype(F32) * column[:, h : h + 1]).astype(BF16)


def chip_and_core():
    me = lax.axis_index("seq")
    return me // 2, me % 2


def fetch(pairs, sems):
    copies = [
        pltpu.make_async_copy(source, target, sems.at[i]) for i, (source, target) in enumerate(pairs)
    ]
    for copy in copies:
        copy.start()
    return copies


def pack_kernel(key_ref, value_ref, out_ref, sems):
    pairs = [(key_ref, out_ref.at[:, :LANES]), (value_ref, out_ref.at[:, LANES:])]
    for copy in fetch(pairs, sems):
        copy.wait()


def split_kernel(states_ref, *refs):
    keep_ref, give_ref, stack_ref = refs[-3:]
    _, core = chip_and_core()
    keep_ref[...] = states_ref[:, pl.ds(pl.multiple_of(core * HALF, HALF), HALF), :]
    give_ref[...] = states_ref[:, pl.ds(pl.multiple_of((1 - core) * HALF, HALF), HALF), :]
    for k, ref in enumerate(refs[:-3]):
        stack_ref[k] = ref[...]


def enter_and_tail(run0, run1):
    t0, t1 = run0[BLOCK - 1 :, :], run1[BLOCK - 1 :, :]
    enter = jnp.concatenate([run0, run1 + t0], axis=0)
    tail = jnp.concatenate([(t0 - run0) + t1, t1 - run1], axis=0)
    return enter, tail, t0 + t1


def local_states_kernel(
    x_ref, g_ref, b_ref, c_ref, step_ref, rate_ref, state_ref, pad_ref, high_ref, rest_ref, log_ref
):
    _, _, run0, run1 = running_logs(step_ref, rate_ref, pad_ref)
    enter_log, tail_log, total = enter_and_tail(run0, run1)
    enter, tail = jnp.exp(enter_log), jnp.exp(tail_log)
    state_ref[:, :, WIDE:] = jnp.broadcast_to(total, (4, NS, LANES))
    cases = ((b_ref, x_ref, tail, tail_log), (c_ref, g_ref, enter, enter_log))
    for direction, (left, right, factor, weight) in enumerate(cases):
        for h in range(HS):
            product = right[:, head(h)].astype(F32) * factor[:, h : h + 1]
            rounded = product.astype(BF16)
            high_ref[:, head(h)] = rounded
            rest_ref[:, head(h)] = (product - rounded.astype(F32)).astype(BF16)
            log_ref[:, head(h)] = (product * weight[:, h : h + 1]).astype(BF16)
        turned_left = left[...].astype(F32).T.astype(BF16)
        state_ref[direction, :, :WIDE] = dot(turned_left, high_ref[...], 1, 0) + dot(
            turned_left, rest_ref[...], 1, 0
        )
        state_ref[3 - direction, :, :WIDE] = dot(turned_left, log_ref[...], 1, 0)


def three_parts(value, rows):
    high = value.astype(BF16).astype(F32)
    middle = (value - high).astype(BF16).astype(F32)
    low = value - high - middle
    index = lax.broadcasted_iota(jnp.int32, (rows, LANES), 0)
    return jnp.where(index == 0, high, jnp.where(index == 1, middle, low)).astype(BF16)


def pair_logs(keep_ref, recv_ref, is0):
    mine, other = keep_ref[0, 0:1, WIDE:], recv_ref[0, 0:1, WIDE:]
    return jnp.where(is0, mine, other), jnp.where(is0, other, mine)


def combine_kernel(chips, keep_ref, recv_ref, _, *message_refs):
    chip, core = chip_and_core()
    is0 = core == 0
    log0, log1 = pair_logs(keep_ref, recv_ref, is0)
    logs = three_parts(log0 + log1, HALF)
    decay0, decay1 = jnp.exp(log0), jnp.exp(log1)
    for h in range(HS):
        mine, other = keep_ref[0, :, head(h)], recv_ref[0, :, head(h)]
        first, second = jnp.where(is0, mine, other), jnp.where(is0, other, mine)
        state = (first * decay1[:, h : h + 1] + second).astype(BF16)
        mine, other = keep_ref[1, :, head(h)], recv_ref[1, :, head(h)]
        first, second = jnp.where(is0, mine, other), jnp.where(is0, other, mine)
        grad = (second * decay0[:, h : h + 1] + first).astype(BF16)
        for k in range(1, chips):
            later = chip + k < chips
            message_refs[k - 1][:, head(h)] = jnp.where(later, state, grad)
    for k in range(1, chips):
        message_refs[k - 1][:, WIDE:] = logs


def chain_kernel(chips, keep_ref, recv_ref, sums_ref, _, *refs):
    message_refs = refs[: chips - 1]
    own_ref, give_ref, total_ref = refs[chips - 1 :]
    chip, core = chip_and_core()
    is0 = core == 0
    log0, log1 = pair_logs(keep_ref, recv_ref, is0)
    decay0, decay1 = jnp.exp(log0), jnp.exp(log1)
    weight0, weight1 = log0 * decay0, log1 * decay1
    factors = [None]
    for ref in message_refs:
        parts = ref[:16, WIDE:].astype(F32)
        factors.append(jnp.exp(parts[0:1, :] + parts[1:2, :] + parts[2:3, :]))
    total_ref[...] = sums_ref[...]
    for h in range(HS):
        column = slice(h, h + 1)
        states = [(keep_ref[kind, :, head(h)], recv_ref[kind, :, head(h)]) for kind in range(4)]
        (s0, s1), (g0, g1), (qs0, qs1), (qg0, qg1) = [
            (jnp.where(is0, mine, other), jnp.where(is0, other, mine)) for mine, other in states
        ]
        state = jnp.zeros((HALF, LANES), F32)
        for k in range(chips - 1, 0, -1):
            new = state * factors[k][:, column] + message_refs[k - 1][:, head(h)].astype(F32)
            state = jnp.where(k <= chip, new, state)
        grad = jnp.zeros((HALF, LANES), F32)
        for k in range(1, chips):
            new = grad * factors[k][:, column] + message_refs[k - 1][:, head(h)].astype(F32)
            grad = jnp.where(k > chip, new, grad)
        h0, l1 = state, grad
        h1 = h0 * decay0[:, column] + s0
        l0 = l1 * decay1[:, column] + g1
        cross = h0 * (l0 * weight0[:, column] + qs0) + h1 * (l1 * weight1[:, column] + qs1)
        cross += l0 * qg0 + l1 * qg1
        total_ref[h : h + 1, :] += jnp.sum(cross, axis=0, keepdims=True)
        h0, h1, l0, l1 = (value.astype(BF16) for value in (h0, h1, l0, l1))
        own_ref[0, :, head(h)] = jnp.where(is0, h0, h1)
        own_ref[1, :, head(h)] = jnp.where(is0, l0, l1)
        give_ref[0, :, head(h)] = jnp.where(is0, h1, h0)
        give_ref[1, :, head(h)] = jnp.where(is0, l1, l0)


def find_slots(row, most, mask_ref, slot_ref):
    for slot in range(most):
        slot_ref[slot] = row

    def note(j, seen):
        hit = mask_ref[row, j]

        @pl.when(hit == 1)
        def _():
            slot_ref[seen] = j

        return seen + hit

    allowed = lax.fori_loop(0, mask_ref.shape[0], note, 0)
    return [(slot_ref[slot], slot < allowed) for slot in range(most)]


def block_attention(
    block, chosen, slots, q_ref, g_ref, kv_ref, out_ref, dq_ref, dq_rows,
    k_ref, k_live_ref, v_ref, q_turned_ref, g_turned_ref, ds_ref, wb_ref,
):
    scale = FACTOR * LOG2E
    lower, upper = slice(0, LANES), slice(LANES, 2 * LANES)
    start, stop = chosen
    at = slice(block * BLOCK, (block + 1) * BLOCK)
    for slot, (index, live) in enumerate(slots):
        source = pl.ds(pl.multiple_of(index * BLOCK, BLOCK), BLOCK)
        target = slice(slot * BLOCK, (slot + 1) * BLOCK)
        k_tile, v_tile = kv_ref[source, lower], kv_ref[source, upper]
        k_ref[target, :] = k_tile
        k_live_ref[target, :] = jnp.where(live, k_tile, jnp.zeros_like(k_tile))
        v_ref[target, lower] = jnp.where(live, v_tile, jnp.zeros_like(v_tile))
        v_ref[target, upper] = jnp.full((BLOCK, LANES), jnp.where(live, 1.0, 0.0), F32).astype(BF16)
    group = 2
    firsts = range(start, stop, group)

    def stacked(ref, first):
        return jnp.concatenate([ref[at, head(h)] for h in range(first, first + group)], axis=0)

    upcoming = dot(stacked(q_ref, start), k_ref[...], 1, 1)
    for first in firsts:
        heads = range(first, first + group)
        rows = slice((first - start) * BLOCK, (first - start + group) * BLOCK)
        q, g = stacked(q_ref, first), stacked(g_ref, first)
        scores = upcoming
        dprobs = dot(g, v_ref[:, lower], 1, 1)
        if first + group < stop:
            upcoming = dot(stacked(q_ref, first + group), k_ref[...], 1, 1)
        best = jnp.max(scores, axis=1, keepdims=True)
        weights = jnp.exp2((scores - best) * scale)
        wb_ref[rows, :] = weights.astype(BF16)
        both = dot(wb_ref[rows, :], v_ref[...], 1, 0)
        inverse = 1.0 / both[:, upper]
        out = both[:, lower] * inverse
        delta = jnp.sum(out * g.astype(F32), axis=1, keepdims=True)
        ds_ref[rows, :] = (weights * (dprobs - delta)).astype(BF16)
        dq = (dot(ds_ref[rows, :], k_live_ref[...], 1, 0) * (inverse * FACTOR)).astype(BF16)
        q_turned_ref[:, rows] = (q.astype(F32) * inverse).astype(BF16).T
        g_turned_ref[:, rows] = (g.astype(F32) * inverse).astype(BF16).T
        for place, h in enumerate(heads):
            part = slice(place * BLOCK, (place + 1) * BLOCK)
            out_ref[:, head(h - start)] = out[part]
            dq_ref[dq_rows, head(h - start)] = dq[part]


def add_key_terms(slots, acc_ref, *parts):
    lower, upper = slice(0, LANES), slice(LANES, 2 * LANES)
    dk = sum(dot(q_turned_ref[...], ds_ref[...], 1, 0) for q_turned_ref, _, ds_ref, _ in parts)
    dv = sum(dot(g_turned_ref[...], wb_ref[...], 1, 0) for _, g_turned_ref, _, wb_ref in parts)
    for slot, (index, live) in enumerate(slots):
        source = slice(slot * BLOCK, (slot + 1) * BLOCK)

        @pl.when(live)
        def _():
            target = pl.ds(pl.multiple_of(index * BLOCK, BLOCK), BLOCK)
            acc_ref[lower, target] += dk[:, source]
            acc_ref[upper, target] += dv[:, source]


def first_attention_kernel(
    chips, most, mask_ref, q_ref, g_ref, stack_ref, other_stack_ref, _, out_ref, dq_ref, acc_ref, kv_ref, slot_ref, *scratch
):
    tokens = q_ref.shape[0]
    chip, core = chip_and_core()
    acc_ref[...] = jnp.zeros_like(acc_ref)
    for k in range(chips):
        for other, ref in enumerate((stack_ref, other_stack_ref)):
            source = 2 * lax.rem(chip + chips - k, chips) + lax.rem(core + other, 2)
            at = pl.ds(pl.multiple_of(source * tokens, tokens), tokens)
            kv_ref[at, :] = ref[k]
    slots = find_slots(2 * lax.axis_index("seq"), most, mask_ref, slot_ref)
    every_row = slice(0, BLOCK)
    block_attention(
        0, (0, QUERY_HEADS), slots, q_ref, g_ref, kv_ref, out_ref, dq_ref, every_row, *scratch
    )
    add_key_terms(slots, acc_ref, scratch[3:])


def half_attention_kernel(
    chosen, most, mask_ref, q_ref, g_ref, kv_ref, _, out_ref, dq_ref,
    q_turned_ref, g_turned_ref, ds_ref, wb_ref, slot_ref, *scratch
):
    slots = find_slots(2 * lax.axis_index("seq") + 1, most, mask_ref, slot_ref)
    products = (q_turned_ref, g_turned_ref, ds_ref, wb_ref)
    every_row = slice(0, BLOCK)
    block_attention(
        1, chosen, slots, q_ref, g_ref, kv_ref, out_ref, dq_ref, every_row, *scratch, *products
    )


def key_terms_kernel(
    most, mask_ref, first_acc_ref, first_dq_ref, early_dq_ref, late_dq_ref, *refs
):
    early, late, (acc_ref, dq_ref, slot_ref) = refs[:4], refs[4:8], refs[8:]
    middle = HALF_HEADS * HEAD_WIDTH
    dq_ref[:BLOCK, :] = first_dq_ref[...]
    dq_ref[BLOCK:, :middle] = early_dq_ref[...]
    dq_ref[BLOCK:, middle:] = late_dq_ref[...]
    acc_ref[...] = first_acc_ref[...]
    slots = find_slots(2 * lax.axis_index("seq") + 1, most, mask_ref, slot_ref)
    add_key_terms(slots, acc_ref, early, late)


def share_kernel(chips, acc_ref, *refs):
    keep_ref, give_ref, sums_ref = refs[-3:]
    tokens = keep_ref.shape[1]
    _, core = chip_and_core()
    sums = refs[0][...]
    for ref in refs[1:-3]:
        sums += ref[...]
    sums_ref[...] = sums
    high = sums.astype(BF16)
    middle = (sums - high.astype(F32)).astype(BF16)
    low = (sums - high.astype(F32) - middle.astype(F32)).astype(BF16)
    give_ref[chips * tokens : chips * tokens + 16, :] = jnp.concatenate([high, middle], axis=1)
    give_ref[chips * tokens + 16 :, :] = jnp.concatenate([low, jnp.zeros_like(low)], axis=1)
    for k in range(chips):
        mine = pl.multiple_of((2 * k + core) * tokens, tokens)
        other = pl.multiple_of((2 * k + 1 - core) * tokens, tokens)
        rows = slice(k * tokens, (k + 1) * tokens)
        keep_ref[rows, :] = acc_ref[:, pl.ds(mine, tokens)].astype(BF16)
        give_ref[rows, :] = acc_ref[:, pl.ds(other, tokens)].astype(BF16)


def pair_sum_kernel(chips, keep_ref, recv_ref, sums_ref, own_ref, total_ref, *message_refs):
    chip, _ = chip_and_core()
    rows = own_ref.shape[0]
    at = pl.ds(pl.multiple_of(chip * rows, rows), rows)
    own_ref[...] = keep_ref[at, :].astype(F32) + recv_ref[at, :].astype(F32)
    total = sums_ref[...] + whole_sums(recv_ref[chips * rows :, :])
    total_ref[...] = total
    high = total.astype(BF16)
    middle = (total - high.astype(F32)).astype(BF16)
    low = (total - high.astype(F32) - middle.astype(F32)).astype(BF16)
    for k in range(1, chips):
        target = pl.ds(pl.multiple_of(lax.rem(chip + k, chips) * rows, rows), rows)
        both = keep_ref[target, :].astype(F32) + recv_ref[target, :].astype(F32)
        message_refs[k - 1][:rows, :] = both.astype(BF16)
        message_refs[k - 1][rows : rows + 16, :] = jnp.concatenate([high, middle], axis=1)
        message_refs[k - 1][rows + 16 :, :] = jnp.concatenate([low, jnp.zeros_like(low)], axis=1)


def whole_sums(tail):
    tail = tail.astype(F32)
    return tail[:16, :LANES] + tail[:16, LANES:] + tail[16:, :LANES]


def owner_sum_kernel(chips, tokens_all, own_ref, sums_ref, *refs):
    parts, (dk_ref, dv_ref, rate_ref, skip_ref) = refs[: chips - 1], refs[chips - 1 :]
    rows = own_ref.shape[0]
    total = own_ref[...]
    sums = sums_ref[...]
    for part in parts:
        total += part[:rows, :].astype(F32)
        sums += whole_sums(part[rows:, :])
    dk_ref[...] = (total[:LANES].T * FACTOR).astype(BF16)
    dv_ref[...] = total[LANES:].T.astype(BF16)
    ones = jnp.ones((8, LANES), F32)
    rate = dot(ones, sums[:HS], 1, 1, HIGH) * (1.0 / tokens_all)
    skip = dot(ones, sums[HS:], 1, 1, HIGH) * (1.0 / (tokens_all * P_SIZE))
    rate_ref[...] = rate[0:1, :]
    skip_ref[...] = skip[0:1, :]


def inner_kernel(
    x_ref, g_ref, b_ref, c_ref, step_ref, rate_ref, skip_ref,
    y_ref, dx_ref, db_ref, dc_ref, sums_ref,
    pad_ref, inner_ref, dinner_ref, m_ref, runt_ref,
):
    tokens = 2 * BLOCK
    flat0, flat1, run0, run1 = running_logs(step_ref, rate_ref, pad_ref)
    own = jnp.concatenate([run0, run1], axis=0)
    runt_ref[:, :BLOCK] = flat0
    runt_ref[:, tokens : tokens + BLOCK] = flat0 - flat0[:, BLOCK - 1 :]
    runt_ref[:, tokens + BLOCK :] = flat1
    b = b_ref[...]
    c = c_ref[...]
    inner_ref[...] = dot(c, b, 1, 1)
    dinner_ref[...] = jnp.zeros_like(dinner_ref)
    row0 = lax.broadcasted_iota(jnp.int32, (BLOCK, BLOCK), 0)
    col0 = lax.broadcasted_iota(jnp.int32, (BLOCK, BLOCK), 1)
    row1 = lax.broadcasted_iota(jnp.int32, (BLOCK, tokens), 0)
    col1 = lax.broadcasted_iota(jnp.int32, (BLOCK, tokens), 1)
    seen0 = row0 >= col0
    seen1 = row1 + BLOCK >= col1
    m_ref[:BLOCK, BLOCK:] = jnp.zeros((BLOCK, BLOCK), BF16)
    for h in range(HS):
        lanes = head(h)
        x = x_ref[:, lanes]
        g = g_ref[:, lanes]
        xf, gf = x.astype(F32), g.astype(F32)
        gain = skip_ref[h]
        spread0 = jnp.where(seen0, own[:BLOCK, h : h + 1] - runt_ref[h : h + 1, :BLOCK], NEG)
        spread1 = jnp.where(seen1, own[BLOCK:, h : h + 1] - runt_ref[h : h + 1, tokens:], NEG)
        decay0, decay1 = jnp.exp(spread0), jnp.exp(spread1)
        dm = dot(g, x, 1, 1)
        e0, e1 = decay0 * dm[:BLOCK, :BLOCK], decay1 * dm[BLOCK:, :]
        m_ref[:BLOCK, :BLOCK] = (decay0 * inner_ref[:BLOCK, :BLOCK]).astype(BF16)
        m_ref[BLOCK:, :] = (decay1 * inner_ref[BLOCK:, :]).astype(BF16)
        dinner_ref[:BLOCK, :BLOCK] += e0
        dinner_ref[BLOCK:, :] += e1
        w0 = jnp.sum(spread0 * (e0 * inner_ref[:BLOCK, :BLOCK]), axis=0, keepdims=True)
        w1 = jnp.sum(spread1 * (e1 * inner_ref[BLOCK:, :]), axis=0, keepdims=True)
        m = m_ref[...]
        y_ref[:, lanes] = dot(m, x, 1, 0) + gain * xf
        dx_ref[:, lanes] = dot(m, g, 0, 0) + gain * gf
        sums_ref[h : h + 1, :] = w0 + w1[:, :BLOCK] + w1[:, BLOCK:]
        sums_ref[HS + h : HS + h + 1, :] = jnp.sum(gf * xf, axis=0, keepdims=True)
    dinner = dinner_ref[...].astype(BF16)
    dc_ref[...] = dot(dinner, b, 1, 0)
    db_ref[...] = dot(dinner, c, 0, 0)


def chunk_kernel(
    x_ref, g_ref, b_ref, c_ref, step_ref, rate_ref, skip_ref,
    state_ref, y_ref, dx_ref, db_ref, dc_ref, sums_ref, pad_ref, *scratch
):
    operands = (x_ref, g_ref, b_ref, c_ref, step_ref, rate_ref)
    local_states_kernel(*operands, state_ref, pad_ref, *scratch[:3])
    inner_kernel(*operands, skip_ref, y_ref, dx_ref, db_ref, dc_ref, sums_ref, pad_ref, *scratch[3:])


def outer_kernel(
    x_ref, g_ref, b_ref, c_ref, step_ref, rate_ref, own_ref, other_ref, first_ref, early_ref, late_ref,
    inner_y_ref, inner_dx_ref, inner_db_ref, inner_dc_ref, _,
    y_ref, dx_ref, db_ref, dc_ref,
    pad_ref, xt_ref, gt_ref, ent_ref,
):
    _, core = chip_and_core()
    ent_ref[:, pl.ds(pl.multiple_of(core * HALF, HALF), HALF), :] = own_ref[...]
    ent_ref[:, pl.ds(pl.multiple_of((1 - core) * HALF, HALF), HALF), :] = other_ref[...]
    _, _, run0, run1 = running_logs(step_ref, rate_ref, pad_ref)
    enter_log, tail_log, _ = enter_and_tail(run0, run1)
    enter, tail = jnp.exp(enter_log), jnp.exp(tail_log)
    scaled(x_ref, tail, xt_ref)
    scaled(g_ref, enter, gt_ref)
    b = b_ref[...]
    c = c_ref[...]
    for h in range(HS):
        lanes = head(h)
        carried = dot(c, ent_ref[0, :, lanes], 1, 0) * enter[:, h : h + 1]
        back = dot(b, ent_ref[1, :, lanes], 1, 0) * tail[:, h : h + 1]
        y = inner_y_ref[:, lanes] + carried
        y_ref[:BLOCK, lanes] = (y[:BLOCK] + first_ref[:, lanes]).astype(BF16)
        second_ref, place = (early_ref, h) if h < HALF_HEADS else (late_ref, h - HALF_HEADS)
        y_ref[BLOCK:, lanes] = (y[BLOCK:] + second_ref[:, head(place)]).astype(BF16)
        dx_ref[:, lanes] = (inner_dx_ref[:, lanes] + back).astype(BF16)
    dc_ref[...] = (inner_dc_ref[...] + dot(gt_ref[...], ent_ref[0], 1, 1)).astype(BF16)
    db_ref[...] = (inner_db_ref[...] + dot(xt_ref[...], ent_ref[1], 1, 1)).astype(BF16)


def swapped(array):
    return lax.ppermute(array, "seq", [(i, i ^ 1) for i in range(lax.axis_size("seq"))])


def from_chip(array, k):
    n = lax.axis_size("seq")
    return lax.ppermute(array, "seq", [(i, (i + 2 * k) % n) for i in range(n)])


def from_replica(array, distance):
    pairs = [(r, r ^ distance) for r in range(lax.axis_size("dp"))]
    return lax.ppermute(array, "dp", pairs)


def call(kernel, outs, ins, scratch, microseconds, name, limit=16):
    return pl.pallas_call(
        kernel,
        out_shape=tuple(jax.ShapeDtypeStruct(*out) for out in outs),
        in_specs=ins,
        out_specs=(VMEM,) * len(outs),
        scratch_shapes=scratch,
        compiler_params=pltpu.CompilerParams(vmem_limit_bytes=limit << 20),
        cost_estimate=cost(microseconds),
        name=name,
    )


def body(query, key, value, ssm_input, in_b, in_c, step, rate_log, skip, block_mask, grad_out):
    n = lax.axis_size("seq")
    chips = n // 2
    replicas = lax.axis_size("dp")
    tokens = query.shape[1]
    blocks = block_mask.shape[1]
    most = 3 * blocks // 8
    every = blocks * BLOCK
    q, g, x = query[0], grad_out[0], ssm_input[0]
    b, c, steps = in_b[0], in_c[0], step[0].T

    (kv,) = call(
        pack_kernel,
        [((tokens, 2 * LANES), BF16)],
        [AFTER] * 2,
        [pltpu.SemaphoreType.DMA((2,))],
        1,
        "pack_kv",
        60,
    )(key[0], value[0])
    kv_parts = [kv] + [from_chip(kv, k) for k in range(1, chips)]

    states, inner_y, inner_dx, inner_db, inner_dc, sums = call(
        chunk_kernel,
        [((4, NS, WIDE + LANES), F32)]
        + [((tokens, WIDE), F32)] * 2
        + [((tokens, NS), F32)] * 2
        + [((2 * HS, LANES), F32)],
        [VMEM] * 5 + [SMEM] * 2,
        [
            pltpu.VMEM((LANES, tokens), F32),
            pltpu.VMEM((tokens, WIDE), BF16),
            pltpu.VMEM((tokens, WIDE), BF16),
            pltpu.VMEM((tokens, WIDE), BF16),
            pltpu.VMEM((tokens, tokens), F32),
            pltpu.VMEM((tokens, tokens), F32),
            pltpu.VMEM((tokens, tokens), BF16),
            pltpu.VMEM((LANES, 2 * tokens), F32),
        ],
        6,
        "chunk_alone",
        20,
    )(x, g, b, c, steps, rate_log, skip)
    half = ((4, HALF, WIDE + LANES), F32)
    keep, give, stack = call(
        split_kernel,
        [half, half, ((chips, tokens, 2 * LANES), BF16)],
        [VMEM] * (1 + chips),
        [],
        1,
        "split_states",
    )(states, *kv_parts)
    received = swapped(give)
    other_stack = swapped(stack)

    messages = call(
        lambda *refs: combine_kernel(chips, *refs),
        [((HALF, WIDE + LANES), BF16)] * (chips - 1),
        [VMEM] * 2 + [AFTER],
        [],
        1,
        "combine_states",
    )(keep, received, sums)
    arrived = [from_chip(messages[k - 1], k) for k in range(1, chips)]

    columns = QUERY_HEADS * BLOCK
    scratch = [
        pltpu.SMEM((most,), jnp.int32),
        pltpu.VMEM((most * BLOCK, LANES), BF16),
        pltpu.VMEM((most * BLOCK, LANES), BF16),
        pltpu.VMEM((most * BLOCK, 2 * LANES), BF16),
        pltpu.VMEM((LANES, columns), BF16),
        pltpu.VMEM((LANES, columns), BF16),
        pltpu.VMEM((columns, most * BLOCK), BF16),
        pltpu.VMEM((columns, most * BLOCK), BF16),
    ]
    first_out, first_dq, first_acc, kv_all = call(
        lambda *refs: first_attention_kernel(chips, most, *refs),
        [
            ((BLOCK, columns), F32),
            ((BLOCK, columns), BF16),
            ((2 * LANES, every), F32),
            ((every, 2 * LANES), BF16),
        ],
        [SMEM] + [VMEM] * 4 + [AFTER],
        scratch,
        5,
        "first_attention",
        18 + most,
    )(block_mask[0], q, g, stack, other_stack, messages[0])
    part = columns // 2
    half_outs = [
        ((BLOCK, part), F32),
        ((BLOCK, part), BF16),
        ((LANES, part), BF16),
        ((LANES, part), BF16),
        ((part, most * BLOCK), BF16),
        ((part, most * BLOCK), BF16),
    ]

    def half_attention(chosen, after, name):
        return call(
            lambda *refs: half_attention_kernel(chosen, most, *refs),
            half_outs,
            [SMEM] + [VMEM] * 3 + [AFTER],
            scratch[:4],
            2,
            name,
            18 + most,
        )(block_mask[0], q, g, kv_all, after)

    early_out, early_dq, *early = half_attention((0, HALF_HEADS), first_dq, "early_attention")

    entering = ((2, HALF, WIDE), BF16)
    own, give, totals = call(
        lambda *refs: chain_kernel(chips, *refs),
        [entering, entering, ((2 * HS, LANES), F32)],
        [VMEM] * 3 + [AFTER] + [VMEM] * (chips - 1),
        [],
        2,
        "chain_states",
    )(keep, received, sums, early_dq, *arrived)
    other = swapped(give)
    rounds = [1 << bit for bit in range((replicas - 1).bit_length())]
    replicated = totals
    for distance in rounds[:-1]:
        replicated = replicated + from_replica(replicated, distance)
    last_round = from_replica(replicated, rounds[-1])

    late_out, late_dq, *late = half_attention((HALF_HEADS, QUERY_HEADS), totals, "late_attention")
    acc, dq = call(
        lambda *refs: key_terms_kernel(most, *refs),
        [((2 * LANES, every), F32), ((tokens, columns), BF16)],
        [SMEM] + [VMEM] * 12,
        scratch[:1],
        2,
        "key_terms",
        18 + most,
    )(block_mask[0], first_acc, first_dq, early_dq, late_dq, *early, *late)
    keep, give, sums = call(
        lambda *refs: share_kernel(chips, *refs),
        [
            ((chips * 2 * LANES, tokens), BF16),
            ((chips * 2 * LANES + 32, tokens), BF16),
            ((2 * HS, LANES), F32),
        ],
        [VMEM] * 3,
        [],
        1,
        "share_key_gradients",
    )(acc, replicated, last_round)
    partial, summed, *messages = call(
        lambda *refs: pair_sum_kernel(chips, *refs),
        [((2 * LANES, tokens), F32), ((2 * HS, LANES), F32)]
        + [((2 * LANES + 32, tokens), BF16)] * (chips - 1),
        [VMEM] * 3,
        [],
        1,
        "pair_sum",
    )(keep, swapped(give), sums)
    arrived = [from_chip(messages[k - 1], k) for k in range(1, chips)]

    y, dx, db, dc = call(
        outer_kernel,
        [((tokens, WIDE), BF16)] * 2 + [((tokens, NS), BF16)] * 2,
        [VMEM] * 5 + [SMEM] + [VMEM] * 9 + [AFTER],
        [
            pltpu.VMEM((LANES, tokens), F32),
            pltpu.VMEM((tokens, WIDE), BF16),
            pltpu.VMEM((tokens, WIDE), BF16),
            pltpu.VMEM((2, NS, WIDE), BF16),
        ],
        3,
        "chunk_outer",
    )(
        x, g, b, c, steps, rate_log, own, other, first_out, early_out, late_out,
        inner_y, inner_dx, inner_db, inner_dc, messages[0],
    )

    tokens_all = replicas * n * tokens
    dk, dv, grad_rate_log, grad_skip = call(
        lambda *refs: owner_sum_kernel(chips, tokens_all, *refs),
        [((tokens, LANES), BF16)] * 2 + [((1, HS), F32)] * 2,
        [VMEM] * (chips + 1),
        [],
        1,
        "owner_sum",
    )(partial, summed, *arrived)
    return (
        y[None],
        dq[None],
        dk[None],
        dv[None],
        dx[None],
        db[None],
        dc[None],
        grad_rate_log.reshape(HS),
        grad_skip.reshape(HS),
    )


def solution(mesh):
    split = P("dp", "seq", None)
    in_specs = (split,) * 7 + (P(), P(), P("dp", None, None), split)
    out_specs = (split,) * 7 + (P(), P())
    return jax.shard_map(body, mesh=mesh, in_specs=in_specs, out_specs=out_specs, check_vma=False)
```
